32 devices in a mesh: chain: 2 (over core), energy: 16 (over z, y, x).
Axes of the slice: x: 2, y: 2, z: 4, core: 2. Of those that a mesh axis runs over, the one named last changes fastest.
Arguments:
- retarded: float32 [16, 4, 2, 256, 256], P('energy', 'chain'), may hold values from -0.625 to 0.625
- lesser_sigma: float32 [16, 4, 2, 256, 256], P('energy', 'chain'), may hold values from -6 to 6
- coupling: float32 [4, 2, 256, 256], P('chain'), may hold values from -1 to 1
- coupling_pattern: int32 [4, 4, 4], P('chain'), may hold values from 0 to 1, as said below
- kept_blocks: int32 [4], replicated, may hold values from 0 to 15, as said below
- lead_lesser: float32 [16, 2, 256, 256], P('energy'), may hold values from -8 to 8
Outputs:
- polarization: float32 [16, 2, 65536], P(None, None, ('chain', 'energy'))
The draws below stay inside these ranges and needn't reach their ends.
Inputs may be any that keep to these rules, and one draw needn't show every extreme that they name: `coupling_pattern`: 0/1 entries; each cell's coupling has exactly 4 ones. `kept_blocks`: distinct block numbers.
All inputs are finite; a program needn't handle non-finite values.
Results may differ from the reference program's by a relative error of at most 0.0001.
Values sent between devices are 32-bit elements; how exact they have to be, the bound alone decides.
No kernel may reach another device: no remote copies, remote signals or barrier semaphores. Data moves between devices by JAX's collectives and lax.ppermute only.
A program may use at most 832 MiB of HBM per device.

```python
import jax
import jax.numpy as jnp
from jax import lax

M = 256
BLOCK = 64
NBLK = 4
KEEP = 4
B_NNZ = 4
LAGS = 16
ENERGIES = 16
NCELLS = 4
ELEMS = 65536


def draw_coupling_pattern(key, part):
    subkeys = jax.random.split(jax.random.fold_in(key, 11), NCELLS)
    orders = jax.vmap(lambda one_key: jax.random.permutation(one_key, NBLK * NBLK))(subkeys)
    return (orders < B_NNZ).astype(jnp.int32).reshape(NCELLS, NBLK, NBLK)


def draw_kept_blocks(key, part):
    middle = jax.random.permutation(jax.random.fold_in(key, 12), NBLK * NBLK - 2) + 1
    first = jnp.zeros((1,), jnp.int32)
    last = jnp.full((1,), NBLK * NBLK - 1, jnp.int32)
    chosen = jnp.concatenate([first, middle[:KEEP - 2].astype(jnp.int32), last])
    return jax.random.permutation(jax.random.fold_in(key, 13), chosen).astype(jnp.int32)


def level_of(rng, dims, shards, smallest, largest):
    def one(dim, blocks):
        draws = jax.random.uniform(jax.random.fold_in(jax.random.fold_in(rng, 6), dim), (blocks,), jnp.float32, smallest / len(shards), largest / len(shards))
        return jnp.repeat(jnp.exp(draws), dims[dim] // blocks).reshape((-1,) + (1,) * (len(dims) - dim - 1))

    gain = one(*shards[0])
    for cut in shards[1:]:
        gain = gain * one(*cut)
    return gain


def gaussian(key, dims, width, limit, shards=(), kind=jnp.bfloat16):
    result = jax.random.normal(key, dims, jnp.float32) * width
    if len(shards) > 0:
        result = level_of(key, dims, shards, -0.22, 0.18) * result
    return jnp.clip(result, min=-limit, max=limit).astype(kind)


def setup_inputs(seed: int = 0) -> dict:
    seeds = jax.random.split(jax.random.key(seed), 7)
    return {
        "retarded": gaussian(seeds[0], (ENERGIES, NCELLS, 2, M, M), ((0.5 / M) ** 0.5), 0.625, ((0, 16), (1, 2)), jnp.float32),
        "lesser_sigma": gaussian(seeds[1], (ENERGIES, NCELLS, 2, M, M), 1.0, 6.0, ((0, 16), (1, 2)), jnp.float32),
        "coupling": gaussian(seeds[2], (NCELLS, 2, M, M), ((0.35 * NBLK * NBLK / (B_NNZ * M)) ** 0.5), 1.0, ((0, 2),), jnp.float32),
        "coupling_pattern": draw_coupling_pattern(jax.random.fold_in(seeds[6], 71), 0),
        "kept_blocks": draw_kept_blocks(jax.random.fold_in(seeds[6], 71), 0),
        "lead_lesser": gaussian(seeds[5], (ENERGIES, 2, M, M), 1.4, 8.0, ((0, 16),), jnp.float32),
    }


def matmul_high(left, right):
    return jnp.matmul(left, right, precision=lax.Precision.HIGHEST)


def complex_product(left, right):
    left_re, left_im = left[..., 0, :, :], left[..., 1, :, :]
    right_re, right_im = right[..., 0, :, :], right[..., 1, :, :]
    real_part = matmul_high(left_re, right_re) - matmul_high(left_im, right_im)
    imag_part = matmul_high(left_re, right_im) + matmul_high(left_im, right_re)
    return jnp.stack([real_part, imag_part], axis=-3)


def product_adjoint(left, right):
    left_re, left_im = left[..., 0, :, :], left[..., 1, :, :]
    right_tr = jnp.swapaxes(right[..., 0, :, :], -1, -2)
    right_ti = jnp.swapaxes(right[..., 1, :, :], -1, -2)
    real_part = matmul_high(left_re, right_tr) + matmul_high(left_im, right_ti)
    imag_part = matmul_high(left_im, right_tr) - matmul_high(left_re, right_ti)
    return jnp.stack([real_part, imag_part], axis=-3)


def expand_pattern(pattern):
    return jnp.repeat(jnp.repeat(pattern.astype(jnp.float32), BLOCK, axis=-2), BLOCK, axis=-1)


def pick_blocks(matrix, kept_blocks):
    lead_shape = matrix.shape[:-2]
    tiles = matrix.reshape(lead_shape + (NBLK, BLOCK, NBLK, BLOCK))
    tiles = jnp.swapaxes(tiles, -3, -2)
    tiles = tiles.reshape(lead_shape + (NBLK * NBLK, BLOCK * BLOCK))
    return jnp.take(tiles, kept_blocks, axis=-2)


def reference(retarded, lesser_sigma, coupling, coupling_pattern, kept_blocks, lead_lesser):
    coupling_full = coupling * expand_pattern(coupling_pattern)[:, None]

    def one_energy(operands):
        green_e, sigma_e, entry_block = operands

        def advance(state_in, inputs):
            green, sigma, bridge = inputs
            joined = complex_product(green, bridge)
            fresh = product_adjoint(complex_product(green, sigma), green)
            state_out = fresh + product_adjoint(complex_product(joined, state_in), joined)
            return state_out, pick_blocks(state_out, kept_blocks)

        _, retained = lax.scan(advance, entry_block, (green_e, sigma_e, coupling_full))
        return retained

    retained = lax.map(one_energy, (retarded, lesser_sigma, lead_lesser))
    retained = jnp.transpose(retained, (0, 2, 1, 3, 4)).reshape(ENERGIES, 2, ELEMS)
    results = []
    for lag_index in range(LAGS):
        shifted = retained[lag_index:]
        earlier = retained[:ENERGIES - lag_index]
        real_part = jnp.sum(shifted[:, 0] * earlier[:, 0] + shifted[:, 1] * earlier[:, 1], axis=0)
        imag_part = jnp.sum(shifted[:, 1] * earlier[:, 0] - shifted[:, 0] * earlier[:, 1], axis=0)
        results.append(jnp.stack([real_part, imag_part], axis=0))
    return jnp.stack(results, axis=0) / jnp.float32(ENERGIES)
```

```python
import functools

import jax
import jax.numpy as jnp
from jax import lax
from jax.experimental import pallas as pl
from jax.experimental.pallas import tpu as pltpu
from jax.sharding import PartitionSpec as P

BLOCK = 64
LAGS = 16
LANES = 128
F32 = jnp.float32
BF16 = jnp.bfloat16


def two_parts(value):
    high = value.astype(BF16)
    return high, (value - high.astype(F32)).astype(BF16)


def as_left(stacked):
    high, low = stacked
    return jnp.concatenate([high, high, low], axis=1)


def combined(product, conjugate):
    m, n = product.shape[0] // 2, product.shape[1] // 2
    rr, ri = product[:m, :n], product[:m, n:]
    ir, ii = product[m:, :n], product[m:, n:]
    if conjugate:
        return rr + ii, ir - ri
    return rr - ii, ri + ir


def complex_product(left, right):
    high, low = right
    wide = jnp.concatenate([high, low, high], axis=0)
    product = lax.dot_general(as_left(left), wide, (((1,), (0,)), ((), ())), preferred_element_type=F32)
    return combined(product, False)


def product_adjoint(left, right):
    high, low = right
    tall = jnp.concatenate([high, low, high], axis=1)
    product = lax.dot_general(as_left(left), tall, (((1,), (1,)), ((), ())), preferred_element_type=F32)
    return combined(product, True)


def above(pair):
    return two_parts(jnp.concatenate(pair, axis=0))


def beside(pair):
    return two_parts(jnp.concatenate(pair, axis=1))


def beside_of(stacked):
    m = stacked[0].shape[0] // 2
    return tuple(jnp.concatenate([part[:m], part[m:]], axis=1) for part in stacked)


def put_state(state_ref, pair):
    for part in range(2):
        for group in range(state_ref.shape[1]):
            state_ref[part, group] = pair[part][:, group * LANES:(group + 1) * LANES]


def get_state(state_ref):
    groups = range(state_ref.shape[1])
    return tuple(jnp.concatenate([state_ref[part, group] for group in groups], axis=1) for part in range(2))


def block_mask(pattern_ref, cell, size):
    nblk = size // BLOCK
    column = lax.broadcasted_iota(jnp.int32, (BLOCK, size), 1) // BLOCK
    rows = []
    for r in range(nblk):
        row = jnp.zeros((BLOCK, size), F32)
        for c in range(nblk):
            row = jnp.where(column == c, pattern_ref[cell, r, c].astype(F32), row)
        rows.append(row)
    return jnp.concatenate(rows, axis=0)


def pick_into(send_ref, e, cell, matrix_ref, kept_ref, keep, share_rows):
    nblk = matrix_ref.shape[-2] // BLOCK
    half = BLOCK // 2
    lane = lax.broadcasted_iota(jnp.int32, (half, LANES), 1)
    piece = min(half, share_rows)
    for k in range(keep):
        number = kept_ref[k]
        top = (number // nblk) * BLOCK
        across = (number % nblk) * BLOCK
        window = across // LANES
        in_upper = jnp.full((half, LANES), across % LANES, jnp.int32) > 0
        for part in range(2):
            even = matrix_ref[part, window, pl.ds(top, half, 2), :]
            odd = matrix_ref[part, window, pl.ds(top + 1, half, 2), :]
            left = jnp.where(in_upper, pltpu.roll(even, BLOCK, 1), even)
            right = jnp.where(in_upper, odd, pltpu.roll(odd, BLOCK, 1))
            flat = jnp.where(lane < BLOCK, left, right)
            first = (cell * keep + k) * half
            for s in range(0, half, piece):
                owner, inside = divmod(first + s, share_rows)
                send_ref[e, owner, pl.ds(part * share_rows + inside, piece), :] = flat[s:s + piece]


def head_kernel(keep, share_rows, g_hbm, s_hbm, b_hbm, pattern_ref, kept_ref, lead_hbm,
                leaving_hbm, send_hbm, joined_hbm, fresh_hbm,
                g_ref, s_ref, b_ref, lead_ref, state_ref, send_ref, joined_ref, fresh_ref, in_sems, out_sems):
    energies, cells, _, size, _ = g_ref.shape
    position = lax.axis_index("chain")

    def fetch(slot, source, target):
        return pltpu.make_async_copy(source, target, in_sems.at[slot])

    lead_copy = fetch(0, lead_hbm, lead_ref)
    b_copies = [fetch(1 + i, b_hbm.at[i], b_ref.at[i]) for i in range(cells)]
    g_copies = [fetch(1 + cells + i, g_hbm.at[:, i], g_ref.at[:, i]) for i in range(cells)]
    s_copies = [fetch(1 + 2 * cells + i, s_hbm.at[:, i], s_ref.at[:, i]) for i in range(cells)]

    @pl.when(position == 0)
    def _():
        lead_copy.start()

    for i in range(cells):
        b_copies[i].start()
        g_copies[i].start()
        s_copies[i].start()

    def masked(i):
        mask = block_mask(pattern_ref, i, size)
        return b_ref[i, 0] * mask, b_ref[i, 1] * mask

    @pl.when(position == 0)
    def _():
        lead_copy.wait()
        for i in range(cells):
            b_copies[i].wait()
            bridge = above(masked(i))
            for e in range(energies):
                if i == 0:
                    state = (lead_ref[e, 0], lead_ref[e, 1])
                else:
                    state = get_state(state_ref.at[e])
                re, im = product_adjoint(above(complex_product(bridge, beside(state))), bridge)
                if e == 0:
                    s_copies[i].wait()
                    g_copies[i].wait()
                inner = beside((s_ref[e, i, 0] + re, s_ref[e, i, 1] + im))
                green = above((g_ref[e, i, 0], g_ref[e, i, 1]))
                re, im = product_adjoint(above(complex_product(green, inner)), green)
                put_state(state_ref.at[e], (re, im))
                if i == cells - 1 and e == energies - 1:
                    pltpu.make_async_copy(state_ref, leaving_hbm, out_sems.at[0]).start()
                pick_into(send_ref, e, i, state_ref.at[e], kept_ref, keep, share_rows)
        send_copy = pltpu.make_async_copy(send_ref, send_hbm, out_sems.at[1])
        send_copy.start()
        pltpu.make_async_copy(state_ref, leaving_hbm, out_sems.at[0]).wait()
        send_copy.wait()

    @pl.when(position > 0)
    def _():
        copies = []
        for i in range(cells):
            b_copies[i].wait()
            bridge = beside(masked(i))
            g_copies[i].wait()
            s_copies[i].wait()
            for e in range(energies):
                green = above((g_ref[e, i, 0], g_ref[e, i, 1]))
                joined = above(complex_product(green, bridge))
                joined_ref[e, i, 0] = joined[0]
                joined_ref[e, i, 1] = joined[1]
                inner = beside((s_ref[e, i, 0], s_ref[e, i, 1]))
                re, im = product_adjoint(above(complex_product(green, inner)), green)
                fresh_ref[e, i, 0] = re
                fresh_ref[e, i, 1] = im
            for out, (source, target) in enumerate(((joined_ref, joined_hbm), (fresh_ref, fresh_hbm))):
                copy = pltpu.make_async_copy(source.at[:, i], target.at[:, i], out_sems.at[2 + 2 * i + out])
                copy.start()
                copies.append(copy)
        for copy in copies:
            copy.wait()


def head(keep, share_rows, owners, retarded, lesser_sigma, coupling, pattern, kept_blocks, lead):
    energies, cells, _, size, _ = retarded.shape
    hbm = pl.BlockSpec(memory_space=pltpu.HBM)
    smem = pl.BlockSpec(memory_space=pltpu.SMEM)
    state_shape = (energies, 2, size // LANES, size, LANES)
    send_shape = (energies, owners, 2 * share_rows, LANES)
    joined_shape = (energies, cells, 2, 2 * size, size)
    fresh_shape = (energies, cells, 2, size, size)
    return pl.pallas_call(
        functools.partial(head_kernel, keep, share_rows),
        out_shape=(
            jax.ShapeDtypeStruct(state_shape, F32),
            jax.ShapeDtypeStruct(send_shape, F32),
            jax.ShapeDtypeStruct(joined_shape, BF16),
            jax.ShapeDtypeStruct(fresh_shape, F32),
        ),
        in_specs=[hbm, hbm, hbm, smem, smem, hbm],
        out_specs=(hbm, hbm, hbm, hbm),
        scratch_shapes=[
            pltpu.VMEM(retarded.shape, F32),
            pltpu.VMEM(lesser_sigma.shape, F32),
            pltpu.VMEM(coupling.shape, F32),
            pltpu.VMEM(lead.shape, F32),
            pltpu.VMEM(state_shape, F32),
            pltpu.VMEM(send_shape, F32),
            pltpu.VMEM(joined_shape, BF16),
            pltpu.VMEM(fresh_shape, F32),
            pltpu.SemaphoreType.DMA((1 + 3 * cells,)),
            pltpu.SemaphoreType.DMA((2 + 2 * cells,)),
        ],
        compiler_params=pltpu.CompilerParams(vmem_limit_bytes=32 << 20),
        name="head_cells",
    )(retarded, lesser_sigma, coupling, pattern, kept_blocks, lead)


def tail_kernel(keep, share_rows, hop, incoming_hbm, joined_hbm, fresh_hbm, kept_ref, leaving_in, send_in,
                leaving_hbm, send_hbm, state_ref, joined_ref, fresh_ref, send_ref, in_sems, out_sems):
    energies, cells, _, size, _ = fresh_ref.shape

    @pl.when(lax.axis_index("chain") == hop + 1)
    def _():
        state_copy = pltpu.make_async_copy(incoming_hbm, state_ref, in_sems.at[0])
        state_copy.start()
        copies = []
        for i in range(cells):
            pair = (
                pltpu.make_async_copy(joined_hbm.at[:, i], joined_ref.at[:, i], in_sems.at[1 + 2 * i]),
                pltpu.make_async_copy(fresh_hbm.at[:, i], fresh_ref.at[:, i], in_sems.at[2 + 2 * i]),
            )
            for copy in pair:
                copy.start()
            copies.append(pair)
        state_copy.wait()
        for i in range(cells):
            for copy in copies[i]:
                copy.wait()
            for e in range(energies):
                joined = (joined_ref[e, i, 0], joined_ref[e, i, 1])
                state = beside(get_state(state_ref.at[e]))
                re, im = product_adjoint(above(complex_product(joined, state)), joined)
                put_state(state_ref.at[e], (fresh_ref[e, i, 0] + re, fresh_ref[e, i, 1] + im))
                pick_into(send_ref, e, i, state_ref.at[e], kept_ref, keep, share_rows)
        send_copy = pltpu.make_async_copy(send_ref, send_hbm, out_sems.at[0])
        send_copy.start()
        leaving_copy = pltpu.make_async_copy(state_ref, leaving_hbm, out_sems.at[1])
        leaving_copy.start()
        send_copy.wait()
        leaving_copy.wait()


def tail(keep, share_rows, hop, incoming, joined, fresh, kept_blocks, leaving, send):
    cells = fresh.shape[1]
    hbm = pl.BlockSpec(memory_space=pltpu.HBM)
    smem = pl.BlockSpec(memory_space=pltpu.SMEM)
    return pl.pallas_call(
        functools.partial(tail_kernel, keep, share_rows, hop),
        out_shape=(
            jax.ShapeDtypeStruct(leaving.shape, F32),
            jax.ShapeDtypeStruct(send.shape, F32),
        ),
        in_specs=[hbm, hbm, hbm, smem, hbm, hbm],
        out_specs=(hbm, hbm),
        input_output_aliases={4: 0, 5: 1},
        scratch_shapes=[
            pltpu.VMEM(incoming.shape, F32),
            pltpu.VMEM(joined.shape, BF16),
            pltpu.VMEM(fresh.shape, F32),
            pltpu.VMEM(send.shape, F32),
            pltpu.SemaphoreType.DMA((1 + 2 * cells,)),
            pltpu.SemaphoreType.DMA((2,)),
        ],
        compiler_params=pltpu.CompilerParams(vmem_limit_bytes=32 << 20),
        name="tail_cells",
    )(incoming, joined, fresh, kept_blocks, leaving, send)


def lag_kernel(in_ref, out_ref):
    energies, double_rows, _ = in_ref.shape
    rows = double_rows // 2
    step = min(8, rows)
    scale = 1.0 / energies
    for first in range(0, rows, step):
        re = [in_ref[e, first:first + step] for e in range(energies)]
        im = [in_ref[e, rows + first:rows + first + step] for e in range(energies)]
        for lag in range(LAGS):
            real_sum = jnp.zeros((step, LANES), F32)
            imag_sum = jnp.zeros((step, LANES), F32)
            for e in range(energies - lag):
                real_sum += re[e + lag] * re[e] + im[e + lag] * im[e]
                imag_sum += im[e + lag] * re[e] - re[e + lag] * im[e]
            out_ref[lag, pl.ds(2 * first, step, 2), :] = real_sum * scale
            out_ref[lag, pl.ds(2 * first + 1, step, 2), :] = imag_sum * scale


def lag_sums(owned):
    energies, double_rows, lanes = owned.shape
    rows = double_rows // 2
    sums = pl.pallas_call(
        lag_kernel,
        out_shape=jax.ShapeDtypeStruct((LAGS, double_rows, lanes), F32),
        name="lag_sums",
    )(owned)
    sums = sums.reshape(LAGS, rows, 2, lanes)
    return jnp.swapaxes(sums, 1, 2).reshape(LAGS, 2, rows * lanes)


def per_device(retarded, lesser_sigma, coupling, coupling_pattern, kept_blocks, lead_lesser):
    energies_here, cells = retarded.shape[:2]
    keep = kept_blocks.shape[0]
    owners = lax.axis_size("energy")
    length = lax.axis_size("chain")
    share_rows = cells * keep * BLOCK * BLOCK // (owners * LANES)
    leaving, send, joined, fresh = head(
        keep, share_rows, owners, retarded, lesser_sigma, coupling, coupling_pattern, kept_blocks, lead_lesser
    )
    for hop in range(length - 1):
        incoming = lax.ppermute(leaving, "chain", [(hop, hop + 1)])
        leaving, send = tail(keep, share_rows, hop, incoming, joined, fresh, kept_blocks, leaving, send)
    owned = lax.all_to_all(send, "energy", split_axis=1, concat_axis=0, tiled=True)
    return lag_sums(owned.reshape((-1,) + owned.shape[2:]))


def solution(mesh):
    return jax.shard_map(
        per_device,
        mesh=mesh,
        in_specs=(
            P("energy", "chain", None, None, None),
            P("energy", "chain", None, None, None),
            P("chain", None, None, None),
            P("chain", None, None),
            P(),
            P("energy", None, None, None),
        ),
        out_specs=P(None, None, ("chain", "energy")),
        check_vma=False,
    )
```

```python
import functools

import jax
import jax.numpy as jnp
from jax import lax
from jax.experimental import pallas as pl
from jax.experimental.pallas import tpu as pltpu
from jax.sharding import PartitionSpec as P

BLOCK = 64
LAGS = 16
LANES = 128
F32 = jnp.float32
BF16 = jnp.bfloat16


def two_parts(value):
    high = value.astype(BF16)
    return high, (value - high.astype(F32)).astype(BF16)


def as_left(stacked):
    high, low = stacked
    return jnp.concatenate([high, high, low], axis=1)


def combined(product, conjugate):
    m, n = product.shape[0] // 2, product.shape[1] // 2
    rr, ri = product[:m, :n], product[:m, n:]
    ir, ii = product[m:, :n], product[m:, n:]
    if conjugate:
        return rr + ii, ir - ri
    return rr - ii, ri + ir


def complex_product(left, right):
    high, low = right
    wide = jnp.concatenate([high, low, high], axis=0)
    product = lax.dot_general(as_left(left), wide, (((1,), (0,)), ((), ())), preferred_element_type=F32)
    return combined(product, False)


def product_adjoint(left, right):
    high, low = right
    tall = jnp.concatenate([high, low, high], axis=1)
    product = lax.dot_general(as_left(left), tall, (((1,), (1,)), ((), ())), preferred_element_type=F32)
    return combined(product, True)


def above(pair):
    return two_parts(jnp.concatenate(pair, axis=0))


def beside(pair):
    return two_parts(jnp.concatenate(pair, axis=1))


def beside_of(stacked):
    m = stacked[0].shape[0] // 2
    return tuple(jnp.concatenate([part[:m], part[m:]], axis=1) for part in stacked)


def put_state(state_ref, pair):
    for part in range(2):
        for group in range(state_ref.shape[1]):
            state_ref[part, group] = pair[part][:, group * LANES:(group + 1) * LANES]


def get_state(state_ref):
    groups = range(state_ref.shape[1])
    return tuple(jnp.concatenate([state_ref[part, group] for group in groups], axis=1) for part in range(2))


def block_mask(pattern_ref, cell, size):
    nblk = size // BLOCK
    column = lax.broadcasted_iota(jnp.int32, (BLOCK, size), 1) // BLOCK
    rows = []
    for r in range(nblk):
        row = jnp.zeros((BLOCK, size), F32)
        for c in range(nblk):
            row = jnp.where(column == c, pattern_ref[cell, r, c].astype(F32), row)
        rows.append(row)
    return jnp.concatenate(rows, axis=0)


def split_owners(owners):
    inner = 1
    while inner * inner < owners:
        inner *= 2
    if owners % inner:
        inner = 1
    return inner, owners // inner


def place(owner, owners):
    inner, outer = split_owners(owners)
    return owner % inner * outer + owner // inner


def pick_into(send_ref, e, cell, matrix_ref, kept_ref, keep, share_rows):
    nblk = matrix_ref.shape[-2] // BLOCK
    owners = send_ref.shape[1]
    half = BLOCK // 2
    lane = lax.broadcasted_iota(jnp.int32, (half, LANES), 1)
    piece = min(half, share_rows)
    for k in range(keep):
        number = kept_ref[k]
        top = (number // nblk) * BLOCK
        across = (number % nblk) * BLOCK
        window = across // LANES
        in_upper = jnp.full((half, LANES), across % LANES, jnp.int32) > 0
        for part in range(2):
            even = matrix_ref[part, window, pl.ds(top, half, 2), :]
            odd = matrix_ref[part, window, pl.ds(top + 1, half, 2), :]
            left = jnp.where(in_upper, pltpu.roll(even, BLOCK, 1), even)
            right = jnp.where(in_upper, odd, pltpu.roll(odd, BLOCK, 1))
            flat = jnp.where(lane < BLOCK, left, right)
            first = (cell * keep + k) * half
            for s in range(0, half, piece):
                owner, inside = divmod(first + s, share_rows)
                send_ref[e, place(owner, owners), pl.ds(part * share_rows + inside, piece), :] = flat[s:s + piece]


def head_kernel(keep, share_rows, g_hbm, s_hbm, b_hbm, pattern_hbm, kept_hbm, lead_hbm,
                leaving_hbm, send_hbm, joined_hbm, fresh_hbm,
                pattern_ref, kept_ref, g_ref, s_ref, b_ref, lead_ref, state_ref, send_ref, joined_ref, fresh_ref, in_sems, out_sems):
    energies, cells, _, size, _ = g_ref.shape
    position = lax.axis_index("chain")

    def fetch(slot, source, target):
        return pltpu.make_async_copy(source, target, in_sems.at[slot])

    lead_copy = fetch(0, lead_hbm, lead_ref)
    b_copies = [fetch(1 + i, b_hbm.at[i], b_ref.at[i]) for i in range(cells)]
    g_copies = [fetch(1 + cells + i, g_hbm.at[:, i], g_ref.at[:, i]) for i in range(cells)]
    s_copies = [fetch(1 + 2 * cells + i, s_hbm.at[:, i], s_ref.at[:, i]) for i in range(cells)]

    pattern_copy = fetch(1 + 3 * cells, pattern_hbm, pattern_ref)
    kept_copy = fetch(2 + 3 * cells, kept_hbm, kept_ref)
    pattern_copy.start()
    kept_copy.start()

    @pl.when(position == 0)
    def _():
        lead_copy.start()

    for i in range(cells):
        b_copies[i].start()
        g_copies[i].start()
        s_copies[i].start()

    pattern_copy.wait()
    kept_copy.wait()

    def masked(i):
        mask = block_mask(pattern_ref, i, size)
        return b_ref[i, 0] * mask, b_ref[i, 1] * mask

    @pl.when(position == 0)
    def _():
        lead_copy.wait()
        for i in range(cells):
            b_copies[i].wait()
            bridge = above(masked(i))
            for e in range(energies):
                if i == 0:
                    state = (lead_ref[e, 0], lead_ref[e, 1])
                else:
                    state = get_state(state_ref.at[e])
                re, im = product_adjoint(above(complex_product(bridge, beside(state))), bridge)
                if e == 0:
                    s_copies[i].wait()
                    g_copies[i].wait()
                inner = beside((s_ref[e, i, 0] + re, s_ref[e, i, 1] + im))
                green = above((g_ref[e, i, 0], g_ref[e, i, 1]))
                re, im = product_adjoint(above(complex_product(green, inner)), green)
                put_state(state_ref.at[e], (re, im))
                if i == cells - 1 and e == energies - 1:
                    pltpu.make_async_copy(state_ref, leaving_hbm, out_sems.at[0]).start()
                pick_into(send_ref, e, i, state_ref.at[e], kept_ref, keep, share_rows)
        send_copy = pltpu.make_async_copy(send_ref, send_hbm, out_sems.at[1])
        send_copy.start()
        pltpu.make_async_copy(state_ref, leaving_hbm, out_sems.at[0]).wait()
        send_copy.wait()

    @pl.when(position > 0)
    def _():
        copies = []
        for i in range(cells):
            b_copies[i].wait()
            bridge = beside(masked(i))
            g_copies[i].wait()
            s_copies[i].wait()
            for e in range(energies):
                green = above((g_ref[e, i, 0], g_ref[e, i, 1]))
                joined = above(complex_product(green, bridge))
                joined_ref[e, i, 0] = joined[0]
                joined_ref[e, i, 1] = joined[1]
                inner = beside((s_ref[e, i, 0], s_ref[e, i, 1]))
                re, im = product_adjoint(above(complex_product(green, inner)), green)
                fresh_ref[e, i, 0] = re
                fresh_ref[e, i, 1] = im
            for out, (source, target) in enumerate(((joined_ref, joined_hbm), (fresh_ref, fresh_hbm))):
                copy = pltpu.make_async_copy(source.at[:, i], target.at[:, i], out_sems.at[2 + 2 * i + out])
                copy.start()
                copies.append(copy)
        for copy in copies:
            copy.wait()


def in_hbm(value):
    return pltpu.with_memory_space_constraint(value, pltpu.HBM)


def head(keep, share_rows, owners, retarded, lesser_sigma, coupling, pattern, kept_blocks, lead):
    energies, cells, _, size, _ = retarded.shape
    hbm = pl.BlockSpec(memory_space=pltpu.HBM)
    state_shape = (energies, 2, size // LANES, size, LANES)
    send_shape = (energies, owners, 2 * share_rows, LANES)
    joined_shape = (energies, cells, 2, 2 * size, size)
    fresh_shape = (energies, cells, 2, size, size)
    return pl.pallas_call(
        functools.partial(head_kernel, keep, share_rows),
        out_shape=(
            jax.ShapeDtypeStruct(state_shape, F32),
            jax.ShapeDtypeStruct(send_shape, F32),
            jax.ShapeDtypeStruct(joined_shape, BF16),
            jax.ShapeDtypeStruct(fresh_shape, F32),
        ),
        in_specs=[hbm] * 6,
        out_specs=(hbm, hbm, hbm, hbm),
        scratch_shapes=[
            pltpu.SMEM(pattern.shape, jnp.int32),
            pltpu.SMEM(kept_blocks.shape, jnp.int32),
            pltpu.VMEM(retarded.shape, F32),
            pltpu.VMEM(lesser_sigma.shape, F32),
            pltpu.VMEM(coupling.shape, F32),
            pltpu.VMEM(lead.shape, F32),
            pltpu.VMEM(state_shape, F32),
            pltpu.VMEM(send_shape, F32),
            pltpu.VMEM(joined_shape, BF16),
            pltpu.VMEM(fresh_shape, F32),
            pltpu.SemaphoreType.DMA((3 + 3 * cells,)),
            pltpu.SemaphoreType.DMA((2 + 2 * cells,)),
        ],
        compiler_params=pltpu.CompilerParams(vmem_limit_bytes=32 << 20),
        name="head_cells",
    )(*(in_hbm(x) for x in (retarded, lesser_sigma, coupling, pattern, kept_blocks, lead)))


def tail_kernel(keep, share_rows, hop, last, incoming_hbm, joined_hbm, fresh_hbm, kept_hbm, *refs):
    if last:
        (_, send_hbm), refs = refs[:2], refs[2:]
    else:
        (_, _, leaving_hbm, send_hbm), refs = refs[:4], refs[4:]
    kept_ref, state_ref, joined_ref, fresh_ref, send_ref, in_sems, out_sems = refs
    energies, cells, _, size, _ = fresh_ref.shape

    @pl.when(lax.axis_index("chain") == hop + 1)
    def _():
        kept_copy = pltpu.make_async_copy(kept_hbm, kept_ref, in_sems.at[1 + 2 * cells])
        kept_copy.start()
        state_copy = pltpu.make_async_copy(incoming_hbm, state_ref, in_sems.at[0])
        state_copy.start()
        copies = []
        for i in range(cells):
            pair = (
                pltpu.make_async_copy(joined_hbm.at[:, i], joined_ref.at[:, i], in_sems.at[1 + 2 * i]),
                pltpu.make_async_copy(fresh_hbm.at[:, i], fresh_ref.at[:, i], in_sems.at[2 + 2 * i]),
            )
            for copy in pair:
                copy.start()
            copies.append(pair)
        state_copy.wait()
        for i in range(cells):
            for copy in copies[i]:
                copy.wait()
            for e in range(energies):
                joined = (joined_ref[e, i, 0], joined_ref[e, i, 1])
                state = beside(get_state(state_ref.at[e]))
                re, im = product_adjoint(above(complex_product(joined, state)), joined)
                put_state(state_ref.at[e], (fresh_ref[e, i, 0] + re, fresh_ref[e, i, 1] + im))
                if i == 0 and e == 0:
                    kept_copy.wait()
                pick_into(send_ref, e, i, state_ref.at[e], kept_ref, keep, share_rows)
        outs = [pltpu.make_async_copy(send_ref, send_hbm, out_sems.at[0])]
        if not last:
            outs.append(pltpu.make_async_copy(state_ref, leaving_hbm, out_sems.at[1]))
        for copy in outs:
            copy.start()
        for copy in outs:
            copy.wait()


def tail(keep, share_rows, hop, last, incoming, joined, fresh, kept_blocks, leaving, send):
    cells = fresh.shape[1]
    hbm = pl.BlockSpec(memory_space=pltpu.HBM)
    carried = (send,) if last else (leaving, send)
    result = pl.pallas_call(
        functools.partial(tail_kernel, keep, share_rows, hop, last),
        out_shape=tuple(jax.ShapeDtypeStruct(value.shape, F32) for value in carried),
        in_specs=[hbm] * (4 + len(carried)),
        out_specs=(hbm,) * len(carried),
        input_output_aliases={4 + i: i for i in range(len(carried))},
        scratch_shapes=[
            pltpu.SMEM(kept_blocks.shape, jnp.int32),
            pltpu.VMEM(incoming.shape, F32),
            pltpu.VMEM(joined.shape, BF16),
            pltpu.VMEM(fresh.shape, F32),
            pltpu.VMEM(send.shape, F32),
            pltpu.SemaphoreType.DMA((2 + 2 * cells,)),
            pltpu.SemaphoreType.DMA((2,)),
        ],
        compiler_params=pltpu.CompilerParams(vmem_limit_bytes=32 << 20),
        name="tail_cells",
    )(incoming, joined, fresh, in_hbm(kept_blocks), *carried)
    return (leaving, result[0]) if last else result


def lag_kernel(in_ref, out_ref):
    energies, double_rows, _ = in_ref.shape
    rows = double_rows // 2
    step = min(8, rows)
    scale = 1.0 / energies
    for first in range(0, rows, step):
        re = [in_ref[e, first:first + step] for e in range(energies)]
        im = [in_ref[e, rows + first:rows + first + step] for e in range(energies)]
        for lag in range(LAGS):
            real_sum = jnp.zeros((step, LANES), F32)
            imag_sum = jnp.zeros((step, LANES), F32)
            for e in range(energies - lag):
                real_sum += re[e + lag] * re[e] + im[e + lag] * im[e]
                imag_sum += im[e + lag] * re[e] - re[e + lag] * im[e]
            out_ref[lag, pl.ds(2 * first, step, 2), :] = real_sum * scale
            out_ref[lag, pl.ds(2 * first + 1, step, 2), :] = imag_sum * scale


def lag_sums(owned):
    energies, double_rows, lanes = owned.shape
    rows = double_rows // 2
    sums = pl.pallas_call(
        lag_kernel,
        out_shape=jax.ShapeDtypeStruct((LAGS, double_rows, lanes), F32),
        name="lag_sums",
    )(owned)
    sums = sums.reshape(LAGS, rows, 2, lanes)
    return jnp.swapaxes(sums, 1, 2).reshape(LAGS, 2, rows * lanes)


def exchange(send):
    energies, owners = send.shape[:2]
    inner, outer = split_owners(owners)
    near = [[o * inner + i for i in range(inner)] for o in range(outer)]
    far = [[o * inner + i for o in range(outer)] for i in range(inner)]
    tail = send.shape[2:]
    send = send.reshape((energies, inner, outer) + tail)
    send = lax.all_to_all(send, "energy", split_axis=1, concat_axis=1, axis_index_groups=near, tiled=True)
    send = jnp.swapaxes(send, 1, 2)
    send = lax.all_to_all(send, "energy", split_axis=1, concat_axis=0, axis_index_groups=far, tiled=True)
    send = send.reshape((outer, energies, inner) + tail)
    return jnp.swapaxes(send, 1, 2).reshape((-1,) + tail)


def per_device(retarded, lesser_sigma, coupling, coupling_pattern, kept_blocks, lead_lesser):
    energies_here, cells = retarded.shape[:2]
    keep = kept_blocks.shape[0]
    owners = lax.axis_size("energy")
    length = lax.axis_size("chain")
    share_rows = cells * keep * BLOCK * BLOCK // (owners * LANES)
    leaving, send, joined, fresh = head(
        keep, share_rows, owners, retarded, lesser_sigma, coupling, coupling_pattern, kept_blocks, lead_lesser
    )
    for hop in range(length - 1):
        incoming = lax.ppermute(leaving, "chain", [(hop, hop + 1)])
        last = hop == length - 2
        leaving, send = tail(keep, share_rows, hop, last, incoming, joined, fresh, kept_blocks, leaving, send)
    return lag_sums(exchange(send))


def solution(mesh):
    return jax.shard_map(
        per_device,
        mesh=mesh,
        in_specs=(
            P("energy", "chain", None, None, None),
            P("energy", "chain", None, None, None),
            P("chain", None, None, None),
            P("chain", None, None),
            P(),
            P("energy", None, None, None),
        ),
        out_specs=P(None, None, ("chain", "energy")),
        check_vma=False,
    )
```

```python
import functools

import jax
import jax.numpy as jnp
from jax import lax
from jax.experimental import pallas as pl
from jax.experimental.pallas import tpu as pltpu
from jax.sharding import PartitionSpec as P

BLOCK = 64
LAGS = 16
LANES = 128
F32 = jnp.float32
BF16 = jnp.bfloat16


def two_parts(value):
    high = value.astype(BF16)
    return high, (value - high.astype(F32)).astype(BF16)


def as_left(stacked):
    high, low = stacked
    return jnp.concatenate([high, high, low], axis=1)


def combined(product, conjugate):
    m, n = product.shape[0] // 2, product.shape[1] // 2
    rr, ri = product[:m, :n], product[:m, n:]
    ir, ii = product[m:, :n], product[m:, n:]
    if conjugate:
        return rr + ii, ir - ri
    return rr - ii, ri + ir


def complex_product(left, right):
    high, low = right
    wide = jnp.concatenate([high, low, high], axis=0)
    product = lax.dot_general(as_left(left), wide, (((1,), (0,)), ((), ())), preferred_element_type=F32)
    return combined(product, False)


def product_adjoint(left, right):
    high, low = right
    tall = jnp.concatenate([high, low, high], axis=1)
    product = lax.dot_general(as_left(left), tall, (((1,), (1,)), ((), ())), preferred_element_type=F32)
    return combined(product, True)


def above(pair):
    return two_parts(jnp.concatenate(pair, axis=0))


def beside(pair):
    return two_parts(jnp.concatenate(pair, axis=1))


def beside_of(stacked):
    m = stacked[0].shape[0] // 2
    return tuple(jnp.concatenate([part[:m], part[m:]], axis=1) for part in stacked)


def put_state(state_ref, pair):
    for part in range(2):
        for group in range(state_ref.shape[1]):
            state_ref[part, group] = pair[part][:, group * LANES:(group + 1) * LANES]


def get_state(state_ref):
    groups = range(state_ref.shape[1])
    return tuple(jnp.concatenate([state_ref[part, group] for group in groups], axis=1) for part in range(2))


def block_mask(pattern_ref, cell, size):
    nblk = size // BLOCK
    column = lax.broadcasted_iota(jnp.int32, (BLOCK, size), 1) // BLOCK
    rows = []
    for r in range(nblk):
        row = jnp.zeros((BLOCK, size), F32)
        for c in range(nblk):
            row = jnp.where(column == c, pattern_ref[cell, r, c].astype(F32), row)
        rows.append(row)
    return jnp.concatenate(rows, axis=0)


def pick_into(send_ref, e, cell, matrix_ref, kept_ref, keep, share_rows):
    nblk = matrix_ref.shape[-2] // BLOCK
    me = lax.axis_index("energy")
    half = BLOCK // 2
    lane = lax.broadcasted_iota(jnp.int32, (half, LANES), 1)
    piece = min(half, share_rows)
    for k in range(keep):
        number = kept_ref[k]
        top = (number // nblk) * BLOCK
        across = (number % nblk) * BLOCK
        window = across // LANES
        in_upper = jnp.full((half, LANES), across % LANES, jnp.int32) > 0
        for part in range(2):
            even = matrix_ref[part, window, pl.ds(top, half, 2), :]
            odd = matrix_ref[part, window, pl.ds(top + 1, half, 2), :]
            left = jnp.where(in_upper, pltpu.roll(even, BLOCK, 1), even)
            right = jnp.where(in_upper, odd, pltpu.roll(odd, BLOCK, 1))
            flat = jnp.where(lane < BLOCK, left, right)
            first = (cell * keep + k) * half
            for s in range(0, half, piece):
                owner, inside = divmod(first + s, share_rows)
                send_ref[owner ^ me, e, pl.ds(part * share_rows + inside, piece), :] = flat[s:s + piece]


def head_kernel(keep, share_rows, g_hbm, s_hbm, b_hbm, pattern_hbm, kept_hbm, lead_hbm,
                leaving_hbm, send_hbm, joined_hbm, fresh_hbm,
                pattern_ref, kept_ref, g_ref, s_ref, b_ref, lead_ref, state_ref, send_ref, joined_ref, fresh_ref, in_sems, out_sems):
    energies, cells, _, size, _ = g_ref.shape
    position = lax.axis_index("chain")

    def fetch(slot, source, target):
        return pltpu.make_async_copy(source, target, in_sems.at[slot])

    lead_copy = fetch(0, lead_hbm, lead_ref)
    b_copies = [fetch(1 + i, b_hbm.at[i], b_ref.at[i]) for i in range(cells)]
    g_copies = [fetch(1 + cells + i, g_hbm.at[:, i], g_ref.at[:, i]) for i in range(cells)]
    s_copies = [fetch(1 + 2 * cells + i, s_hbm.at[:, i], s_ref.at[:, i]) for i in range(cells)]

    pattern_copy = fetch(1 + 3 * cells, pattern_hbm, pattern_ref)
    kept_copy = fetch(2 + 3 * cells, kept_hbm, kept_ref)
    pattern_copy.start()
    kept_copy.start()

    @pl.when(position == 0)
    def _():
        lead_copy.start()

    for i in range(cells):
        b_copies[i].start()
        g_copies[i].start()
        s_copies[i].start()

    pattern_copy.wait()
    kept_copy.wait()

    def masked(i):
        mask = block_mask(pattern_ref, i, size)
        return b_ref[i, 0] * mask, b_ref[i, 1] * mask

    @pl.when(position == 0)
    def _():
        lead_copy.wait()
        for i in range(cells):
            b_copies[i].wait()
            bridge = above(masked(i))
            for e in range(energies):
                if i == 0:
                    state = (lead_ref[e, 0], lead_ref[e, 1])
                else:
                    state = get_state(state_ref.at[e])
                re, im = product_adjoint(above(complex_product(bridge, beside(state))), bridge)
                if e == 0:
                    s_copies[i].wait()
                    g_copies[i].wait()
                inner = beside((s_ref[e, i, 0] + re, s_ref[e, i, 1] + im))
                green = above((g_ref[e, i, 0], g_ref[e, i, 1]))
                re, im = product_adjoint(above(complex_product(green, inner)), green)
                put_state(state_ref.at[e], (re, im))
                if i == cells - 1 and e == energies - 1:
                    pltpu.make_async_copy(state_ref, leaving_hbm, out_sems.at[0]).start()
                pick_into(send_ref, e, i, state_ref.at[e], kept_ref, keep, share_rows)
        send_copy = pltpu.make_async_copy(send_ref, send_hbm, out_sems.at[1])
        send_copy.start()
        pltpu.make_async_copy(state_ref, leaving_hbm, out_sems.at[0]).wait()
        send_copy.wait()

    @pl.when(position > 0)
    def _():
        copies = []
        for i in range(cells):
            b_copies[i].wait()
            bridge = beside(masked(i))
            g_copies[i].wait()
            s_copies[i].wait()
            for e in range(energies):
                green = above((g_ref[e, i, 0], g_ref[e, i, 1]))
                joined = above(complex_product(green, bridge))
                joined_ref[e, i, 0] = joined[0]
                joined_ref[e, i, 1] = joined[1]
                inner = beside((s_ref[e, i, 0], s_ref[e, i, 1]))
                re, im = product_adjoint(above(complex_product(green, inner)), green)
                fresh_ref[e, i, 0] = re
                fresh_ref[e, i, 1] = im
            for out, (source, target) in enumerate(((joined_ref, joined_hbm), (fresh_ref, fresh_hbm))):
                copy = pltpu.make_async_copy(source.at[:, i], target.at[:, i], out_sems.at[2 + 2 * i + out])
                copy.start()
                copies.append(copy)
        for copy in copies:
            copy.wait()


def in_hbm(value):
    return pltpu.with_memory_space_constraint(value, pltpu.HBM)


def head(keep, share_rows, owners, retarded, lesser_sigma, coupling, pattern, kept_blocks, lead):
    energies, cells, _, size, _ = retarded.shape
    hbm = pl.BlockSpec(memory_space=pltpu.HBM)
    state_shape = (energies, 2, size // LANES, size, LANES)
    send_shape = (owners, energies, 2 * share_rows, LANES)
    joined_shape = (energies, cells, 2, 2 * size, size)
    fresh_shape = (energies, cells, 2, size, size)
    return pl.pallas_call(
        functools.partial(head_kernel, keep, share_rows),
        out_shape=(
            jax.ShapeDtypeStruct(state_shape, F32),
            jax.ShapeDtypeStruct(send_shape, F32),
            jax.ShapeDtypeStruct(joined_shape, BF16),
            jax.ShapeDtypeStruct(fresh_shape, F32),
        ),
        in_specs=[hbm] * 6,
        out_specs=(hbm, hbm, hbm, hbm),
        scratch_shapes=[
            pltpu.SMEM(pattern.shape, jnp.int32),
            pltpu.SMEM(kept_blocks.shape, jnp.int32),
            pltpu.VMEM(retarded.shape, F32),
            pltpu.VMEM(lesser_sigma.shape, F32),
            pltpu.VMEM(coupling.shape, F32),
            pltpu.VMEM(lead.shape, F32),
            pltpu.VMEM(state_shape, F32),
            pltpu.VMEM(send_shape, F32),
            pltpu.VMEM(joined_shape, BF16),
            pltpu.VMEM(fresh_shape, F32),
            pltpu.SemaphoreType.DMA((3 + 3 * cells,)),
            pltpu.SemaphoreType.DMA((2 + 2 * cells,)),
        ],
        compiler_params=pltpu.CompilerParams(vmem_limit_bytes=32 << 20),
        name="head_cells",
    )(*(in_hbm(x) for x in (retarded, lesser_sigma, coupling, pattern, kept_blocks, lead)))


def tail_kernel(keep, share_rows, hop, last, incoming_hbm, joined_hbm, fresh_hbm, kept_hbm, *refs):
    if last:
        (_, send_hbm), refs = refs[:2], refs[2:]
    else:
        (_, _, leaving_hbm, send_hbm), refs = refs[:4], refs[4:]
    kept_ref, state_ref, joined_ref, fresh_ref, send_ref, in_sems, out_sems = refs
    energies, cells, _, size, _ = fresh_ref.shape

    @pl.when(lax.axis_index("chain") == hop + 1)
    def _():
        kept_copy = pltpu.make_async_copy(kept_hbm, kept_ref, in_sems.at[1 + 2 * cells])
        kept_copy.start()
        state_copy = pltpu.make_async_copy(incoming_hbm, state_ref, in_sems.at[0])
        state_copy.start()
        copies = []
        for i in range(cells):
            pair = (
                pltpu.make_async_copy(joined_hbm.at[:, i], joined_ref.at[:, i], in_sems.at[1 + 2 * i]),
                pltpu.make_async_copy(fresh_hbm.at[:, i], fresh_ref.at[:, i], in_sems.at[2 + 2 * i]),
            )
            for copy in pair:
                copy.start()
            copies.append(pair)
        state_copy.wait()
        for i in range(cells):
            for copy in copies[i]:
                copy.wait()
            for e in range(energies):
                joined = (joined_ref[e, i, 0], joined_ref[e, i, 1])
                state = beside(get_state(state_ref.at[e]))
                re, im = product_adjoint(above(complex_product(joined, state)), joined)
                put_state(state_ref.at[e], (fresh_ref[e, i, 0] + re, fresh_ref[e, i, 1] + im))
                if i == 0 and e == 0:
                    kept_copy.wait()
                pick_into(send_ref, e, i, state_ref.at[e], kept_ref, keep, share_rows)
        outs = [pltpu.make_async_copy(send_ref, send_hbm, out_sems.at[0])]
        if not last:
            outs.append(pltpu.make_async_copy(state_ref, leaving_hbm, out_sems.at[1]))
        for copy in outs:
            copy.start()
        for copy in outs:
            copy.wait()


def tail(keep, share_rows, hop, last, incoming, joined, fresh, kept_blocks, leaving, send):
    cells = fresh.shape[1]
    hbm = pl.BlockSpec(memory_space=pltpu.HBM)
    carried = (send,) if last else (leaving, send)
    result = pl.pallas_call(
        functools.partial(tail_kernel, keep, share_rows, hop, last),
        out_shape=tuple(jax.ShapeDtypeStruct(value.shape, F32) for value in carried),
        in_specs=[hbm] * (4 + len(carried)),
        out_specs=(hbm,) * len(carried),
        input_output_aliases={4 + i: i for i in range(len(carried))},
        scratch_shapes=[
            pltpu.SMEM(kept_blocks.shape, jnp.int32),
            pltpu.VMEM(incoming.shape, F32),
            pltpu.VMEM(joined.shape, BF16),
            pltpu.VMEM(fresh.shape, F32),
            pltpu.VMEM(send.shape, F32),
            pltpu.SemaphoreType.DMA((2 + 2 * cells,)),
            pltpu.SemaphoreType.DMA((2,)),
        ],
        compiler_params=pltpu.CompilerParams(vmem_limit_bytes=32 << 20),
        name="tail_cells",
    )(incoming, joined, fresh, in_hbm(kept_blocks), *carried)
    return (leaving, result[0]) if last else result


def lag_kernel(places, *refs):
    *in_refs, out_ref, all_ref = refs
    energies, double_rows, _ = all_ref.shape
    here = energies // len(places)
    rows = double_rows // 2
    step = min(8, rows)
    scale = 1.0 / energies
    me = lax.axis_index("energy")
    for r, (bundle, i) in enumerate(places):
        all_ref[pl.ds((me ^ r) * here, here)] = in_refs[bundle][i]
    for first in range(0, rows, step):
        re = [all_ref[e, first:first + step] for e in range(energies)]
        im = [all_ref[e, rows + first:rows + first + step] for e in range(energies)]
        for lag in range(LAGS):
            real_sum = jnp.zeros((step, LANES), F32)
            imag_sum = jnp.zeros((step, LANES), F32)
            for e in range(energies - lag):
                real_sum += re[e + lag] * re[e] + im[e + lag] * im[e]
                imag_sum += im[e + lag] * re[e] - re[e + lag] * im[e]
            out_ref[lag, pl.ds(2 * first, step, 2), :] = real_sum * scale
            out_ref[lag, pl.ds(2 * first + 1, step, 2), :] = imag_sum * scale


def lag_sums(slots):
    bundles, places = [], []
    for bundle, i in slots:
        known = [n for n, other in enumerate(bundles) if other is bundle]
        if not known:
            known = [len(bundles)]
            bundles.append(bundle)
        places.append((known[0], i))
    _, here, double_rows, lanes = bundles[0].shape
    rows = double_rows // 2
    sums = pl.pallas_call(
        functools.partial(lag_kernel, places),
        out_shape=jax.ShapeDtypeStruct((LAGS, double_rows, lanes), F32),
        scratch_shapes=[pltpu.VMEM((here * len(places), double_rows, lanes), F32)],
        name="lag_sums",
    )(*bundles)
    sums = sums.reshape(LAGS, rows, 2, lanes)
    return jnp.swapaxes(sums, 1, 2).reshape(LAGS, 2, rows * lanes)


def digits_of(owners):
    bits = owners.bit_length() - 1
    groups = []
    while bits:
        width = 2 if bits >= 2 else 1
        bits -= width
        groups.append((bits, 1 << width))
    return groups


def exchange(send):
    owners = send.shape[0]
    slots = [(send, r) for r in range(owners)]
    for shift, values in digits_of(owners):
        arrived = []
        for value in range(1, values):
            moving = [r for r in range(owners) if (r >> shift) % values == value]
            bundle = jnp.stack([slots[r][0][slots[r][1]] for r in moving])
            pairs = [(d, d ^ (value << shift)) for d in range(owners)]
            arrived.append((moving, lax.ppermute(bundle, "energy", pairs)))
        for moving, bundle in arrived:
            for i, r in enumerate(moving):
                slots[r] = (bundle, i)
    return slots


def per_device(retarded, lesser_sigma, coupling, coupling_pattern, kept_blocks, lead_lesser):
    energies_here, cells = retarded.shape[:2]
    keep = kept_blocks.shape[0]
    owners = lax.axis_size("energy")
    length = lax.axis_size("chain")
    share_rows = cells * keep * BLOCK * BLOCK // (owners * LANES)
    leaving, send, joined, fresh = head(
        keep, share_rows, owners, retarded, lesser_sigma, coupling, coupling_pattern, kept_blocks, lead_lesser
    )
    for hop in range(length - 1):
        incoming = lax.ppermute(leaving, "chain", [(hop, hop + 1)])
        last = hop == length - 2
        leaving, send = tail(keep, share_rows, hop, last, incoming, joined, fresh, kept_blocks, leaving, send)
    return lag_sums(exchange(send))


def solution(mesh):
    return jax.shard_map(
        per_device,
        mesh=mesh,
        in_specs=(
            P("energy", "chain", None, None, None),
            P("energy", "chain", None, None, None),
            P("chain", None, None, None),
            P("chain", None, None),
            P(),
            P("energy", None, None, None),
        ),
        out_specs=P(None, None, ("chain", "energy")),
        check_vma=False,
    )
```

```python
import functools

import jax
import jax.numpy as jnp
from jax import lax
from jax.experimental import pallas as pl
from jax.experimental.pallas import tpu as pltpu
from jax.sharding import PartitionSpec as P

BLOCK = 64
LAGS = 16
LANES = 128
F32 = jnp.float32
BF16 = jnp.bfloat16


def two_parts(value):
    high = value.astype(BF16)
    return high, (value - high.astype(F32)).astype(BF16)


def dot(left, right):
    return lax.dot_general(left, right, (((1,), (0,)), ((), ())), preferred_element_type=F32)


def left_parts(pair):
    return two_parts(jnp.concatenate(pair, axis=1))


def right_parts(pair):
    both = []
    for re, im in zip(two_parts(pair[0]), two_parts(pair[1])):
        both.append(jnp.concatenate([jnp.concatenate([re, im], axis=1), jnp.concatenate([-im, re], axis=1)], axis=0))
    return tuple(both)


def adjoint(pair):
    return pair[0].T, -pair[1].T


def product(left, right):
    wide = jnp.concatenate([left[0], left[0], left[1]], axis=1)
    tall = jnp.concatenate([right[0], right[1], right[0]], axis=0)
    both = dot(wide, tall)
    half = both.shape[1] // 2
    return both[:, :half], both[:, half:]


def plus(one, other):
    return one[0] + other[0], one[1] + other[1]


def put_state(state_ref, pair):
    for part in range(2):
        for group in range(state_ref.shape[1]):
            state_ref[part, group] = pair[part][:, group * LANES:(group + 1) * LANES]


def get_state(state_ref):
    groups = range(state_ref.shape[1])
    return tuple(jnp.concatenate([state_ref[part, group] for group in groups], axis=1) for part in range(2))


def block_mask(pattern_ref, cell, size):
    nblk = size // BLOCK
    column = lax.broadcasted_iota(jnp.int32, (BLOCK, size), 1) // BLOCK
    rows = []
    for r in range(nblk):
        row = jnp.zeros((BLOCK, size), F32)
        for c in range(nblk):
            row = jnp.where(column == c, pattern_ref[cell, r, c].astype(F32), row)
        rows.append(row)
    return jnp.concatenate(rows, axis=0)


def pick_into(send_ref, e, cell, matrix_ref, kept_ref, keep, share_rows):
    nblk = matrix_ref.shape[-2] // BLOCK
    half = BLOCK // 2
    lane = lax.broadcasted_iota(jnp.int32, (half, LANES), 1)
    piece = min(half, share_rows)
    for k in range(keep):
        number = kept_ref[k]
        top = (number // nblk) * BLOCK
        across = (number % nblk) * BLOCK
        window = across // LANES
        in_upper = jnp.full((half, LANES), across % LANES, jnp.int32) > 0
        for part in range(2):
            even = matrix_ref[part, window, pl.ds(top, half, 2), :]
            odd = matrix_ref[part, window, pl.ds(top + 1, half, 2), :]
            left = jnp.where(in_upper, pltpu.roll(even, BLOCK, 1), even)
            right = jnp.where(in_upper, odd, pltpu.roll(odd, BLOCK, 1))
            flat = jnp.where(lane < BLOCK, left, right)
            first = (cell * keep + k) * half
            for s in range(0, half, piece):
                owner, inside = divmod(first + s, share_rows)
                send_ref[e, owner, pl.ds(part * share_rows + inside, piece), :] = flat[s:s + piece]


def head_kernel(keep, share_rows, g_hbm, s_hbm, b_hbm, pattern_hbm, kept_hbm, lead_hbm,
                leaving_ref, send_ref, left_ref, right_ref, fresh_ref,
                pattern_ref, kept_ref, g_ref, s_ref, b_ref, lead_ref, state_ref, sems):
    energies, cells, _, size, _ = g_ref.shape
    position = lax.axis_index("chain")

    def fetch(slot, source, target):
        return pltpu.make_async_copy(source, target, sems.at[slot])

    lead_copy = fetch(0, lead_hbm, lead_ref)
    b_copies = [fetch(1 + i, b_hbm.at[i], b_ref.at[i]) for i in range(cells)]
    g_copies = [fetch(1 + cells + i, g_hbm.at[:, i], g_ref.at[:, i]) for i in range(cells)]
    s_copies = [fetch(1 + 2 * cells + i, s_hbm.at[:, i], s_ref.at[:, i]) for i in range(cells)]
    pattern_copy = fetch(1 + 3 * cells, pattern_hbm, pattern_ref)
    kept_copy = fetch(2 + 3 * cells, kept_hbm, kept_ref)
    pattern_copy.start()
    kept_copy.start()

    @pl.when(position == 0)
    def _():
        lead_copy.start()

    for i in range(cells):
        b_copies[i].start()
        g_copies[i].start()
        s_copies[i].start()
    pattern_copy.wait()
    kept_copy.wait()

    def bridge_of(i):
        mask = block_mask(pattern_ref, i, size)
        return b_ref[i, 0] * mask, b_ref[i, 1] * mask

    def matrix(ref, e, i):
        return ref[e, i, 0], ref[e, i, 1]

    @pl.when(position == 0)
    def _():
        lead_copy.wait()
        states = [(lead_ref[e, 0], lead_ref[e, 1]) for e in range(energies)]
        for i in range(cells):
            b_copies[i].wait()
            bridge = bridge_of(i)
            bridge_left, bridge_right = left_parts(bridge), right_parts(adjoint(bridge))
            for e in range(energies):
                entered = product(left_parts(product(bridge_left, right_parts(states[e]))), bridge_right)
                if e == 0:
                    g_copies[i].wait()
                    s_copies[i].wait()
                green = matrix(g_ref, e, i)
                green_left, green_right = left_parts(green), right_parts(adjoint(green))
                inner = right_parts(plus(matrix(s_ref, e, i), entered))
                states[e] = product(left_parts(product(green_left, inner)), green_right)
                out_ref = leaving_ref.at[e] if i == cells - 1 else state_ref.at[e, i]
                put_state(out_ref, states[e])
                pick_into(send_ref, e, i, out_ref, kept_ref, keep, share_rows)

    @pl.when(position > 0)
    def _():
        states, joined = [None] * energies, [None] * energies
        for i in range(cells):
            b_copies[i].wait()
            g_copies[i].wait()
            s_copies[i].wait()
            bridge = bridge_of(i)
            for e in range(energies):
                green = matrix(g_ref, e, i)
                green_left, green_right = left_parts(green), right_parts(adjoint(green))
                inner = matrix(s_ref, e, i)
                if i == 0:
                    joined[e] = product(green_left, right_parts(bridge))
                else:
                    bridge_left, bridge_right = left_parts(bridge), right_parts(adjoint(bridge))
                    half = left_parts(product(bridge_left, right_parts(states[e])))
                    across = right_parts(product(bridge_left, right_parts(joined[e])))
                    inner = plus(inner, product(half, bridge_right))
                    joined[e] = product(green_left, across)
                states[e] = product(left_parts(product(green_left, right_parts(inner))), green_right)
                left_ref[e, i, 0], left_ref[e, i, 1] = left_parts(joined[e])
                right_ref[e, i, 0], right_ref[e, i, 1] = right_parts(adjoint(joined[e]))
                fresh_ref[e, i, 0], fresh_ref[e, i, 1] = states[e]


def in_hbm(value):
    return pltpu.with_memory_space_constraint(value, pltpu.HBM)


def head(keep, share_rows, owners, retarded, lesser_sigma, coupling, pattern, kept_blocks, lead):
    energies, cells, _, size, _ = retarded.shape
    hbm = pl.BlockSpec(memory_space=pltpu.HBM)
    vmem = pl.BlockSpec(memory_space=pltpu.VMEM)
    state_shape = (2, size // LANES, size, LANES)
    return pl.pallas_call(
        functools.partial(head_kernel, keep, share_rows),
        out_shape=(
            jax.ShapeDtypeStruct((energies,) + state_shape, F32),
            jax.ShapeDtypeStruct((energies, owners, 2 * share_rows, LANES), F32),
            jax.ShapeDtypeStruct((energies, cells, 2, size, 2 * size), BF16),
            jax.ShapeDtypeStruct((energies, cells, 2, 2 * size, 2 * size), BF16),
            jax.ShapeDtypeStruct((energies, cells, 2, size, size), F32),
        ),
        in_specs=[hbm] * 6,
        out_specs=(vmem,) * 5,
        scratch_shapes=[
            pltpu.SMEM(pattern.shape, jnp.int32),
            pltpu.SMEM(kept_blocks.shape, jnp.int32),
            pltpu.VMEM(retarded.shape, F32),
            pltpu.VMEM(lesser_sigma.shape, F32),
            pltpu.VMEM(coupling.shape, F32),
            pltpu.VMEM(lead.shape, F32),
            pltpu.VMEM((energies, cells) + state_shape, F32),
            pltpu.SemaphoreType.DMA((3 + 3 * cells,)),
        ],
        compiler_params=pltpu.CompilerParams(vmem_limit_bytes=32 << 20),
        name="head_cells",
    )(*(in_hbm(x) for x in (retarded, lesser_sigma, coupling, pattern, kept_blocks, lead)))


def tail_kernel(keep, share_rows, hop, last, incoming_ref, left_ref, right_ref, fresh_ref, kept_hbm, *refs):
    if last:
        (_, send_ref), refs = refs[:2], refs[2:]
        leaving_ref = None
    else:
        (_, _, leaving_ref, send_ref), refs = refs[:4], refs[4:]
    kept_ref, state_ref, sem = refs
    energies, cells, _, size, _ = fresh_ref.shape

    @pl.when(lax.axis_index("chain") == hop + 1)
    def _():
        kept_copy = pltpu.make_async_copy(kept_hbm, kept_ref, sem)
        kept_copy.start()
        for e in range(energies):
            state = right_parts(get_state(incoming_ref.at[e]))
            halves = []
            for i in range(cells):
                halves.append(left_parts(product((left_ref[e, i, 0], left_ref[e, i, 1]), state)))
            for i in range(cells):
                grown = product(halves[i], (right_ref[e, i, 0], right_ref[e, i, 1]))
                put_state(state_ref.at[e, i], plus((fresh_ref[e, i, 0], fresh_ref[e, i, 1]), grown))
                if i == 0 and e == 0:
                    kept_copy.wait()
                pick_into(send_ref, e, i, state_ref.at[e, i], kept_ref, keep, share_rows)
            if not last:
                leaving_ref[e] = state_ref[e, cells - 1]


def tail(keep, share_rows, hop, last, incoming, left, right, fresh, kept_blocks, leaving, send):
    energies, cells = fresh.shape[:2]
    hbm = pl.BlockSpec(memory_space=pltpu.HBM)
    vmem = pl.BlockSpec(memory_space=pltpu.VMEM)
    carried = (send,) if last else (leaving, send)
    result = pl.pallas_call(
        functools.partial(tail_kernel, keep, share_rows, hop, last),
        out_shape=tuple(jax.ShapeDtypeStruct(value.shape, F32) for value in carried),
        in_specs=[vmem] * 4 + [hbm] + [vmem] * len(carried),
        out_specs=(vmem,) * len(carried),
        input_output_aliases={5 + i: i for i in range(len(carried))},
        scratch_shapes=[
            pltpu.SMEM(kept_blocks.shape, jnp.int32),
            pltpu.VMEM((energies, cells) + incoming.shape[1:], F32),
            pltpu.SemaphoreType.DMA,
        ],
        compiler_params=pltpu.CompilerParams(vmem_limit_bytes=32 << 20),
        name="tail_cells",
    )(incoming, left, right, fresh, in_hbm(kept_blocks), *carried)
    return (leaving, result[0]) if last else result


def lag_kernel(in_ref, out_ref):
    energies, double_rows, _ = in_ref.shape
    rows = double_rows // 2
    step = min(8, rows)
    scale = 1.0 / energies
    for first in range(0, rows, step):
        re = [in_ref[e, first:first + step] for e in range(energies)]
        im = [in_ref[e, rows + first:rows + first + step] for e in range(energies)]
        for lag in range(LAGS):
            real_sum = jnp.zeros((step, LANES), F32)
            imag_sum = jnp.zeros((step, LANES), F32)
            for e in range(energies - lag):
                real_sum += re[e + lag] * re[e] + im[e + lag] * im[e]
                imag_sum += im[e + lag] * re[e] - re[e + lag] * im[e]
            out_ref[lag, pl.ds(2 * first, step, 2), :] = real_sum * scale
            out_ref[lag, pl.ds(2 * first + 1, step, 2), :] = imag_sum * scale


def lag_sums(owned):
    energies, double_rows, lanes = owned.shape
    rows = double_rows // 2
    vmem = pl.BlockSpec(memory_space=pltpu.VMEM)
    sums = pl.pallas_call(
        lag_kernel,
        out_shape=jax.ShapeDtypeStruct((LAGS, double_rows, lanes), F32),
        in_specs=[vmem],
        out_specs=vmem,
        name="lag_sums",
    )(owned)
    sums = sums.reshape(LAGS, rows, 2, lanes)
    return jnp.swapaxes(sums, 1, 2).reshape(LAGS, 2, rows * lanes)


def per_device(retarded, lesser_sigma, coupling, coupling_pattern, kept_blocks, lead_lesser):
    cells = retarded.shape[1]
    keep = kept_blocks.shape[0]
    owners = lax.axis_size("energy")
    length = lax.axis_size("chain")
    share_rows = cells * keep * BLOCK * BLOCK // (owners * LANES)
    leaving, send, left, right, fresh = head(
        keep, share_rows, owners, retarded, lesser_sigma, coupling, coupling_pattern, kept_blocks, lead_lesser
    )
    for hop in range(length - 1):
        incoming = lax.ppermute(leaving, "chain", [(i, (i + 1) % length) for i in range(length)])
        last = hop == length - 2
        leaving, send = tail(keep, share_rows, hop, last, incoming, left, right, fresh, kept_blocks, leaving, send)
    owned = lax.all_to_all(send, "energy", split_axis=1, concat_axis=0, tiled=True)
    return lag_sums(owned.reshape((-1,) + owned.shape[2:]))


def solution(mesh):
    return jax.shard_map(
        per_device,
        mesh=mesh,
        in_specs=(
            P("energy", "chain", None, None, None),
            P("energy", "chain", None, None, None),
            P("chain", None, None, None),
            P("chain", None, None),
            P(),
            P("energy", None, None, None),
        ),
        out_specs=P(None, None, ("chain", "energy")),
        check_vma=False,
    )
```

```python
import functools

import jax
import jax.numpy as jnp
from jax import lax
from jax.experimental import pallas as pl
from jax.experimental.pallas import tpu as pltpu
from jax.sharding import PartitionSpec as P

BLOCK = 64
LAGS = 16
LANES = 128
F32 = jnp.float32
BF16 = jnp.bfloat16


def two_parts(value):
    high = value.astype(BF16)
    return high, (value - high.astype(F32)).astype(BF16)


def dot(left, right):
    return lax.dot_general(left, right, (((1,), (0,)), ((), ())), preferred_element_type=F32)


def left_parts(pair):
    return two_parts(jnp.concatenate(pair, axis=1))


def right_parts(pair):
    both = []
    for re, im in zip(two_parts(pair[0]), two_parts(pair[1])):
        both.append(jnp.concatenate([jnp.concatenate([re, im], axis=1), jnp.concatenate([-im, re], axis=1)], axis=0))
    return tuple(both)


def adjoint(pair):
    return pair[0].T, -pair[1].T


def product(left, right):
    wide = jnp.concatenate([left[0], left[0], left[1]], axis=1)
    tall = jnp.concatenate([right[0], right[1], right[0]], axis=0)
    both = dot(wide, tall)
    half = both.shape[1] // 2
    return both[:, :half], both[:, half:]


def plus(one, other):
    return one[0] + other[0], one[1] + other[1]


def put_state(state_ref, pair):
    for part in range(2):
        for group in range(state_ref.shape[1]):
            state_ref[part, group] = pair[part][:, group * LANES:(group + 1) * LANES]


def get_state(state_ref):
    groups = range(state_ref.shape[1])
    return tuple(jnp.concatenate([state_ref[part, group] for group in groups], axis=1) for part in range(2))


def block_mask(pattern_ref, cell, size):
    nblk = size // BLOCK
    column = lax.broadcasted_iota(jnp.int32, (BLOCK, size), 1) // BLOCK
    rows = []
    for r in range(nblk):
        row = jnp.zeros((BLOCK, size), F32)
        for c in range(nblk):
            row = jnp.where(column == c, pattern_ref[cell, r, c].astype(F32), row)
        rows.append(row)
    return jnp.concatenate(rows, axis=0)


def pick_into(send_ref, e, cell, matrix_ref, kept_ref, keep, share_rows):
    nblk = matrix_ref.shape[-2] // BLOCK
    half = BLOCK // 2
    lane = lax.broadcasted_iota(jnp.int32, (half, LANES), 1)
    piece = min(half, share_rows)
    for k in range(keep):
        number = kept_ref[k]
        top = (number // nblk) * BLOCK
        across = (number % nblk) * BLOCK
        window = across // LANES
        in_upper = jnp.full((half, LANES), across % LANES, jnp.int32) > 0
        for part in range(2):
            even = matrix_ref[part, window, pl.ds(top, half, 2), :]
            odd = matrix_ref[part, window, pl.ds(top + 1, half, 2), :]
            left = jnp.where(in_upper, pltpu.roll(even, BLOCK, 1), even)
            right = jnp.where(in_upper, odd, pltpu.roll(odd, BLOCK, 1))
            flat = jnp.where(lane < BLOCK, left, right)
            first = (cell * keep + k) * half
            for s in range(0, half, piece):
                owner, inside = divmod(first + s, share_rows)
                send_ref[e, send_ref.shape[1] - 1 - owner, pl.ds(part * share_rows + inside, piece), :] = flat[s:s + piece]


def head_kernel(keep, share_rows, g_hbm, s_hbm, b_hbm, pattern_hbm, kept_hbm, lead_hbm,
                leaving_ref, send_ref, left_ref, right_ref, fresh_ref,
                pattern_ref, kept_ref, g_ref, s_ref, b_ref, lead_ref, state_ref, sems):
    energies, cells, _, size, _ = g_ref.shape
    position = lax.axis_index("chain")

    def fetch(slot, source, target):
        return pltpu.make_async_copy(source, target, sems.at[slot])

    lead_copy = fetch(0, lead_hbm, lead_ref)
    b_copies = [fetch(1 + i, b_hbm.at[i], b_ref.at[i]) for i in range(cells)]
    g_copies = [fetch(1 + cells + i, g_hbm.at[:, i], g_ref.at[:, i]) for i in range(cells)]
    s_copies = [fetch(1 + 2 * cells + i, s_hbm.at[:, i], s_ref.at[:, i]) for i in range(cells)]
    pattern_copy = fetch(1 + 3 * cells, pattern_hbm, pattern_ref)
    kept_copy = fetch(2 + 3 * cells, kept_hbm, kept_ref)
    pattern_copy.start()
    kept_copy.start()

    @pl.when(position == 0)
    def _():
        lead_copy.start()

    for i in range(cells):
        b_copies[i].start()
        g_copies[i].start()
        s_copies[i].start()
    pattern_copy.wait()
    kept_copy.wait()

    def bridge_of(i):
        mask = block_mask(pattern_ref, i, size)
        return b_ref[i, 0] * mask, b_ref[i, 1] * mask

    def matrix(ref, e, i):
        return ref[e, i, 0], ref[e, i, 1]

    @pl.when(position == 0)
    def _():
        lead_copy.wait()
        states = [(lead_ref[e, 0], lead_ref[e, 1]) for e in range(energies)]
        for i in range(cells):
            b_copies[i].wait()
            bridge = bridge_of(i)
            bridge_left, bridge_right = left_parts(bridge), right_parts(adjoint(bridge))
            for e in range(energies):
                entered = product(left_parts(product(bridge_left, right_parts(states[e]))), bridge_right)
                if e == 0:
                    g_copies[i].wait()
                    s_copies[i].wait()
                green = matrix(g_ref, e, i)
                green_left, green_right = left_parts(green), right_parts(adjoint(green))
                inner = right_parts(plus(matrix(s_ref, e, i), entered))
                states[e] = product(left_parts(product(green_left, inner)), green_right)
                out_ref = leaving_ref.at[e] if i == cells - 1 else state_ref.at[e, i]
                put_state(out_ref, states[e])
                pick_into(send_ref, e, i, out_ref, kept_ref, keep, share_rows)

    @pl.when(position > 0)
    def _():
        states, joined = [None] * energies, [None] * energies
        for i in range(cells):
            b_copies[i].wait()
            g_copies[i].wait()
            s_copies[i].wait()
            bridge = bridge_of(i)
            for e in range(energies):
                green = matrix(g_ref, e, i)
                green_left, green_right = left_parts(green), right_parts(adjoint(green))
                inner = matrix(s_ref, e, i)
                if i == 0:
                    joined[e] = product(green_left, right_parts(bridge))
                else:
                    bridge_left, bridge_right = left_parts(bridge), right_parts(adjoint(bridge))
                    half = left_parts(product(bridge_left, right_parts(states[e])))
                    across = right_parts(product(bridge_left, right_parts(joined[e])))
                    inner = plus(inner, product(half, bridge_right))
                    joined[e] = product(green_left, across)
                states[e] = product(left_parts(product(green_left, right_parts(inner))), green_right)
                left_ref[e, i, 0], left_ref[e, i, 1] = left_parts(joined[e])
                right_ref[e, i, 0], right_ref[e, i, 1] = right_parts(adjoint(joined[e]))
                fresh_ref[e, i, 0], fresh_ref[e, i, 1] = states[e]


def in_hbm(value):
    return pltpu.with_memory_space_constraint(value, pltpu.HBM)


def head(keep, share_rows, owners, retarded, lesser_sigma, coupling, pattern, kept_blocks, lead):
    energies, cells, _, size, _ = retarded.shape
    hbm = pl.BlockSpec(memory_space=pltpu.HBM)
    vmem = pl.BlockSpec(memory_space=pltpu.VMEM)
    state_shape = (2, size // LANES, size, LANES)
    return pl.pallas_call(
        functools.partial(head_kernel, keep, share_rows),
        out_shape=(
            jax.ShapeDtypeStruct((energies,) + state_shape, F32),
            jax.ShapeDtypeStruct((energies, owners, 2 * share_rows, LANES), F32),
            jax.ShapeDtypeStruct((energies, cells, 2, size, 2 * size), BF16),
            jax.ShapeDtypeStruct((energies, cells, 2, 2 * size, 2 * size), BF16),
            jax.ShapeDtypeStruct((energies, cells, 2, size, size), F32),
        ),
        in_specs=[hbm] * 6,
        out_specs=(vmem,) * 5,
        scratch_shapes=[
            pltpu.SMEM(pattern.shape, jnp.int32),
            pltpu.SMEM(kept_blocks.shape, jnp.int32),
            pltpu.VMEM(retarded.shape, F32),
            pltpu.VMEM(lesser_sigma.shape, F32),
            pltpu.VMEM(coupling.shape, F32),
            pltpu.VMEM(lead.shape, F32),
            pltpu.VMEM((energies, cells) + state_shape, F32),
            pltpu.SemaphoreType.DMA((3 + 3 * cells,)),
        ],
        compiler_params=pltpu.CompilerParams(vmem_limit_bytes=32 << 20),
        name="head_cells",
    )(*(in_hbm(x) for x in (retarded, lesser_sigma, coupling, pattern, kept_blocks, lead)))


def tail_kernel(keep, share_rows, hop, last, incoming_ref, left_ref, right_ref, fresh_ref, kept_hbm, *refs):
    if last:
        (_, send_ref), refs = refs[:2], refs[2:]
        leaving_ref = None
    else:
        (_, _, leaving_ref, send_ref), refs = refs[:4], refs[4:]
    kept_ref, state_ref, sem = refs
    energies, cells, _, size, _ = fresh_ref.shape

    @pl.when(lax.axis_index("chain") == hop + 1)
    def _():
        kept_copy = pltpu.make_async_copy(kept_hbm, kept_ref, sem)
        kept_copy.start()
        for e in range(energies):
            state = right_parts(get_state(incoming_ref.at[e]))
            halves = []
            for i in range(cells):
                halves.append(left_parts(product((left_ref[e, i, 0], left_ref[e, i, 1]), state)))
            for i in range(cells):
                grown = product(halves[i], (right_ref[e, i, 0], right_ref[e, i, 1]))
                put_state(state_ref.at[e, i], plus((fresh_ref[e, i, 0], fresh_ref[e, i, 1]), grown))
                if i == 0 and e == 0:
                    kept_copy.wait()
                pick_into(send_ref, e, i, state_ref.at[e, i], kept_ref, keep, share_rows)
            if not last:
                leaving_ref[e] = state_ref[e, cells - 1]


def tail(keep, share_rows, hop, last, incoming, left, right, fresh, kept_blocks, leaving, send):
    energies, cells = fresh.shape[:2]
    hbm = pl.BlockSpec(memory_space=pltpu.HBM)
    vmem = pl.BlockSpec(memory_space=pltpu.VMEM)
    carried = (send,) if last else (leaving, send)
    result = pl.pallas_call(
        functools.partial(tail_kernel, keep, share_rows, hop, last),
        out_shape=tuple(jax.ShapeDtypeStruct(value.shape, F32) for value in carried),
        in_specs=[vmem] * 4 + [hbm] + [vmem] * len(carried),
        out_specs=(vmem,) * len(carried),
        input_output_aliases={5 + i: i for i in range(len(carried))},
        scratch_shapes=[
            pltpu.SMEM(kept_blocks.shape, jnp.int32),
            pltpu.VMEM((energies, cells) + incoming.shape[1:], F32),
            pltpu.SemaphoreType.DMA,
        ],
        compiler_params=pltpu.CompilerParams(vmem_limit_bytes=32 << 20),
        name="tail_cells",
    )(incoming, left, right, fresh, in_hbm(kept_blocks), *carried)
    return (leaving, result[0]) if last else result


def lag_kernel(here, in_ref, out_hbm, out_ref, sems):
    energies, double_rows, _ = in_ref.shape
    rows = double_rows // 2
    step = min(8, rows)
    scale = 1.0 / energies
    groups = sems.shape[0]
    width = LAGS // groups

    def at(e, first):
        place = (energies // here - 1 - e // here) * here + e % here
        return in_ref[place, first:first + step]

    copies = []
    for group in range(groups):
        for lag in range(group * width, (group + 1) * width):
            for first in range(0, rows, step):
                real_sum = jnp.zeros((step, LANES), F32)
                imag_sum = jnp.zeros((step, LANES), F32)
                for e in range(energies - lag):
                    late_re, late_im = at(e + lag, first), at(e + lag, rows + first)
                    early_re, early_im = at(e, first), at(e, rows + first)
                    real_sum += late_re * early_re + late_im * early_im
                    imag_sum += late_im * early_re - late_re * early_im
                out_ref[lag, pl.ds(2 * first, step, 2), :] = real_sum * scale
                out_ref[lag, pl.ds(2 * first + 1, step, 2), :] = imag_sum * scale
        part = pl.ds(group * width, width)
        copies.append(pltpu.make_async_copy(out_ref.at[part], out_hbm.at[part], sems.at[group]))
        copies[-1].start()
    for copy in copies:
        copy.wait()


def lag_sums(here, owned):
    energies, double_rows, lanes = owned.shape
    rows = double_rows // 2
    sums = pl.pallas_call(
        functools.partial(lag_kernel, here),
        out_shape=jax.ShapeDtypeStruct((LAGS, double_rows, lanes), F32),
        in_specs=[pl.BlockSpec(memory_space=pltpu.VMEM)],
        out_specs=pl.BlockSpec(memory_space=pltpu.HBM),
        scratch_shapes=[
            pltpu.VMEM((LAGS, double_rows, lanes), F32),
            pltpu.SemaphoreType.DMA((4,)),
        ],
        name="lag_sums",
    )(owned)
    sums = sums.reshape(LAGS, rows, 2, lanes)
    return jnp.swapaxes(sums, 1, 2).reshape(LAGS, 2, rows * lanes)


def per_device(retarded, lesser_sigma, coupling, coupling_pattern, kept_blocks, lead_lesser):
    cells = retarded.shape[1]
    keep = kept_blocks.shape[0]
    owners = lax.axis_size("energy")
    length = lax.axis_size("chain")
    share_rows = cells * keep * BLOCK * BLOCK // (owners * LANES)
    leaving, send, left, right, fresh = head(
        keep, share_rows, owners, retarded, lesser_sigma, coupling, coupling_pattern, kept_blocks, lead_lesser
    )
    for hop in range(length - 1):
        incoming = lax.ppermute(leaving, "chain", [(i, (i + 1) % length) for i in range(length)])
        last = hop == length - 2
        leaving, send = tail(keep, share_rows, hop, last, incoming, left, right, fresh, kept_blocks, leaving, send)
    backwards = [list(range(owners))[::-1]]
    owned = lax.all_to_all(send, "energy", split_axis=1, concat_axis=0, axis_index_groups=backwards, tiled=True)
    return lag_sums(retarded.shape[0], owned.reshape((-1,) + owned.shape[2:]))


def solution(mesh):
    return jax.shard_map(
        per_device,
        mesh=mesh,
        in_specs=(
            P("energy", "chain", None, None, None),
            P("energy", "chain", None, None, None),
            P("chain", None, None, None),
            P("chain", None, None),
            P(),
            P("energy", None, None, None),
        ),
        out_specs=P(None, None, ("chain", "energy")),
        check_vma=False,
    )
```

```python
import functools

import jax
import jax.numpy as jnp
from jax import lax
from jax.experimental import pallas as pl
from jax.experimental.pallas import tpu as pltpu
from jax.sharding import PartitionSpec as P

BLOCK = 64
LAGS = 16
LANES = 128
F32 = jnp.float32
BF16 = jnp.bfloat16


def two_parts(value):
    high = value.astype(BF16)
    return high, (value - high.astype(F32)).astype(BF16)


def dot(left, right):
    return lax.dot_general(left, right, (((1,), (0,)), ((), ())), preferred_element_type=F32)


def left_parts(pair):
    return two_parts(jnp.concatenate(pair, axis=1))


def right_parts(pair):
    both = []
    for re, im in zip(two_parts(pair[0]), two_parts(pair[1])):
        both.append(jnp.concatenate([jnp.concatenate([re, im], axis=1), jnp.concatenate([-im, re], axis=1)], axis=0))
    return tuple(both)


def adjoint(pair):
    return pair[0].T, -pair[1].T


def product(left, right):
    wide = jnp.concatenate([left[0], left[0], left[1]], axis=1)
    tall = jnp.concatenate([right[0], right[1], right[0]], axis=0)
    both = dot(wide, tall)
    half = both.shape[1] // 2
    return both[:, :half], both[:, half:]


def plus(one, other):
    return one[0] + other[0], one[1] + other[1]


def put_state(state_ref, pair):
    for part in range(2):
        for group in range(state_ref.shape[1]):
            state_ref[part, group] = pair[part][:, group * LANES:(group + 1) * LANES]


def get_state(state_ref):
    groups = range(state_ref.shape[1])
    return tuple(jnp.concatenate([state_ref[part, group] for group in groups], axis=1) for part in range(2))


def block_mask(pattern_ref, cell, size):
    nblk = size // BLOCK
    column = lax.broadcasted_iota(jnp.int32, (BLOCK, size), 1) // BLOCK
    rows = []
    for r in range(nblk):
        row = jnp.zeros((BLOCK, size), F32)
        for c in range(nblk):
            row = jnp.where(column == c, pattern_ref[cell, r, c].astype(F32), row)
        rows.append(row)
    return jnp.concatenate(rows, axis=0)


def sending_order(owners):
    half = [0]
    while len(half) * 2 < owners:
        half = [2 * n for n in half] + [2 * n + 1 for n in half]
    if len(half) * 2 != owners:
        return list(range(owners))[::-1]
    return [n for near in half for n in (owners - 1 - near, near)]


def pick_into(send_ref, e, cell, matrix_ref, kept_ref, keep, share_rows):
    order = sending_order(send_ref.shape[1])
    nblk = matrix_ref.shape[-2] // BLOCK
    half = BLOCK // 2
    lane = lax.broadcasted_iota(jnp.int32, (half, LANES), 1)
    piece = min(half, share_rows)
    for k in range(keep):
        number = kept_ref[k]
        top = (number // nblk) * BLOCK
        across = (number % nblk) * BLOCK
        window = across // LANES
        in_upper = jnp.full((half, LANES), across % LANES, jnp.int32) > 0
        for part in range(2):
            even = matrix_ref[part, window, pl.ds(top, half, 2), :]
            odd = matrix_ref[part, window, pl.ds(top + 1, half, 2), :]
            left = jnp.where(in_upper, pltpu.roll(even, BLOCK, 1), even)
            right = jnp.where(in_upper, odd, pltpu.roll(odd, BLOCK, 1))
            flat = jnp.where(lane < BLOCK, left, right)
            first = (cell * keep + k) * half
            for s in range(0, half, piece):
                owner, inside = divmod(first + s, share_rows)
                send_ref[e, order.index(owner), pl.ds(part * share_rows + inside, piece), :] = flat[s:s + piece]


def head_kernel(keep, share_rows, g_hbm, s_hbm, b_hbm, pattern_hbm, kept_hbm, lead_hbm,
                leaving_ref, send_ref, left_ref, right_ref, fresh_ref,
                pattern_ref, kept_ref, g_ref, s_ref, b_ref, lead_ref, state_ref, sems):
    energies, cells, _, size, _ = g_ref.shape
    position = lax.axis_index("chain")

    def fetch(slot, source, target):
        return pltpu.make_async_copy(source, target, sems.at[slot])

    lead_copy = fetch(0, lead_hbm, lead_ref)
    b_copies = [fetch(1 + i, b_hbm.at[i], b_ref.at[i]) for i in range(cells)]
    g_copies = [fetch(1 + cells + i, g_hbm.at[:, i], g_ref.at[:, i]) for i in range(cells)]
    s_copies = [fetch(1 + 2 * cells + i, s_hbm.at[:, i], s_ref.at[:, i]) for i in range(cells)]
    pattern_copy = fetch(1 + 3 * cells, pattern_hbm, pattern_ref)
    kept_copy = fetch(2 + 3 * cells, kept_hbm, kept_ref)
    pattern_copy.start()
    kept_copy.start()

    @pl.when(position == 0)
    def _():
        lead_copy.start()

    for i in range(cells):
        b_copies[i].start()
        g_copies[i].start()
        s_copies[i].start()
    pattern_copy.wait()
    kept_copy.wait()

    def bridge_of(i):
        mask = block_mask(pattern_ref, i, size)
        return b_ref[i, 0] * mask, b_ref[i, 1] * mask

    def matrix(ref, e, i):
        return ref[e, i, 0], ref[e, i, 1]

    @pl.when(position == 0)
    def _():
        lead_copy.wait()
        states = [(lead_ref[e, 0], lead_ref[e, 1]) for e in range(energies)]
        for i in range(cells):
            b_copies[i].wait()
            bridge = bridge_of(i)
            bridge_left, bridge_right = left_parts(bridge), right_parts(adjoint(bridge))
            for e in range(energies):
                entered = product(left_parts(product(bridge_left, right_parts(states[e]))), bridge_right)
                if e == 0:
                    g_copies[i].wait()
                    s_copies[i].wait()
                green = matrix(g_ref, e, i)
                green_left, green_right = left_parts(green), right_parts(adjoint(green))
                inner = right_parts(plus(matrix(s_ref, e, i), entered))
                states[e] = product(left_parts(product(green_left, inner)), green_right)
                out_ref = leaving_ref.at[e] if i == cells - 1 else state_ref.at[e, i]
                put_state(out_ref, states[e])
                pick_into(send_ref, e, i, out_ref, kept_ref, keep, share_rows)

    @pl.when(position > 0)
    def _():
        states, joined = [None] * energies, [None] * energies
        for i in range(cells):
            b_copies[i].wait()
            g_copies[i].wait()
            s_copies[i].wait()
            bridge = bridge_of(i)
            for e in range(energies):
                green = matrix(g_ref, e, i)
                green_left, green_right = left_parts(green), right_parts(adjoint(green))
                inner = matrix(s_ref, e, i)
                if i == 0:
                    joined[e] = product(green_left, right_parts(bridge))
                else:
                    bridge_left, bridge_right = left_parts(bridge), right_parts(adjoint(bridge))
                    half = left_parts(product(bridge_left, right_parts(states[e])))
                    across = right_parts(product(bridge_left, right_parts(joined[e])))
                    inner = plus(inner, product(half, bridge_right))
                    joined[e] = product(green_left, across)
                states[e] = product(left_parts(product(green_left, right_parts(inner))), green_right)
                left_ref[e, i, 0], left_ref[e, i, 1] = left_parts(joined[e])
                right_ref[e, i, 0], right_ref[e, i, 1] = right_parts(adjoint(joined[e]))
                fresh_ref[e, i, 0], fresh_ref[e, i, 1] = states[e]


def in_hbm(value):
    return pltpu.with_memory_space_constraint(value, pltpu.HBM)


def head(keep, share_rows, owners, retarded, lesser_sigma, coupling, pattern, kept_blocks, lead):
    energies, cells, _, size, _ = retarded.shape
    hbm = pl.BlockSpec(memory_space=pltpu.HBM)
    vmem = pl.BlockSpec(memory_space=pltpu.VMEM)
    state_shape = (2, size // LANES, size, LANES)
    return pl.pallas_call(
        functools.partial(head_kernel, keep, share_rows),
        out_shape=(
            jax.ShapeDtypeStruct((energies,) + state_shape, F32),
            jax.ShapeDtypeStruct((energies, owners, 2 * share_rows, LANES), F32),
            jax.ShapeDtypeStruct((energies, cells, 2, size, 2 * size), BF16),
            jax.ShapeDtypeStruct((energies, cells, 2, 2 * size, 2 * size), BF16),
            jax.ShapeDtypeStruct((energies, cells, 2, size, size), F32),
        ),
        in_specs=[hbm] * 6,
        out_specs=(vmem,) * 5,
        scratch_shapes=[
            pltpu.SMEM(pattern.shape, jnp.int32),
            pltpu.SMEM(kept_blocks.shape, jnp.int32),
            pltpu.VMEM(retarded.shape, F32),
            pltpu.VMEM(lesser_sigma.shape, F32),
            pltpu.VMEM(coupling.shape, F32),
            pltpu.VMEM(lead.shape, F32),
            pltpu.VMEM((energies, cells) + state_shape, F32),
            pltpu.SemaphoreType.DMA((3 + 3 * cells,)),
        ],
        compiler_params=pltpu.CompilerParams(vmem_limit_bytes=32 << 20),
        name="head_cells",
    )(*(in_hbm(x) for x in (retarded, lesser_sigma, coupling, pattern, kept_blocks, lead)))


def tail_kernel(keep, share_rows, hop, last, incoming_ref, left_ref, right_ref, fresh_ref, kept_hbm, *refs):
    if last:
        (_, send_ref), refs = refs[:2], refs[2:]
        leaving_ref = None
    else:
        (_, _, leaving_ref, send_ref), refs = refs[:4], refs[4:]
    kept_ref, state_ref, sem = refs
    energies, cells, _, size, _ = fresh_ref.shape

    @pl.when(lax.axis_index("chain") == hop + 1)
    def _():
        kept_copy = pltpu.make_async_copy(kept_hbm, kept_ref, sem)
        kept_copy.start()
        for e in range(energies):
            state = right_parts(get_state(incoming_ref.at[e]))
            halves = []
            for i in range(cells):
                halves.append(left_parts(product((left_ref[e, i, 0], left_ref[e, i, 1]), state)))
            for i in range(cells):
                grown = product(halves[i], (right_ref[e, i, 0], right_ref[e, i, 1]))
                put_state(state_ref.at[e, i], plus((fresh_ref[e, i, 0], fresh_ref[e, i, 1]), grown))
                if i == 0 and e == 0:
                    kept_copy.wait()
                pick_into(send_ref, e, i, state_ref.at[e, i], kept_ref, keep, share_rows)
            if not last:
                leaving_ref[e] = state_ref[e, cells - 1]


def tail(keep, share_rows, hop, last, incoming, left, right, fresh, kept_blocks, leaving, send):
    energies, cells = fresh.shape[:2]
    hbm = pl.BlockSpec(memory_space=pltpu.HBM)
    vmem = pl.BlockSpec(memory_space=pltpu.VMEM)
    carried = (send,) if last else (leaving, send)
    result = pl.pallas_call(
        functools.partial(tail_kernel, keep, share_rows, hop, last),
        out_shape=tuple(jax.ShapeDtypeStruct(value.shape, F32) for value in carried),
        in_specs=[vmem] * 4 + [hbm] + [vmem] * len(carried),
        out_specs=(vmem,) * len(carried),
        input_output_aliases={5 + i: i for i in range(len(carried))},
        scratch_shapes=[
            pltpu.SMEM(kept_blocks.shape, jnp.int32),
            pltpu.VMEM((energies, cells) + incoming.shape[1:], F32),
            pltpu.SemaphoreType.DMA,
        ],
        compiler_params=pltpu.CompilerParams(vmem_limit_bytes=32 << 20),
        name="tail_cells",
    )(incoming, left, right, fresh, in_hbm(kept_blocks), *carried)
    return (leaving, result[0]) if last else result


def lag_kernel(here, in_ref, out_hbm, out_ref, sems):
    energies, double_rows, _ = in_ref.shape
    rows = double_rows // 2
    step = min(8, rows)
    scale = 1.0 / energies
    groups = sems.shape[0]
    width = LAGS // groups

    order = sending_order(energies // here)

    def at(e, part):
        place = order.index(e // here) * here + e % here
        start = part * rows
        return [in_ref[place, start + first:start + first + step] for first in range(0, rows, step)]

    copies = []
    for group in range(groups):
        lags = range(group * width, (group + 1) * width)
        sums = {}
        for e in range(energies):
            early_re, early_im = at(e, 0), at(e, 1)
            for lag in lags:
                if e + lag >= energies:
                    continue
                late_re, late_im = at(e + lag, 0), at(e + lag, 1)
                for n in range(rows // step):
                    re = late_re[n] * early_re[n] + late_im[n] * early_im[n]
                    im = late_im[n] * early_re[n] - late_re[n] * early_im[n]
                    if (lag, n) in sums:
                        re, im = sums[lag, n][0] + re, sums[lag, n][1] + im
                    sums[lag, n] = re, im
        for (lag, n), (re, im) in sums.items():
            out_ref[lag, pl.ds(2 * n * step, step, 2), :] = re * scale
            out_ref[lag, pl.ds(2 * n * step + 1, step, 2), :] = im * scale
        part = pl.ds(group * width, width)
        copies.append(pltpu.make_async_copy(out_ref.at[part], out_hbm.at[part], sems.at[group]))
        copies[-1].start()
    for copy in copies:
        copy.wait()


def lag_sums(here, owned):
    energies, double_rows, lanes = owned.shape
    rows = double_rows // 2
    sums = pl.pallas_call(
        functools.partial(lag_kernel, here),
        out_shape=jax.ShapeDtypeStruct((LAGS, double_rows, lanes), F32),
        in_specs=[pl.BlockSpec(memory_space=pltpu.VMEM)],
        out_specs=pl.BlockSpec(memory_space=pltpu.HBM),
        scratch_shapes=[
            pltpu.VMEM((LAGS, double_rows, lanes), F32),
            pltpu.SemaphoreType.DMA((4,)),
        ],
        name="lag_sums",
    )(owned)
    sums = sums.reshape(LAGS, rows, 2, lanes)
    return jnp.swapaxes(sums, 1, 2).reshape(LAGS, 2, rows * lanes)


def per_device(retarded, lesser_sigma, coupling, coupling_pattern, kept_blocks, lead_lesser):
    cells = retarded.shape[1]
    keep = kept_blocks.shape[0]
    owners = lax.axis_size("energy")
    length = lax.axis_size("chain")
    share_rows = cells * keep * BLOCK * BLOCK // (owners * LANES)
    leaving, send, left, right, fresh = head(
        keep, share_rows, owners, retarded, lesser_sigma, coupling, coupling_pattern, kept_blocks, lead_lesser
    )
    for hop in range(length - 1):
        incoming = lax.ppermute(leaving, "chain", [(i, (i + 1) % length) for i in range(length)])
        last = hop == length - 2
        leaving, send = tail(keep, share_rows, hop, last, incoming, left, right, fresh, kept_blocks, leaving, send)
    groups = [sending_order(owners)]
    owned = lax.all_to_all(send, "energy", split_axis=1, concat_axis=0, axis_index_groups=groups, tiled=True)
    return lag_sums(retarded.shape[0], owned.reshape((-1,) + owned.shape[2:]))


def solution(mesh):
    return jax.shard_map(
        per_device,
        mesh=mesh,
        in_specs=(
            P("energy", "chain", None, None, None),
            P("energy", "chain", None, None, None),
            P("chain", None, None, None),
            P("chain", None, None),
            P(),
            P("energy", None, None, None),
        ),
        out_specs=P(None, None, ("chain", "energy")),
        check_vma=False,
    )
```

```python
import functools

import jax
import jax.numpy as jnp
from jax import lax
from jax.experimental import pallas as pl
from jax.experimental.pallas import tpu as pltpu
from jax.sharding import PartitionSpec as P

BLOCK = 64
LAGS = 16
LANES = 128
F32 = jnp.float32
BF16 = jnp.bfloat16


def two_parts(value):
    high = value.astype(BF16)
    return high, (value - high.astype(F32)).astype(BF16)


def dot(left, right):
    return lax.dot_general(left, right, (((1,), (0,)), ((), ())), preferred_element_type=F32)


def left_parts(pair):
    return two_parts(jnp.concatenate(pair, axis=1))


def right_parts(pair):
    both = []
    for re, im in zip(two_parts(pair[0]), two_parts(pair[1])):
        both.append(jnp.concatenate([jnp.concatenate([re, im], axis=1), jnp.concatenate([-im, re], axis=1)], axis=0))
    return tuple(both)


def adjoint(pair):
    return pair[0].T, -pair[1].T


def product(left, right):
    wide = jnp.concatenate([left[0], left[0], left[1]], axis=1)
    tall = jnp.concatenate([right[0], right[1], right[0]], axis=0)
    both = dot(wide, tall)
    half = both.shape[1] // 2
    return both[:, :half], both[:, half:]


def plus(one, other):
    return one[0] + other[0], one[1] + other[1]


def put_state(state_ref, pair):
    for part in range(2):
        for group in range(state_ref.shape[1]):
            state_ref[part, group] = pair[part][:, group * LANES:(group + 1) * LANES]


def get_state(state_ref):
    groups = range(state_ref.shape[1])
    return tuple(jnp.concatenate([state_ref[part, group] for group in groups], axis=1) for part in range(2))


def block_mask(size, value_of):
    nblk = size // BLOCK
    column = lax.broadcasted_iota(jnp.int32, (BLOCK, size), 1) // BLOCK
    rows = []
    for r in range(nblk):
        row = jnp.zeros((BLOCK, size), F32)
        for c in range(nblk):
            row = jnp.where(column == c, value_of(r, c).astype(F32), row)
        rows.append(row)
    return jnp.concatenate(rows, axis=0)


def pick_into(send_ref, e, cell, matrix_ref, kept_ref, keep, share_rows):
    nblk = matrix_ref.shape[-2] // BLOCK
    owners = send_ref.shape[1]
    half = BLOCK // 2
    lane = lax.broadcasted_iota(jnp.int32, (half, LANES), 1)
    piece = min(half, share_rows)
    per_share = share_rows // piece
    for k in range(keep):
        number = kept_ref[k]
        top = (number // nblk) * BLOCK
        across = (number % nblk) * BLOCK
        window = across // LANES
        in_upper = jnp.full((half, LANES), across % LANES, jnp.int32) > 0
        for part in range(2):
            even = matrix_ref[part, window, pl.ds(top, half, 2), :]
            odd = matrix_ref[part, window, pl.ds(top + 1, half, 2), :]
            left = jnp.where(in_upper, pltpu.roll(even, BLOCK, 1), even)
            right = jnp.where(in_upper, odd, pltpu.roll(odd, BLOCK, 1))
            flat = jnp.where(lane < BLOCK, left, right)
            for s in range(half // piece):
                index = (cell * keep + k) * (half // piece) + s
                owner, inside = index, 0
                if per_share > 1:
                    owner, inside = index // per_share, pl.multiple_of(index % per_share * piece, piece)
                rows = pl.ds(part * share_rows + inside, piece)
                send_ref[e, owners - 1 - owner, rows, :] = flat[s * piece:(s + 1) * piece]


def put_parts(ref, parts):
    ref[0], ref[1] = parts


def parts_of(ref):
    return ref[0], ref[1]


def head_kernel(keep, share_rows, g_hbm, s_hbm, b_hbm, pattern_hbm, kept_hbm, lead_hbm,
                leaving_ref, send_ref, left_ref, right_ref, fresh_ref,
                pattern_ref, kept_ref, m_ref, s_ref, lead_ref, m_left, state_right, joined_right, sems, m_sems):
    energies, cells, _, size, _ = s_ref.shape
    position = lax.axis_index("chain")
    is_first = position == 0

    def m_copy(e, k, i, source_hbm):
        source = source_hbm.at[i] if source_hbm is b_hbm else source_hbm.at[e, i]
        return pltpu.make_async_copy(source, m_ref.at[e, k], m_sems.at[e, k])

    lead_copy = pltpu.make_async_copy(lead_hbm, lead_ref, sems.at[0])
    pattern_copy = pltpu.make_async_copy(pattern_hbm, pattern_ref, sems.at[1])
    kept_copy = pltpu.make_async_copy(kept_hbm, kept_ref, sems.at[2])

    def s_copy(i):
        return pltpu.make_async_copy(s_hbm.at[:, i], s_ref.at[:, i], sems.at[3 + i])

    pattern_copy.start()
    kept_copy.start()

    @pl.when(is_first)
    def _():
        lead_copy.start()

    for i in range(cells):
        for e in range(energies):
            m_copy(e, 2 * i, i, b_hbm).start()
        s_copy(i).start()
        for e in range(energies):
            m_copy(e, 2 * i + 1, i, g_hbm).start()
    pattern_copy.wait()
    kept_copy.wait()

    def matrix(ref, e, i):
        return ref[e, i, 0], ref[e, i, 1]

    def masked(e, k):
        bridge = k % 2 == 0
        mask = block_mask(size, lambda r, c: jnp.where(bridge, pattern_ref[k // 2, r, c], 1))
        return m_ref[e, k, 0] * mask, m_ref[e, k, 1] * mask

    @pl.when(is_first)
    def _():
        lead_copy.wait()
        for e in range(energies):
            put_parts(state_right.at[e], right_parts((lead_ref[e, 0], lead_ref[e, 1])))

    @pl.when(jnp.logical_not(is_first))
    def _():
        s_copy(0).wait()
        for e in range(energies):
            m_copy(e, 0, 0, b_hbm).wait()
            put_parts(state_right.at[e], right_parts(matrix(s_ref, e, 0)))
            put_parts(joined_right.at[e], right_parts(masked(e, 0)))

    def step(k, carry):
        cell = k // 2
        done = k % 2 == 1

        @pl.when(jnp.logical_not(done))
        def _():
            s_copy(cell).wait()

        kept_share = (1 - k % 2).astype(F32)
        for e in range(energies):
            m_copy(e, k, 0, b_hbm).wait()
            factor = masked(e, k)
            left = left_parts(factor)
            put_parts(m_left, left)
            half = left_parts(product(left, parts_of(state_right.at[e])))
            grown = product(half, right_parts(adjoint(factor)))
            added = matrix(s_ref, e, cell)
            state = plus(grown, (added[0] * kept_share, added[1] * kept_share))
            put_parts(state_right.at[e], right_parts(state))
            put_state(fresh_ref.at[e, cell], state)

            @pl.when(jnp.logical_not(is_first))
            def _():
                joined = product(parts_of(m_left), parts_of(joined_right.at[e]))
                put_parts(joined_right.at[e], right_parts(joined))

                @pl.when(done)
                def _():
                    put_parts(left_ref.at[e, cell], left_parts(joined))
                    put_parts(right_ref.at[e, cell], right_parts(adjoint(joined)))

            @pl.when(jnp.logical_and(is_first, done))
            def _():
                pick_into(send_ref, e, cell, fresh_ref.at[e, cell], kept_ref, keep, share_rows)

        return carry

    lax.fori_loop(jnp.where(is_first, 0, 1), 2 * cells, step, 0)

    @pl.when(is_first)
    def _():
        for e in range(energies):
            leaving_ref[e] = fresh_ref[e, cells - 1]


def in_hbm(value):
    return pltpu.with_memory_space_constraint(value, pltpu.HBM)


def head(keep, share_rows, owners, retarded, lesser_sigma, coupling, pattern, kept_blocks, lead):
    energies, cells, _, size, _ = retarded.shape
    hbm = pl.BlockSpec(memory_space=pltpu.HBM)
    vmem = pl.BlockSpec(memory_space=pltpu.VMEM)
    state_shape = (2, size // LANES, size, LANES)
    return pl.pallas_call(
        functools.partial(head_kernel, keep, share_rows),
        out_shape=(
            jax.ShapeDtypeStruct((energies,) + state_shape, F32),
            jax.ShapeDtypeStruct((energies, owners, 2 * share_rows, LANES), F32),
            jax.ShapeDtypeStruct((energies, cells, 2, size, 2 * size), BF16),
            jax.ShapeDtypeStruct((energies, cells, 2, 2 * size, 2 * size), BF16),
            jax.ShapeDtypeStruct((energies, cells) + state_shape, F32),
        ),
        in_specs=[hbm] * 6,
        out_specs=(vmem,) * 5,
        scratch_shapes=[
            pltpu.SMEM(pattern.shape, jnp.int32),
            pltpu.SMEM(kept_blocks.shape, jnp.int32),
            pltpu.VMEM((energies, 2 * cells, 2, size, size), F32),
            pltpu.VMEM(lesser_sigma.shape, F32),
            pltpu.VMEM(lead.shape, F32),
            pltpu.VMEM((2, size, 2 * size), BF16),
            pltpu.VMEM((energies, 2, 2 * size, 2 * size), BF16),
            pltpu.VMEM((energies, 2, 2 * size, 2 * size), BF16),
            pltpu.SemaphoreType.DMA((3 + cells,)),
            pltpu.SemaphoreType.DMA((energies, 2 * cells)),
        ],
        compiler_params=pltpu.CompilerParams(vmem_limit_bytes=32 << 20),
        name="head_cells",
    )(*(in_hbm(x) for x in (retarded, lesser_sigma, coupling, pattern, kept_blocks, lead)))


def tail_kernel(keep, share_rows, hop, last, incoming_ref, left_ref, right_ref, fresh_ref, kept_hbm, *refs):
    if last:
        (_, send_ref), refs = refs[:2], refs[2:]
        leaving_ref = None
    else:
        (_, _, leaving_ref, send_ref), refs = refs[:4], refs[4:]
    kept_ref, state_ref, state_right, sem = refs
    energies, cells = fresh_ref.shape[:2]

    @pl.when(lax.axis_index("chain") == hop + 1)
    def _():
        kept_copy = pltpu.make_async_copy(kept_hbm, kept_ref, sem)
        kept_copy.start()
        for e in range(energies):
            put_parts(state_right.at[e], right_parts(get_state(incoming_ref.at[e])))
        kept_copy.wait()

        def step(i, carry):
            for e in range(energies):
                half = left_parts(product(parts_of(left_ref.at[e, i]), parts_of(state_right.at[e])))
                grown = product(half, parts_of(right_ref.at[e, i]))
                put_state(state_ref.at[e], plus(get_state(fresh_ref.at[e, i]), grown))
                pick_into(send_ref, e, i, state_ref.at[e], kept_ref, keep, share_rows)
            return carry

        lax.fori_loop(0, cells, step, 0)
        if not last:
            leaving_ref[...] = state_ref[...]


def tail(keep, share_rows, hop, last, incoming, left, right, fresh, kept_blocks, leaving, send):
    energies = fresh.shape[0]
    hbm = pl.BlockSpec(memory_space=pltpu.HBM)
    vmem = pl.BlockSpec(memory_space=pltpu.VMEM)
    carried = (send,) if last else (leaving, send)
    result = pl.pallas_call(
        functools.partial(tail_kernel, keep, share_rows, hop, last),
        out_shape=tuple(jax.ShapeDtypeStruct(value.shape, F32) for value in carried),
        in_specs=[vmem] * 4 + [hbm] + [vmem] * len(carried),
        out_specs=(vmem,) * len(carried),
        input_output_aliases={5 + i: i for i in range(len(carried))},
        scratch_shapes=[
            pltpu.SMEM(kept_blocks.shape, jnp.int32),
            pltpu.VMEM(incoming.shape, F32),
            pltpu.VMEM((energies,) + right.shape[2:], BF16),
            pltpu.SemaphoreType.DMA,
        ],
        compiler_params=pltpu.CompilerParams(vmem_limit_bytes=32 << 20),
        name="tail_cells",
    )(incoming, left, right, fresh, in_hbm(kept_blocks), *carried)
    return (leaving, result[0]) if last else result


def lag_kernel(here, in_ref, out_hbm, out_ref, all_ref, sems):
    energies, double_rows, _ = in_ref.shape
    rows = double_rows // 2
    step = min(8, rows)
    scale = 1.0 / energies
    for e in range(energies):
        all_ref[e] = in_ref[(energies // here - 1 - e // here) * here + e % here]
    for e in range(energies, all_ref.shape[0]):
        all_ref[e] = jnp.zeros((double_rows, LANES), F32)

    def out_copy(lag):
        return pltpu.make_async_copy(out_ref.at[lag], out_hbm.at[lag], sems.at[lag])

    def one_lag(lag, carry):
        for first in range(0, rows, step):
            sums = [jnp.zeros((step, LANES), F32) for _ in range(4)]
            for e in range(energies):
                early_re, early_im = all_ref[e, pl.ds(first, step)], all_ref[e, pl.ds(rows + first, step)]
                late_re, late_im = all_ref[e + lag, pl.ds(first, step)], all_ref[e + lag, pl.ds(rows + first, step)]
                sums[0] += late_re * early_re
                sums[1] += late_im * early_im
                sums[2] += late_im * early_re
                sums[3] += late_re * early_im
            out_ref[lag, pl.ds(2 * first, step, 2), :] = (sums[0] + sums[1]) * scale
            out_ref[lag, pl.ds(2 * first + 1, step, 2), :] = (sums[2] - sums[3]) * scale
        out_copy(lag).start()
        return carry

    def finish(lag, carry):
        out_copy(lag).wait()
        return carry

    lax.fori_loop(0, LAGS, one_lag, 0)
    lax.fori_loop(0, LAGS, finish, 0)


def lag_sums(here, owned):
    energies, double_rows, lanes = owned.shape
    rows = double_rows // 2
    sums = pl.pallas_call(
        functools.partial(lag_kernel, here),
        out_shape=jax.ShapeDtypeStruct((LAGS, double_rows, lanes), F32),
        in_specs=[pl.BlockSpec(memory_space=pltpu.VMEM)],
        out_specs=pl.BlockSpec(memory_space=pltpu.HBM),
        scratch_shapes=[
            pltpu.VMEM((LAGS, double_rows, lanes), F32),
            pltpu.VMEM((energies + LAGS - 1, double_rows, lanes), F32),
            pltpu.SemaphoreType.DMA((LAGS,)),
        ],
        name="lag_sums",
    )(owned)
    sums = sums.reshape(LAGS, rows, 2, lanes)
    return jnp.swapaxes(sums, 1, 2).reshape(LAGS, 2, rows * lanes)


def per_device(retarded, lesser_sigma, coupling, coupling_pattern, kept_blocks, lead_lesser):
    cells = retarded.shape[1]
    keep = kept_blocks.shape[0]
    owners = lax.axis_size("energy")
    length = lax.axis_size("chain")
    share_rows = cells * keep * BLOCK * BLOCK // (owners * LANES)
    leaving, send, left, right, fresh = head(
        keep, share_rows, owners, retarded, lesser_sigma, coupling, coupling_pattern, kept_blocks, lead_lesser
    )
    for hop in range(length - 1):
        incoming = lax.ppermute(leaving, "chain", [(i, (i + 1) % length) for i in range(length)])
        last = hop == length - 2
        leaving, send = tail(keep, share_rows, hop, last, incoming, left, right, fresh, kept_blocks, leaving, send)
    backwards = [list(range(owners))[::-1]]
    owned = lax.all_to_all(send, "energy", split_axis=1, concat_axis=0, axis_index_groups=backwards, tiled=True)
    return lag_sums(retarded.shape[0], owned.reshape((-1,) + owned.shape[2:]))


def solution(mesh):
    return jax.shard_map(
        per_device,
        mesh=mesh,
        in_specs=(
            P("energy", "chain", None, None, None),
            P("energy", "chain", None, None, None),
            P("chain", None, None, None),
            P("chain", None, None),
            P(),
            P("energy", None, None, None),
        ),
        out_specs=P(None, None, ("chain", "energy")),
        check_vma=False,
    )
```

```python
import functools

import jax
import jax.numpy as jnp
from jax import lax
from jax.experimental import pallas as pl
from jax.experimental.pallas import tpu as pltpu
from jax.sharding import PartitionSpec as P

BLOCK = 64
LAGS = 16
LANES = 128
F32 = jnp.float32
BF16 = jnp.bfloat16


def two_parts(value):
    high = value.astype(BF16)
    return high, (value - high.astype(F32)).astype(BF16)


def dot(left, right):
    return lax.dot_general(left, right, (((1,), (0,)), ((), ())), preferred_element_type=F32)


def parts(pair):
    return tuple(part for value in (pair[0], pair[1], pair[0] + pair[1]) for part in two_parts(value))


def adjoint(pair):
    return pair[0].T, -pair[1].T


def product(left, right):
    real = []
    for n in range(0, 6, 2):
        wide = jnp.concatenate([left[n], left[n], left[n + 1]], axis=1)
        tall = jnp.concatenate([right[n], right[n + 1], right[n]], axis=0)
        real.append(dot(wide, tall))
    return real[0] - real[1], real[2] - real[0] - real[1]


def put_parts(ref, values):
    for n, value in enumerate(values):
        ref[n] = value


def get_parts(ref):
    return tuple(ref[n] for n in range(6))


def plus(one, other):
    return one[0] + other[0], one[1] + other[1]


def put_state(state_ref, pair):
    for part in range(2):
        for group in range(state_ref.shape[1]):
            state_ref[part, group] = pair[part][:, group * LANES:(group + 1) * LANES]


def get_state(state_ref):
    groups = range(state_ref.shape[1])
    return tuple(jnp.concatenate([state_ref[part, group] for group in groups], axis=1) for part in range(2))


def block_mask(pattern_ref, cell, size):
    nblk = size // BLOCK
    column = lax.broadcasted_iota(jnp.int32, (BLOCK, size), 1) // BLOCK
    rows = []
    for r in range(nblk):
        row = jnp.zeros((BLOCK, size), F32)
        for c in range(nblk):
            row = jnp.where(column == c, pattern_ref[cell, r, c].astype(F32), row)
        rows.append(row)
    return jnp.concatenate(rows, axis=0)


def pick_into(send_ref, e, cell, matrix_ref, kept_ref, keep, share_rows):
    nblk = matrix_ref.shape[-2] // BLOCK
    half = BLOCK // 2
    lane = lax.broadcasted_iota(jnp.int32, (half, LANES), 1)
    piece = min(half, share_rows)
    for k in range(keep):
        number = kept_ref[k]
        top = (number // nblk) * BLOCK
        across = (number % nblk) * BLOCK
        window = across // LANES
        in_upper = jnp.full((half, LANES), across % LANES, jnp.int32) > 0
        for part in range(2):
            even = matrix_ref[part, window, pl.ds(top, half, 2), :]
            odd = matrix_ref[part, window, pl.ds(top + 1, half, 2), :]
            left = jnp.where(in_upper, pltpu.roll(even, BLOCK, 1), even)
            right = jnp.where(in_upper, odd, pltpu.roll(odd, BLOCK, 1))
            flat = jnp.where(lane < BLOCK, left, right)
            first = (cell * keep + k) * half
            for s in range(0, half, piece):
                owner, inside = divmod(first + s, share_rows)
                send_ref[e, send_ref.shape[1] - 1 - owner, pl.ds(part * share_rows + inside, piece), :] = flat[s:s + piece]


def head_kernel(keep, share_rows, g_hbm, s_hbm, b_hbm, pattern_hbm, kept_hbm, lead_hbm,
                leaving_ref, send_ref, left_ref, right_ref, fresh_ref,
                pattern_ref, kept_ref, g_ref, s_ref, b_ref, lead_ref, state_ref, sems):
    energies, cells, _, size, _ = g_ref.shape
    position = lax.axis_index("chain")

    def fetch(slot, source, target):
        return pltpu.make_async_copy(source, target, sems.at[slot])

    lead_copy = fetch(0, lead_hbm, lead_ref)
    b_copies = [fetch(1 + i, b_hbm.at[i], b_ref.at[i]) for i in range(cells)]
    g_copies = [fetch(1 + cells + i, g_hbm.at[:, i], g_ref.at[:, i]) for i in range(cells)]
    s_copies = [fetch(1 + 2 * cells + i, s_hbm.at[:, i], s_ref.at[:, i]) for i in range(cells)]
    pattern_copy = fetch(1 + 3 * cells, pattern_hbm, pattern_ref)
    kept_copy = fetch(2 + 3 * cells, kept_hbm, kept_ref)
    pattern_copy.start()
    kept_copy.start()

    @pl.when(position == 0)
    def _():
        lead_copy.start()

    for i in range(cells):
        b_copies[i].start()
        g_copies[i].start()
        s_copies[i].start()
    pattern_copy.wait()
    kept_copy.wait()

    def bridge_of(i):
        mask = block_mask(pattern_ref, i, size)
        return b_ref[i, 0] * mask, b_ref[i, 1] * mask

    def matrix(ref, e, i):
        return ref[e, i, 0], ref[e, i, 1]

    @pl.when(position == 0)
    def _():
        lead_copy.wait()
        states = [(lead_ref[e, 0], lead_ref[e, 1]) for e in range(energies)]
        for i in range(cells):
            b_copies[i].wait()
            bridge = bridge_of(i)
            bridge_left, bridge_right = parts(bridge), parts(adjoint(bridge))
            for e in range(energies):
                entered = product(parts(product(bridge_left, parts(states[e]))), bridge_right)
                if e == 0:
                    g_copies[i].wait()
                    s_copies[i].wait()
                green = matrix(g_ref, e, i)
                green_left, green_right = parts(green), parts(adjoint(green))
                inner = parts(plus(matrix(s_ref, e, i), entered))
                states[e] = product(parts(product(green_left, inner)), green_right)
                out_ref = leaving_ref.at[e] if i == cells - 1 else state_ref.at[e, i]
                put_state(out_ref, states[e])
                pick_into(send_ref, e, i, out_ref, kept_ref, keep, share_rows)

    @pl.when(position > 0)
    def _():
        states, joined = [None] * energies, [None] * energies
        for i in range(cells):
            b_copies[i].wait()
            g_copies[i].wait()
            s_copies[i].wait()
            bridge = bridge_of(i)
            for e in range(energies):
                green = matrix(g_ref, e, i)
                green_left, green_right = parts(green), parts(adjoint(green))
                inner = matrix(s_ref, e, i)
                if i == 0:
                    joined[e] = product(green_left, parts(bridge))
                else:
                    bridge_left, bridge_right = parts(bridge), parts(adjoint(bridge))
                    half = parts(product(bridge_left, parts(states[e])))
                    across = parts(product(bridge_left, parts(joined[e])))
                    inner = plus(inner, product(half, bridge_right))
                    joined[e] = product(green_left, across)
                states[e] = product(parts(product(green_left, parts(inner))), green_right)
                put_parts(left_ref.at[e, i], parts(joined[e]))
                put_parts(right_ref.at[e, i], parts(adjoint(joined[e])))
                fresh_ref[e, i, 0], fresh_ref[e, i, 1] = states[e]


def in_hbm(value):
    return pltpu.with_memory_space_constraint(value, pltpu.HBM)


def head(keep, share_rows, owners, retarded, lesser_sigma, coupling, pattern, kept_blocks, lead):
    energies, cells, _, size, _ = retarded.shape
    hbm = pl.BlockSpec(memory_space=pltpu.HBM)
    vmem = pl.BlockSpec(memory_space=pltpu.VMEM)
    state_shape = (2, size // LANES, size, LANES)
    return pl.pallas_call(
        functools.partial(head_kernel, keep, share_rows),
        out_shape=(
            jax.ShapeDtypeStruct((energies,) + state_shape, F32),
            jax.ShapeDtypeStruct((energies, owners, 2 * share_rows, LANES), F32),
            jax.ShapeDtypeStruct((energies, cells, 6, size, size), BF16),
            jax.ShapeDtypeStruct((energies, cells, 6, size, size), BF16),
            jax.ShapeDtypeStruct((energies, cells, 2, size, size), F32),
        ),
        in_specs=[hbm] * 6,
        out_specs=(vmem,) * 5,
        scratch_shapes=[
            pltpu.SMEM(pattern.shape, jnp.int32),
            pltpu.SMEM(kept_blocks.shape, jnp.int32),
            pltpu.VMEM(retarded.shape, F32),
            pltpu.VMEM(lesser_sigma.shape, F32),
            pltpu.VMEM(coupling.shape, F32),
            pltpu.VMEM(lead.shape, F32),
            pltpu.VMEM((energies, cells) + state_shape, F32),
            pltpu.SemaphoreType.DMA((3 + 3 * cells,)),
        ],
        compiler_params=pltpu.CompilerParams(vmem_limit_bytes=32 << 20),
        name="head_cells",
    )(*(in_hbm(x) for x in (retarded, lesser_sigma, coupling, pattern, kept_blocks, lead)))


def tail_kernel(keep, share_rows, hop, last, incoming_ref, left_ref, right_ref, fresh_ref, kept_hbm, *refs):
    if last:
        (_, send_ref), refs = refs[:2], refs[2:]
        leaving_ref = None
    else:
        (_, _, leaving_ref, send_ref), refs = refs[:4], refs[4:]
    kept_ref, state_ref, sem = refs
    energies, cells, _, size, _ = fresh_ref.shape

    @pl.when(lax.axis_index("chain") == hop + 1)
    def _():
        kept_copy = pltpu.make_async_copy(kept_hbm, kept_ref, sem)
        kept_copy.start()
        for e in range(energies):
            state = parts(get_state(incoming_ref.at[e]))
            halves = []
            for i in range(cells):
                halves.append(parts(product(get_parts(left_ref.at[e, i]), state)))
            for i in range(cells):
                grown = product(halves[i], get_parts(right_ref.at[e, i]))
                put_state(state_ref.at[e, i], plus((fresh_ref[e, i, 0], fresh_ref[e, i, 1]), grown))
                if i == 0 and e == 0:
                    kept_copy.wait()
                pick_into(send_ref, e, i, state_ref.at[e, i], kept_ref, keep, share_rows)
            if not last:
                leaving_ref[e] = state_ref[e, cells - 1]


def tail(keep, share_rows, hop, last, incoming, left, right, fresh, kept_blocks, leaving, send):
    energies, cells = fresh.shape[:2]
    hbm = pl.BlockSpec(memory_space=pltpu.HBM)
    vmem = pl.BlockSpec(memory_space=pltpu.VMEM)
    carried = (send,) if last else (leaving, send)
    result = pl.pallas_call(
        functools.partial(tail_kernel, keep, share_rows, hop, last),
        out_shape=tuple(jax.ShapeDtypeStruct(value.shape, F32) for value in carried),
        in_specs=[vmem] * 4 + [hbm] + [vmem] * len(carried),
        out_specs=(vmem,) * len(carried),
        input_output_aliases={5 + i: i for i in range(len(carried))},
        scratch_shapes=[
            pltpu.SMEM(kept_blocks.shape, jnp.int32),
            pltpu.VMEM((energies, cells) + incoming.shape[1:], F32),
            pltpu.SemaphoreType.DMA,
        ],
        compiler_params=pltpu.CompilerParams(vmem_limit_bytes=32 << 20),
        name="tail_cells",
    )(incoming, left, right, fresh, in_hbm(kept_blocks), *carried)
    return (leaving, result[0]) if last else result


def lag_kernel(here, in_ref, out_hbm, out_ref, sems):
    energies, double_rows, _ = in_ref.shape
    rows = double_rows // 2
    step = min(8, rows)
    scale = 1.0 / energies
    groups = sems.shape[0]
    width = LAGS // groups

    def at(e, first):
        place = (energies // here - 1 - e // here) * here + e % here
        return in_ref[place, first:first + step]

    copies = []
    for group in range(groups):
        for lag in range(group * width, (group + 1) * width):
            for first in range(0, rows, step):
                real_sum = jnp.zeros((step, LANES), F32)
                imag_sum = jnp.zeros((step, LANES), F32)
                for e in range(energies - lag):
                    late_re, late_im = at(e + lag, first), at(e + lag, rows + first)
                    early_re, early_im = at(e, first), at(e, rows + first)
                    real_sum += late_re * early_re + late_im * early_im
                    imag_sum += late_im * early_re - late_re * early_im
                out_ref[lag, pl.ds(2 * first, step, 2), :] = real_sum * scale
                out_ref[lag, pl.ds(2 * first + 1, step, 2), :] = imag_sum * scale
        part = pl.ds(group * width, width)
        copies.append(pltpu.make_async_copy(out_ref.at[part], out_hbm.at[part], sems.at[group]))
        copies[-1].start()
    for copy in copies:
        copy.wait()


def lag_sums(here, owned):
    energies, double_rows, lanes = owned.shape
    rows = double_rows // 2
    sums = pl.pallas_call(
        functools.partial(lag_kernel, here),
        out_shape=jax.ShapeDtypeStruct((LAGS, double_rows, lanes), F32),
        in_specs=[pl.BlockSpec(memory_space=pltpu.VMEM)],
        out_specs=pl.BlockSpec(memory_space=pltpu.HBM),
        scratch_shapes=[
            pltpu.VMEM((LAGS, double_rows, lanes), F32),
            pltpu.SemaphoreType.DMA((4,)),
        ],
        name="lag_sums",
    )(owned)
    sums = sums.reshape(LAGS, rows, 2, lanes)
    return jnp.swapaxes(sums, 1, 2).reshape(LAGS, 2, rows * lanes)


def per_device(retarded, lesser_sigma, coupling, coupling_pattern, kept_blocks, lead_lesser):
    cells = retarded.shape[1]
    keep = kept_blocks.shape[0]
    owners = lax.axis_size("energy")
    length = lax.axis_size("chain")
    share_rows = cells * keep * BLOCK * BLOCK // (owners * LANES)
    leaving, send, left, right, fresh = head(
        keep, share_rows, owners, retarded, lesser_sigma, coupling, coupling_pattern, kept_blocks, lead_lesser
    )
    for hop in range(length - 1):
        incoming = lax.ppermute(leaving, "chain", [(i, (i + 1) % length) for i in range(length)])
        last = hop == length - 2
        leaving, send = tail(keep, share_rows, hop, last, incoming, left, right, fresh, kept_blocks, leaving, send)
    backwards = [list(range(owners))[::-1]]
    owned = lax.all_to_all(send, "energy", split_axis=1, concat_axis=0, axis_index_groups=backwards, tiled=True)
    return lag_sums(retarded.shape[0], owned.reshape((-1,) + owned.shape[2:]))


def solution(mesh):
    return jax.shard_map(
        per_device,
        mesh=mesh,
        in_specs=(
            P("energy", "chain", None, None, None),
            P("energy", "chain", None, None, None),
            P("chain", None, None, None),
            P("chain", None, None),
            P(),
            P("energy", None, None, None),
        ),
        out_specs=P(None, None, ("chain", "energy")),
        check_vma=False,
    )
```

```python
import functools

import jax
import jax.numpy as jnp
from jax import lax
from jax.experimental import pallas as pl
from jax.experimental.pallas import tpu as pltpu
from jax.sharding import PartitionSpec as P

BLOCK = 64
LAGS = 16
LANES = 128
F32 = jnp.float32
BF16 = jnp.bfloat16


def two_parts(value):
    high = value.astype(BF16)
    return high, (value - high.astype(F32)).astype(BF16)


def dot(left, right):
    return lax.dot_general(left, right, (((1,), (0,)), ((), ())), preferred_element_type=F32)


def parts(pair):
    return tuple(part for value in (pair[0], pair[1], pair[0] + pair[1]) for part in two_parts(value))


def adjoint(pair):
    return pair[0].T, -pair[1].T


def product(left, right):
    real = []
    for n in range(0, 6, 2):
        wide = jnp.concatenate([left[n], left[n], left[n + 1]], axis=1)
        tall = jnp.concatenate([right[n], right[n + 1], right[n]], axis=0)
        real.append(dot(wide, tall))
    return real[0] - real[1], real[2] - real[0] - real[1]


def put_parts(ref, values):
    for n, value in enumerate(values):
        ref[n] = value


def get_parts(ref):
    return tuple(ref[n] for n in range(6))


def plus(one, other):
    return one[0] + other[0], one[1] + other[1]


def put_state(state_ref, pair):
    for part in range(2):
        for group in range(state_ref.shape[1]):
            state_ref[part, group] = pair[part][:, group * LANES:(group + 1) * LANES]


def get_state(state_ref):
    groups = range(state_ref.shape[1])
    return tuple(jnp.concatenate([state_ref[part, group] for group in groups], axis=1) for part in range(2))


def block_mask(pattern_ref, cell, size):
    nblk = size // BLOCK
    column = lax.broadcasted_iota(jnp.int32, (BLOCK, size), 1) // BLOCK
    rows = []
    for r in range(nblk):
        row = jnp.zeros((BLOCK, size), F32)
        for c in range(nblk):
            row = jnp.where(column == c, pattern_ref[cell, r, c].astype(F32), row)
        rows.append(row)
    return jnp.concatenate(rows, axis=0)


def sending_order(owners):
    codes = [n ^ (n >> 1) for n in range(owners)]
    if sorted(codes) != list(range(owners)):
        codes = list(range(owners))
    return [owners - 1 - code for code in codes]


def pick_into(send_ref, e, cell, matrix_ref, kept_ref, keep, share_rows):
    order = sending_order(send_ref.shape[1])
    nblk = matrix_ref.shape[-2] // BLOCK
    half = BLOCK // 2
    lane = lax.broadcasted_iota(jnp.int32, (half, LANES), 1)
    piece = min(half, share_rows)
    for k in range(keep):
        number = kept_ref[k]
        top = (number // nblk) * BLOCK
        across = (number % nblk) * BLOCK
        window = across // LANES
        in_upper = jnp.full((half, LANES), across % LANES, jnp.int32) > 0
        for part in range(2):
            even = matrix_ref[part, window, pl.ds(top, half, 2), :]
            odd = matrix_ref[part, window, pl.ds(top + 1, half, 2), :]
            left = jnp.where(in_upper, pltpu.roll(even, BLOCK, 1), even)
            right = jnp.where(in_upper, odd, pltpu.roll(odd, BLOCK, 1))
            flat = jnp.where(lane < BLOCK, left, right)
            first = (cell * keep + k) * half
            for s in range(0, half, piece):
                owner, inside = divmod(first + s, share_rows)
                send_ref[e, order.index(owner), pl.ds(part * share_rows + inside, piece), :] = flat[s:s + piece]


def head_kernel(keep, share_rows, g_hbm, s_hbm, b_hbm, pattern_hbm, kept_hbm, lead_hbm,
                leaving_ref, send_ref, left_ref, right_ref, fresh_ref,
                pattern_ref, kept_ref, g_ref, s_ref, b_ref, lead_ref, state_ref, sems):
    energies, cells, _, size, _ = g_ref.shape
    position = lax.axis_index("chain")

    def fetch(slot, source, target):
        return pltpu.make_async_copy(source, target, sems.at[slot])

    lead_copy = fetch(0, lead_hbm, lead_ref)
    b_copies = [fetch(1 + i, b_hbm.at[i], b_ref.at[i]) for i in range(cells)]
    g_copies = [fetch(1 + cells + i, g_hbm.at[:, i], g_ref.at[:, i]) for i in range(cells)]
    s_copies = [fetch(1 + 2 * cells + i, s_hbm.at[:, i], s_ref.at[:, i]) for i in range(cells)]
    pattern_copy = fetch(1 + 3 * cells, pattern_hbm, pattern_ref)
    kept_copy = fetch(2 + 3 * cells, kept_hbm, kept_ref)
    pattern_copy.start()
    kept_copy.start()

    @pl.when(position == 0)
    def _():
        lead_copy.start()

    for i in range(cells):
        b_copies[i].start()
        g_copies[i].start()
        s_copies[i].start()
    pattern_copy.wait()
    kept_copy.wait()

    def bridge_of(i):
        mask = block_mask(pattern_ref, i, size)
        return b_ref[i, 0] * mask, b_ref[i, 1] * mask

    def matrix(ref, e, i):
        return ref[e, i, 0], ref[e, i, 1]

    @pl.when(position == 0)
    def _():
        lead_copy.wait()
        states = [(lead_ref[e, 0], lead_ref[e, 1]) for e in range(energies)]
        for i in range(cells):
            b_copies[i].wait()
            bridge = bridge_of(i)
            bridge_left, bridge_right = parts(bridge), parts(adjoint(bridge))
            for e in range(energies):
                entered = product(parts(product(bridge_left, parts(states[e]))), bridge_right)
                if e == 0:
                    g_copies[i].wait()
                    s_copies[i].wait()
                green = matrix(g_ref, e, i)
                green_left, green_right = parts(green), parts(adjoint(green))
                inner = parts(plus(matrix(s_ref, e, i), entered))
                states[e] = product(parts(product(green_left, inner)), green_right)
                out_ref = leaving_ref.at[e] if i == cells - 1 else state_ref.at[e, i]
                put_state(out_ref, states[e])
                if i < cells - 1:
                    pick_into(send_ref, e, i, out_ref, kept_ref, keep, share_rows)

    @pl.when(position > 0)
    def _():
        states, joined = [None] * energies, [None] * energies
        for i in range(cells):
            b_copies[i].wait()
            g_copies[i].wait()
            s_copies[i].wait()
            bridge = bridge_of(i)
            for e in range(energies):
                green = matrix(g_ref, e, i)
                green_left, green_right = parts(green), parts(adjoint(green))
                inner = matrix(s_ref, e, i)
                if i == 0:
                    joined[e] = product(green_left, parts(bridge))
                else:
                    bridge_left, bridge_right = parts(bridge), parts(adjoint(bridge))
                    half = parts(product(bridge_left, parts(states[e])))
                    across = parts(product(bridge_left, parts(joined[e])))
                    inner = plus(inner, product(half, bridge_right))
                    joined[e] = product(green_left, across)
                states[e] = product(parts(product(green_left, parts(inner))), green_right)
                put_parts(left_ref.at[e, i], parts(joined[e]))
                put_parts(right_ref.at[e, i], parts(adjoint(joined[e])))
                fresh_ref[e, i, 0], fresh_ref[e, i, 1] = states[e]


def in_hbm(value):
    return pltpu.with_memory_space_constraint(value, pltpu.HBM)


def head(keep, share_rows, owners, retarded, lesser_sigma, coupling, pattern, kept_blocks, lead):
    energies, cells, _, size, _ = retarded.shape
    hbm = pl.BlockSpec(memory_space=pltpu.HBM)
    vmem = pl.BlockSpec(memory_space=pltpu.VMEM)
    state_shape = (2, size // LANES, size, LANES)
    return pl.pallas_call(
        functools.partial(head_kernel, keep, share_rows),
        out_shape=(
            jax.ShapeDtypeStruct((energies,) + state_shape, F32),
            jax.ShapeDtypeStruct((energies, owners, 2 * share_rows, LANES), F32),
            jax.ShapeDtypeStruct((energies, cells, 6, size, size), BF16),
            jax.ShapeDtypeStruct((energies, cells, 6, size, size), BF16),
            jax.ShapeDtypeStruct((energies, cells, 2, size, size), F32),
        ),
        in_specs=[hbm] * 6,
        out_specs=(vmem,) * 5,
        scratch_shapes=[
            pltpu.SMEM(pattern.shape, jnp.int32),
            pltpu.SMEM(kept_blocks.shape, jnp.int32),
            pltpu.VMEM(retarded.shape, F32),
            pltpu.VMEM(lesser_sigma.shape, F32),
            pltpu.VMEM(coupling.shape, F32),
            pltpu.VMEM(lead.shape, F32),
            pltpu.VMEM((energies, cells) + state_shape, F32),
            pltpu.SemaphoreType.DMA((3 + 3 * cells,)),
        ],
        compiler_params=pltpu.CompilerParams(vmem_limit_bytes=32 << 20),
        name="head_cells",
    )(*(in_hbm(x) for x in (retarded, lesser_sigma, coupling, pattern, kept_blocks, lead)))


def tail_kernel(keep, share_rows, hop, last, incoming_ref, left_ref, right_ref, fresh_ref, kept_hbm, *refs):
    if last:
        (left_by, _, send_ref), refs = refs[:3], refs[3:]
        leaving_ref = None
    else:
        (left_by, _, leaving_ref, send_ref), refs = refs[:4], refs[4:]
    kept_ref, state_ref, sem = refs
    energies, cells, _, size, _ = fresh_ref.shape
    position = lax.axis_index("chain")
    kept_copy = pltpu.make_async_copy(kept_hbm, kept_ref, sem)
    kept_copy.start()

    if hop == 0:
        @pl.when(position == 0)
        def _():
            kept_copy.wait()
            for e in range(energies):
                pick_into(send_ref, e, cells - 1, left_by.at[e], kept_ref, keep, share_rows)

    @pl.when(position == hop + 1)
    def _():
        for e in range(energies):
            state = parts(get_state(incoming_ref.at[e]))
            halves = []
            for i in range(cells):
                halves.append(parts(product(get_parts(left_ref.at[e, i]), state)))
            for i in range(cells):
                grown = product(halves[i], get_parts(right_ref.at[e, i]))
                put_state(state_ref.at[e, i], plus((fresh_ref[e, i, 0], fresh_ref[e, i, 1]), grown))
                if i == 0 and e == 0:
                    kept_copy.wait()
                pick_into(send_ref, e, i, state_ref.at[e, i], kept_ref, keep, share_rows)
            if not last:
                leaving_ref[e] = state_ref[e, cells - 1]

    waited = position == hop + 1
    if hop == 0:
        waited = jnp.logical_or(waited, position == 0)

    @pl.when(jnp.logical_not(waited))
    def _():
        kept_copy.wait()


def tail(keep, share_rows, hop, last, incoming, left, right, fresh, kept_blocks, leaving, send):
    energies, cells = fresh.shape[:2]
    hbm = pl.BlockSpec(memory_space=pltpu.HBM)
    vmem = pl.BlockSpec(memory_space=pltpu.VMEM)
    carried = (send,) if last else (leaving, send)
    result = pl.pallas_call(
        functools.partial(tail_kernel, keep, share_rows, hop, last),
        out_shape=tuple(jax.ShapeDtypeStruct(value.shape, F32) for value in carried),
        in_specs=[vmem] * 4 + [hbm] + [vmem] * 2,
        out_specs=(vmem,) * len(carried),
        input_output_aliases={6: 0} if last else {5: 0, 6: 1},
        scratch_shapes=[
            pltpu.SMEM(kept_blocks.shape, jnp.int32),
            pltpu.VMEM((energies, cells) + incoming.shape[1:], F32),
            pltpu.SemaphoreType.DMA,
        ],
        compiler_params=pltpu.CompilerParams(vmem_limit_bytes=32 << 20),
        name="tail_cells",
    )(incoming, left, right, fresh, in_hbm(kept_blocks), leaving, send)
    return (leaving, result[0]) if last else result


def lag_kernel(here, in_ref, out_hbm, out_ref, sems):
    energies, double_rows, _ = in_ref.shape
    rows = double_rows // 2
    step = min(8, rows)
    scale = 1.0 / energies
    groups = sems.shape[0]
    width = LAGS // groups

    order = sending_order(energies // here)

    def at(e, first):
        place = order.index(e // here) * here + e % here
        return in_ref[place, first:first + step]

    copies = []
    for group in range(groups):
        for lag in range(group * width, (group + 1) * width):
            for first in range(0, rows, step):
                real_sum = jnp.zeros((step, LANES), F32)
                imag_sum = jnp.zeros((step, LANES), F32)
                for e in range(energies - lag):
                    late_re, late_im = at(e + lag, first), at(e + lag, rows + first)
                    early_re, early_im = at(e, first), at(e, rows + first)
                    real_sum += late_re * early_re + late_im * early_im
                    imag_sum += late_im * early_re - late_re * early_im
                out_ref[lag, pl.ds(2 * first, step, 2), :] = real_sum * scale
                out_ref[lag, pl.ds(2 * first + 1, step, 2), :] = imag_sum * scale
        part = pl.ds(group * width, width)
        copies.append(pltpu.make_async_copy(out_ref.at[part], out_hbm.at[part], sems.at[group]))
        copies[-1].start()
    for copy in copies:
        copy.wait()


def lag_sums(here, owned):
    energies, double_rows, lanes = owned.shape
    rows = double_rows // 2
    sums = pl.pallas_call(
        functools.partial(lag_kernel, here),
        out_shape=jax.ShapeDtypeStruct((LAGS, double_rows, lanes), F32),
        in_specs=[pl.BlockSpec(memory_space=pltpu.VMEM)],
        out_specs=pl.BlockSpec(memory_space=pltpu.HBM),
        scratch_shapes=[
            pltpu.VMEM((LAGS, double_rows, lanes), F32),
            pltpu.SemaphoreType.DMA((4,)),
        ],
        name="lag_sums",
    )(owned)
    sums = sums.reshape(LAGS, rows, 2, lanes)
    return jnp.swapaxes(sums, 1, 2).reshape(LAGS, 2, rows * lanes)


def per_device(retarded, lesser_sigma, coupling, coupling_pattern, kept_blocks, lead_lesser):
    cells = retarded.shape[1]
    keep = kept_blocks.shape[0]
    owners = lax.axis_size("energy")
    length = lax.axis_size("chain")
    share_rows = cells * keep * BLOCK * BLOCK // (owners * LANES)
    leaving, send, left, right, fresh = head(
        keep, share_rows, owners, retarded, lesser_sigma, coupling, coupling_pattern, kept_blocks, lead_lesser
    )
    for hop in range(length - 1):
        incoming = lax.ppermute(leaving, "chain", [(i, (i + 1) % length) for i in range(length)])
        last = hop == length - 2
        leaving, send = tail(keep, share_rows, hop, last, incoming, left, right, fresh, kept_blocks, leaving, send)
    groups = [sending_order(owners)]
    owned = lax.all_to_all(send, "energy", split_axis=1, concat_axis=0, axis_index_groups=groups, tiled=True)
    return lag_sums(retarded.shape[0], owned.reshape((-1,) + owned.shape[2:]))


def solution(mesh):
    return jax.shard_map(
        per_device,
        mesh=mesh,
        in_specs=(
            P("energy", "chain", None, None, None),
            P("energy", "chain", None, None, None),
            P("chain", None, None, None),
            P("chain", None, None),
            P(),
            P("energy", None, None, None),
        ),
        out_specs=P(None, None, ("chain", "energy")),
        check_vma=False,
    )
```

```python
import functools

import jax
import jax.numpy as jnp
from jax import lax
from jax.experimental import pallas as pl
from jax.experimental.pallas import tpu as pltpu
from jax.sharding import PartitionSpec as P

BLOCK = 64
LAGS = 16
LANES = 128
F32 = jnp.float32
BF16 = jnp.bfloat16


def two_parts(value):
    high = value.astype(BF16)
    return high, (value - high.astype(F32)).astype(BF16)


def dot(left, right):
    return lax.dot_general(left, right, (((1,), (0,)), ((), ())), preferred_element_type=F32)


def parts(pair):
    return tuple(part for value in (pair[0], pair[1], pair[0] + pair[1]) for part in two_parts(value))


def adjoint(pair):
    return pair[0].T, -pair[1].T


def product(left, right):
    real = []
    for n in range(0, 6, 2):
        wide = jnp.concatenate([left[n], left[n], left[n + 1]], axis=1)
        tall = jnp.concatenate([right[n], right[n + 1], right[n]], axis=0)
        real.append(dot(wide, tall))
    return real[0] - real[1], real[2] - real[0] - real[1]


def put_parts(ref, values):
    for n, value in enumerate(values):
        ref[n] = value


def get_parts(ref):
    return tuple(ref[n] for n in range(6))


def plus(one, other):
    return one[0] + other[0], one[1] + other[1]


def put_state(state_ref, pair):
    for part in range(2):
        for group in range(state_ref.shape[1]):
            state_ref[part, group] = pair[part][:, group * LANES:(group + 1) * LANES]


def get_state(state_ref):
    groups = range(state_ref.shape[1])
    return tuple(jnp.concatenate([state_ref[part, group] for group in groups], axis=1) for part in range(2))


def block_mask(pattern_ref, cell, size):
    nblk = size // BLOCK
    column = lax.broadcasted_iota(jnp.int32, (BLOCK, size), 1) // BLOCK
    rows = []
    for r in range(nblk):
        row = jnp.zeros((BLOCK, size), F32)
        for c in range(nblk):
            row = jnp.where(column == c, pattern_ref[cell, r, c].astype(F32), row)
        rows.append(row)
    return jnp.concatenate(rows, axis=0)


def pick_into(send_ref, e, cell, matrix_ref, kept_ref, keep, share_rows):
    nblk = matrix_ref.shape[-2] // BLOCK
    half = BLOCK // 2
    lane = lax.broadcasted_iota(jnp.int32, (half, LANES), 1)
    piece = min(half, share_rows)
    for k in range(keep):
        number = kept_ref[k]
        top = (number // nblk) * BLOCK
        across = (number % nblk) * BLOCK
        window = across // LANES
        in_upper = jnp.full((half, LANES), across % LANES, jnp.int32) > 0
        for part in range(2):
            even = matrix_ref[part, window, pl.ds(top, half, 2), :]
            odd = matrix_ref[part, window, pl.ds(top + 1, half, 2), :]
            left = jnp.where(in_upper, pltpu.roll(even, BLOCK, 1), even)
            right = jnp.where(in_upper, odd, pltpu.roll(odd, BLOCK, 1))
            flat = jnp.where(lane < BLOCK, left, right)
            first = (cell * keep + k) * half
            for s in range(0, half, piece):
                owner, inside = divmod(first + s, share_rows)
                send_ref[e, send_ref.shape[1] - 1 - owner, pl.ds(part * share_rows + inside, piece), :] = flat[s:s + piece]


def head_kernel(keep, share_rows, g_hbm, s_hbm, b_hbm, pattern_hbm, kept_hbm, lead_hbm,
                leaving_ref, send_ref, left_ref, right_ref, fresh_ref,
                pattern_ref, kept_ref, g_ref, s_ref, b_ref, lead_ref, state_ref, sems):
    energies, cells, _, size, _ = g_ref.shape
    position = lax.axis_index("chain")

    def fetch(slot, source, target):
        return pltpu.make_async_copy(source, target, sems.at[slot])

    lead_copy = fetch(0, lead_hbm, lead_ref)
    b_copies = [fetch(1 + i, b_hbm.at[i], b_ref.at[i]) for i in range(cells)]
    g_copies = [fetch(1 + cells + i, g_hbm.at[:, i], g_ref.at[:, i]) for i in range(cells)]
    s_copies = [fetch(1 + 2 * cells + i, s_hbm.at[:, i], s_ref.at[:, i]) for i in range(cells)]
    pattern_copy = fetch(1 + 3 * cells, pattern_hbm, pattern_ref)
    kept_copy = fetch(2 + 3 * cells, kept_hbm, kept_ref)
    pattern_copy.start()
    kept_copy.start()

    later = [copy for i in range(1, cells) for copy in (b_copies[i], g_copies[i], s_copies[i])]

    @pl.when(position == 0)
    def _():
        lead_copy.start()
        b_copies[0].start()
        lead_copy.wait()
        b_copies[0].wait()
        g_copies[0].start()
        s_copies[0].start()
        for copy in later:
            copy.start()

    @pl.when(position > 0)
    def _():
        g_copies[0].start()
        b_copies[0].start()
        s_copies[0].start()
        g_copies[0].wait()
        b_copies[0].wait()
        for copy in later:
            copy.start()

    pattern_copy.wait()
    kept_copy.wait()

    def bridge_of(i):
        mask = block_mask(pattern_ref, i, size)
        return b_ref[i, 0] * mask, b_ref[i, 1] * mask

    def matrix(ref, e, i):
        return ref[e, i, 0], ref[e, i, 1]

    @pl.when(position == 0)
    def _():
        states = [(lead_ref[e, 0], lead_ref[e, 1]) for e in range(energies)]
        for i in range(cells):
            if i > 0:
                b_copies[i].wait()
            bridge = bridge_of(i)
            bridge_left, bridge_right = parts(bridge), parts(adjoint(bridge))
            for e in range(energies):
                entered = product(parts(product(bridge_left, parts(states[e]))), bridge_right)
                if e == 0:
                    g_copies[i].wait()
                    s_copies[i].wait()
                green = matrix(g_ref, e, i)
                green_left, green_right = parts(green), parts(adjoint(green))
                inner = parts(plus(matrix(s_ref, e, i), entered))
                states[e] = product(parts(product(green_left, inner)), green_right)
                out_ref = leaving_ref.at[e] if i == cells - 1 else state_ref.at[e, i]
                put_state(out_ref, states[e])
                pick_into(send_ref, e, i, out_ref, kept_ref, keep, share_rows)

    @pl.when(position > 0)
    def _():
        states, joined = [None] * energies, [None] * energies
        for i in range(cells):
            if i > 0:
                b_copies[i].wait()
                g_copies[i].wait()
            s_copies[i].wait()
            bridge = bridge_of(i)
            for e in range(energies):
                green = matrix(g_ref, e, i)
                green_left, green_right = parts(green), parts(adjoint(green))
                inner = matrix(s_ref, e, i)
                if i == 0:
                    joined[e] = product(green_left, parts(bridge))
                else:
                    bridge_left, bridge_right = parts(bridge), parts(adjoint(bridge))
                    half = parts(product(bridge_left, parts(states[e])))
                    across = parts(product(bridge_left, parts(joined[e])))
                    inner = plus(inner, product(half, bridge_right))
                    joined[e] = product(green_left, across)
                states[e] = product(parts(product(green_left, parts(inner))), green_right)
                put_parts(left_ref.at[e, i], parts(joined[e]))
                put_parts(right_ref.at[e, i], parts(adjoint(joined[e])))
                fresh_ref[e, i, 0], fresh_ref[e, i, 1] = states[e]


def in_hbm(value):
    return pltpu.with_memory_space_constraint(value, pltpu.HBM)


def head(keep, share_rows, owners, retarded, lesser_sigma, coupling, pattern, kept_blocks, lead):
    energies, cells, _, size, _ = retarded.shape
    hbm = pl.BlockSpec(memory_space=pltpu.HBM)
    vmem = pl.BlockSpec(memory_space=pltpu.VMEM)
    state_shape = (2, size // LANES, size, LANES)
    return pl.pallas_call(
        functools.partial(head_kernel, keep, share_rows),
        out_shape=(
            jax.ShapeDtypeStruct((energies,) + state_shape, F32),
            jax.ShapeDtypeStruct((energies, owners, 2 * share_rows, LANES), F32),
            jax.ShapeDtypeStruct((energies, cells, 6, size, size), BF16),
            jax.ShapeDtypeStruct((energies, cells, 6, size, size), BF16),
            jax.ShapeDtypeStruct((energies, cells, 2, size, size), F32),
        ),
        in_specs=[hbm] * 6,
        out_specs=(vmem,) * 5,
        scratch_shapes=[
            pltpu.SMEM(pattern.shape, jnp.int32),
            pltpu.SMEM(kept_blocks.shape, jnp.int32),
            pltpu.VMEM(retarded.shape, F32),
            pltpu.VMEM(lesser_sigma.shape, F32),
            pltpu.VMEM(coupling.shape, F32),
            pltpu.VMEM(lead.shape, F32),
            pltpu.VMEM((energies, cells) + state_shape, F32),
            pltpu.SemaphoreType.DMA((3 + 3 * cells,)),
        ],
        compiler_params=pltpu.CompilerParams(vmem_limit_bytes=32 << 20),
        name="head_cells",
    )(*(in_hbm(x) for x in (retarded, lesser_sigma, coupling, pattern, kept_blocks, lead)))


def tail_kernel(keep, share_rows, hop, last, incoming_ref, left_ref, right_ref, fresh_ref, kept_hbm, *refs):
    if last:
        (_, send_ref), refs = refs[:2], refs[2:]
        leaving_ref = None
    else:
        (_, _, leaving_ref, send_ref), refs = refs[:4], refs[4:]
    kept_ref, state_ref, sem = refs
    energies, cells, _, size, _ = fresh_ref.shape

    @pl.when(lax.axis_index("chain") == hop + 1)
    def _():
        kept_copy = pltpu.make_async_copy(kept_hbm, kept_ref, sem)
        kept_copy.start()
        for e in range(energies):
            state = parts(get_state(incoming_ref.at[e]))
            halves = []
            for i in range(cells):
                halves.append(parts(product(get_parts(left_ref.at[e, i]), state)))
            for i in range(cells):
                grown = product(halves[i], get_parts(right_ref.at[e, i]))
                put_state(state_ref.at[e, i], plus((fresh_ref[e, i, 0], fresh_ref[e, i, 1]), grown))
                if i == 0 and e == 0:
                    kept_copy.wait()
                pick_into(send_ref, e, i, state_ref.at[e, i], kept_ref, keep, share_rows)
            if not last:
                leaving_ref[e] = state_ref[e, cells - 1]


def tail(keep, share_rows, hop, last, incoming, left, right, fresh, kept_blocks, leaving, send):
    energies, cells = fresh.shape[:2]
    hbm = pl.BlockSpec(memory_space=pltpu.HBM)
    vmem = pl.BlockSpec(memory_space=pltpu.VMEM)
    carried = (send,) if last else (leaving, send)
    result = pl.pallas_call(
        functools.partial(tail_kernel, keep, share_rows, hop, last),
        out_shape=tuple(jax.ShapeDtypeStruct(value.shape, F32) for value in carried),
        in_specs=[vmem] * 4 + [hbm] + [vmem] * len(carried),
        out_specs=(vmem,) * len(carried),
        input_output_aliases={5 + i: i for i in range(len(carried))},
        scratch_shapes=[
            pltpu.SMEM(kept_blocks.shape, jnp.int32),
            pltpu.VMEM((energies, cells) + incoming.shape[1:], F32),
            pltpu.SemaphoreType.DMA,
        ],
        compiler_params=pltpu.CompilerParams(vmem_limit_bytes=32 << 20),
        name="tail_cells",
    )(incoming, left, right, fresh, in_hbm(kept_blocks), *carried)
    return (leaving, result[0]) if last else result


def lag_kernel(here, in_ref, out_hbm, out_ref, sems):
    energies, double_rows, _ = in_ref.shape
    rows = double_rows // 2
    step = min(8, rows)
    scale = 1.0 / energies
    groups = sems.shape[0]
    width = LAGS // groups

    def at(e, first):
        place = (energies // here - 1 - e // here) * here + e % here
        return in_ref[place, first:first + step]

    copies = []
    for group in range(groups):
        for lag in range(group * width, (group + 1) * width):
            for first in range(0, rows, step):
                real_sum = jnp.zeros((step, LANES), F32)
                imag_sum = jnp.zeros((step, LANES), F32)
                for e in range(energies - lag):
                    late_re, late_im = at(e + lag, first), at(e + lag, rows + first)
                    early_re, early_im = at(e, first), at(e, rows + first)
                    real_sum += late_re * early_re + late_im * early_im
                    imag_sum += late_im * early_re - late_re * early_im
                out_ref[lag, pl.ds(2 * first, step, 2), :] = real_sum * scale
                out_ref[lag, pl.ds(2 * first + 1, step, 2), :] = imag_sum * scale
        part = pl.ds(group * width, width)
        copies.append(pltpu.make_async_copy(out_ref.at[part], out_hbm.at[part], sems.at[group]))
        copies[-1].start()
    for copy in copies:
        copy.wait()


def lag_sums(here, owned):
    energies, double_rows, lanes = owned.shape
    rows = double_rows // 2
    sums = pl.pallas_call(
        functools.partial(lag_kernel, here),
        out_shape=jax.ShapeDtypeStruct((LAGS, double_rows, lanes), F32),
        in_specs=[pl.BlockSpec(memory_space=pltpu.VMEM)],
        out_specs=pl.BlockSpec(memory_space=pltpu.HBM),
        scratch_shapes=[
            pltpu.VMEM((LAGS, double_rows, lanes), F32),
            pltpu.SemaphoreType.DMA((4,)),
        ],
        name="lag_sums",
    )(owned)
    sums = sums.reshape(LAGS, rows, 2, lanes)
    return jnp.swapaxes(sums, 1, 2).reshape(LAGS, 2, rows * lanes)


def per_device(retarded, lesser_sigma, coupling, coupling_pattern, kept_blocks, lead_lesser):
    cells = retarded.shape[1]
    keep = kept_blocks.shape[0]
    owners = lax.axis_size("energy")
    length = lax.axis_size("chain")
    share_rows = cells * keep * BLOCK * BLOCK // (owners * LANES)
    leaving, send, left, right, fresh = head(
        keep, share_rows, owners, retarded, lesser_sigma, coupling, coupling_pattern, kept_blocks, lead_lesser
    )
    for hop in range(length - 1):
        incoming = lax.ppermute(leaving, "chain", [(i, (i + 1) % length) for i in range(length)])
        last = hop == length - 2
        leaving, send = tail(keep, share_rows, hop, last, incoming, left, right, fresh, kept_blocks, leaving, send)
    backwards = [list(range(owners))[::-1]]
    owned = lax.all_to_all(send, "energy", split_axis=1, concat_axis=0, axis_index_groups=backwards, tiled=True)
    return lag_sums(retarded.shape[0], owned.reshape((-1,) + owned.shape[2:]))


def solution(mesh):
    return jax.shard_map(
        per_device,
        mesh=mesh,
        in_specs=(
            P("energy", "chain", None, None, None),
            P("energy", "chain", None, None, None),
            P("chain", None, None, None),
            P("chain", None, None),
            P(),
            P("energy", None, None, None),
        ),
        out_specs=P(None, None, ("chain", "energy")),
        check_vma=False,
    )
```

```python
import functools

import jax
import jax.numpy as jnp
from jax import lax
from jax.experimental import pallas as pl
from jax.experimental.pallas import tpu as pltpu
from jax.sharding import PartitionSpec as P

BLOCK = 64
LAGS = 16
LANES = 128
F32 = jnp.float32
BF16 = jnp.bfloat16


def two_parts(value):
    high = value.astype(BF16)
    return high, (value - high.astype(F32)).astype(BF16)


def dot(left, right):
    return lax.dot_general(left, right, (((1,), (0,)), ((), ())), preferred_element_type=F32)


def parts(pair):
    return tuple(part for value in (pair[0], pair[1], pair[0] + pair[1]) for part in two_parts(value))


def adjoint(pair):
    return pair[0].T, -pair[1].T


def product(left, right):
    real = []
    for n in range(0, 6, 2):
        wide = jnp.concatenate([left[n], left[n], left[n + 1]], axis=1)
        tall = jnp.concatenate([right[n], right[n + 1], right[n]], axis=0)
        real.append(dot(wide, tall))
    return real[0] - real[1], real[2] - real[0] - real[1]


def put_parts(ref, values):
    for n, value in enumerate(values):
        ref[n] = value


def get_parts(ref):
    return tuple(ref[n] for n in range(6))


def plus(one, other):
    return one[0] + other[0], one[1] + other[1]


def put_state(state_ref, pair):
    for part in range(2):
        for group in range(state_ref.shape[1]):
            state_ref[part, group] = pair[part][:, group * LANES:(group + 1) * LANES]


def get_state(state_ref):
    groups = range(state_ref.shape[1])
    return tuple(jnp.concatenate([state_ref[part, group] for group in groups], axis=1) for part in range(2))


def block_mask(pattern_ref, cell, size):
    nblk = size // BLOCK
    column = lax.broadcasted_iota(jnp.int32, (BLOCK, size), 1) // BLOCK
    rows = []
    for r in range(nblk):
        row = jnp.zeros((BLOCK, size), F32)
        for c in range(nblk):
            row = jnp.where(column == c, pattern_ref[cell, r, c].astype(F32), row)
        rows.append(row)
    return jnp.concatenate(rows, axis=0)


def pick_into(send_ref, e, cell, matrix_ref, kept_ref, keep, share_rows):
    nblk = matrix_ref.shape[-2] // BLOCK
    half = BLOCK // 2
    lane = lax.broadcasted_iota(jnp.int32, (half, LANES), 1)
    piece = min(half, share_rows)
    for k in range(keep):
        number = kept_ref[k]
        top = (number // nblk) * BLOCK
        across = (number % nblk) * BLOCK
        window = across // LANES
        in_upper = jnp.full((half, LANES), across % LANES, jnp.int32) > 0
        for part in range(2):
            even = matrix_ref[part, window, pl.ds(top, half, 2), :]
            odd = matrix_ref[part, window, pl.ds(top + 1, half, 2), :]
            left = jnp.where(in_upper, pltpu.roll(even, BLOCK, 1), even)
            right = jnp.where(in_upper, odd, pltpu.roll(odd, BLOCK, 1))
            flat = jnp.where(lane < BLOCK, left, right)
            first = (cell * keep + k) * half
            for s in range(0, half, piece):
                owner, inside = divmod(first + s, share_rows)
                send_ref[e, send_ref.shape[1] - 1 - owner, pl.ds(part * share_rows + inside, piece), :] = flat[s:s + piece]


def head_kernel(g_hbm, s_hbm, b_hbm, pattern_hbm, lead_hbm,
                inner_ref, fresh_ref, factor_ref, green_ref, bridge_ref,
                pattern_ref, g_ref, s_ref, b_ref, lead_ref, sems):
    energies, cells, _, size, _ = s_ref.shape
    position = lax.axis_index("chain")
    final = cells - 1

    def fetch(slot, source, target):
        return pltpu.make_async_copy(source, target, sems.at[slot])

    def g_place(i):
        return green_ref if i == final else g_ref.at[:, i]

    lead_copy = fetch(0, lead_hbm, lead_ref)
    b_copies = [fetch(1 + i, b_hbm.at[i], b_ref.at[i]) for i in range(cells)]
    g_copies = [fetch(1 + cells + i, g_hbm.at[:, i], g_place(i)) for i in range(cells)]
    s_copies = [fetch(1 + 2 * cells + i, s_hbm.at[:, i], s_ref.at[:, i]) for i in range(cells)]
    pattern_copy = fetch(1 + 3 * cells, pattern_hbm, pattern_ref)
    pattern_copy.start()

    @pl.when(position == 0)
    def _():
        lead_copy.start()

    for i in range(cells):
        b_copies[i].start()
        g_copies[i].start()
        s_copies[i].start()
    pattern_copy.wait()

    def bridge_of(i):
        mask = block_mask(pattern_ref, i, size)
        return b_ref[i, 0] * mask, b_ref[i, 1] * mask

    def green_of(e, i):
        if i == final:
            return green_ref[e, 0], green_ref[e, 1]
        return g_ref[e, i, 0], g_ref[e, i, 1]

    @pl.when(position == 0)
    def _():
        lead_copy.wait()
        states = [(lead_ref[e, 0], lead_ref[e, 1]) for e in range(energies)]
        for i in range(cells):
            b_copies[i].wait()
            bridge = bridge_of(i)
            bridge_left, bridge_right = parts(bridge), parts(adjoint(bridge))
            for e in range(energies):
                entered = product(parts(product(bridge_left, parts(states[e]))), bridge_right)
                if e == 0:
                    g_copies[i].wait()
                    s_copies[i].wait()
                inner = plus((s_ref[e, i, 0], s_ref[e, i, 1]), entered)
                if i == final:
                    put_state(inner_ref.at[e], inner)
                else:
                    green = green_of(e, i)
                    states[e] = product(parts(product(parts(green), parts(inner))), parts(adjoint(green)))
                    put_state(fresh_ref.at[e, i], states[e])

    @pl.when(position > 0)
    def _():
        states = [None] * energies
        for i in range(cells):
            b_copies[i].wait()
            g_copies[i].wait()
            s_copies[i].wait()
            bridge = bridge_of(i)
            if i == final:
                bridge_ref[0], bridge_ref[1] = bridge
            for e in range(energies):
                green = green_of(e, i)
                green_left, green_right = parts(green), parts(adjoint(green))
                inner = s_ref[e, i, 0], s_ref[e, i, 1]
                if i < final:
                    put_parts(factor_ref.at[e, i], parts(product(green_left, parts(bridge))))
                if i > 0:
                    half = parts(product(parts(bridge), parts(states[e])))
                    inner = plus(inner, product(half, parts(adjoint(bridge))))
                states[e] = product(parts(product(green_left, parts(inner))), green_right)
                put_state(fresh_ref.at[e, i], states[e])


def in_hbm(value):
    return pltpu.with_memory_space_constraint(value, pltpu.HBM)


def head(retarded, lesser_sigma, coupling, pattern, lead):
    energies, cells, _, size, _ = retarded.shape
    hbm = pl.BlockSpec(memory_space=pltpu.HBM)
    vmem = pl.BlockSpec(memory_space=pltpu.VMEM)
    state_shape = (2, size // LANES, size, LANES)
    others = max(cells - 1, 1)
    return pl.pallas_call(
        head_kernel,
        out_shape=(
            jax.ShapeDtypeStruct((energies,) + state_shape, F32),
            jax.ShapeDtypeStruct((energies, cells) + state_shape, F32),
            jax.ShapeDtypeStruct((energies, others, 6, size, size), BF16),
            jax.ShapeDtypeStruct((energies, 2, size, size), F32),
            jax.ShapeDtypeStruct((2, size, size), F32),
        ),
        in_specs=[hbm] * 5,
        out_specs=(vmem,) * 5,
        scratch_shapes=[
            pltpu.SMEM(pattern.shape, jnp.int32),
            pltpu.VMEM((energies, others, 2, size, size), F32),
            pltpu.VMEM(lesser_sigma.shape, F32),
            pltpu.VMEM(coupling.shape, F32),
            pltpu.VMEM(lead.shape, F32),
            pltpu.SemaphoreType.DMA((2 + 3 * cells,)),
        ],
        compiler_params=pltpu.CompilerParams(vmem_limit_bytes=32 << 20),
        name="head_cells",
    )(*(in_hbm(x) for x in (retarded, lesser_sigma, coupling, pattern, lead)))


def middle_kernel(keep, share_rows, before_ref, inner_ref, fresh_ref, factor_ref, green_ref, bridge_ref, kept_hbm,
                  send_ref, left_ref, right_ref, kept_ref, state_ref, sem):
    energies, cells = fresh_ref.shape[:2]
    final = cells - 1
    position = lax.axis_index("chain")
    kept_copy = pltpu.make_async_copy(kept_hbm, kept_ref, sem)
    kept_copy.start()

    @pl.when(position == 0)
    def _():
        for e in range(energies):
            green = green_ref[e, 0], green_ref[e, 1]
            inner = parts(get_state(inner_ref.at[e]))
            put_state(state_ref.at[e], product(parts(product(parts(green), inner)), parts(adjoint(green))))
            if e == 0:
                kept_copy.wait()
            for i in range(cells):
                matrix_ref = state_ref.at[e] if i == final else fresh_ref.at[e, i]
                pick_into(send_ref, e, i, matrix_ref, kept_ref, keep, share_rows)

    def chain_of_factors(with_before):
        for e in range(energies):
            last_factor = product(parts((green_ref[e, 0], green_ref[e, 1])), parts((bridge_ref[0], bridge_ref[1])))
            joined = None
            if with_before:
                joined = before_ref[e, final, 0], before_ref[e, final, 1]
            for i in range(cells):
                if joined is not None:
                    factor = parts(last_factor) if i == final else get_parts(factor_ref.at[e, i])
                    joined = product(factor, parts(joined))
                    put_parts(left_ref.at[e, i], parts(joined))
                    put_parts(right_ref.at[e, i], parts(adjoint(joined)))
                    continue
                if i == final:
                    joined = last_factor
                else:
                    whole = get_parts(factor_ref.at[e, i])
                    joined = tuple(whole[n].astype(F32) + whole[n + 1].astype(F32) for n in (0, 2))
                put_parts(left_ref.at[e, i], parts(joined))
                put_parts(right_ref.at[e, i], parts(adjoint(joined)))

    @pl.when(position == 1)
    def _():
        chain_of_factors(True)
        kept_copy.wait()

    if lax.axis_size("chain") > 2:
        @pl.when(position > 1)
        def _():
            chain_of_factors(False)
            kept_copy.wait()


def middle(keep, share_rows, owners, before, inner, fresh, factor, green, bridge, kept_blocks):
    energies, cells = fresh.shape[:2]
    size = bridge.shape[-1]
    hbm = pl.BlockSpec(memory_space=pltpu.HBM)
    vmem = pl.BlockSpec(memory_space=pltpu.VMEM)
    return pl.pallas_call(
        functools.partial(middle_kernel, keep, share_rows),
        out_shape=(
            jax.ShapeDtypeStruct((energies, owners, 2 * share_rows, LANES), F32),
            jax.ShapeDtypeStruct((energies, cells, 6, size, size), BF16),
            jax.ShapeDtypeStruct((energies, cells, 6, size, size), BF16),
        ),
        in_specs=[vmem] * 6 + [hbm],
        out_specs=(vmem,) * 3,
        scratch_shapes=[
            pltpu.SMEM(kept_blocks.shape, jnp.int32),
            pltpu.VMEM(inner.shape, F32),
            pltpu.SemaphoreType.DMA,
        ],
        compiler_params=pltpu.CompilerParams(vmem_limit_bytes=32 << 20),
        cost_estimate=pl.CostEstimate(flops=12 * 2 * size**3, bytes_accessed=4 * size * size, transcendentals=0),
        name="middle_cells",
    )(before, inner, fresh, factor, green, bridge, in_hbm(kept_blocks))


def tail_kernel(keep, share_rows, hop, last, incoming_ref, left_ref, right_ref, fresh_ref, kept_hbm, *refs):
    if last:
        (_, send_ref), refs = refs[:2], refs[2:]
        leaving_ref = None
    else:
        (_, _, leaving_ref, send_ref), refs = refs[:4], refs[4:]
    kept_ref, state_ref, sem = refs
    energies, cells = fresh_ref.shape[:2]

    @pl.when(lax.axis_index("chain") == hop + 1)
    def _():
        kept_copy = pltpu.make_async_copy(kept_hbm, kept_ref, sem)
        kept_copy.start()
        for e in range(energies):
            state = parts(get_state(incoming_ref.at[e]))
            halves = []
            for i in range(cells):
                halves.append(parts(product(get_parts(left_ref.at[e, i]), state)))
            for i in range(cells):
                grown = product(halves[i], get_parts(right_ref.at[e, i]))
                put_state(state_ref.at[e, i], plus(get_state(fresh_ref.at[e, i]), grown))
                if i == 0 and e == 0:
                    kept_copy.wait()
                pick_into(send_ref, e, i, state_ref.at[e, i], kept_ref, keep, share_rows)
            if not last:
                leaving_ref[e] = state_ref[e, cells - 1]


def tail(keep, share_rows, hop, last, incoming, left, right, fresh, kept_blocks, leaving, send):
    energies, cells = fresh.shape[:2]
    hbm = pl.BlockSpec(memory_space=pltpu.HBM)
    vmem = pl.BlockSpec(memory_space=pltpu.VMEM)
    carried = (send,) if last else (leaving, send)
    result = pl.pallas_call(
        functools.partial(tail_kernel, keep, share_rows, hop, last),
        out_shape=tuple(jax.ShapeDtypeStruct(value.shape, F32) for value in carried),
        in_specs=[vmem] * 4 + [hbm] + [vmem] * len(carried),
        out_specs=(vmem,) * len(carried),
        input_output_aliases={5 + i: i for i in range(len(carried))},
        scratch_shapes=[
            pltpu.SMEM(kept_blocks.shape, jnp.int32),
            pltpu.VMEM((energies, cells) + incoming.shape[1:], F32),
            pltpu.SemaphoreType.DMA,
        ],
        compiler_params=pltpu.CompilerParams(vmem_limit_bytes=32 << 20),
        name="tail_cells",
    )(incoming, left, right, fresh, in_hbm(kept_blocks), *carried)
    return (leaving, result[0]) if last else result


def lag_kernel(here, in_ref, out_hbm, out_ref, sems):
    energies, double_rows, _ = in_ref.shape
    rows = double_rows // 2
    step = min(8, rows)
    scale = 1.0 / energies
    groups = sems.shape[0]
    width = LAGS // groups

    def at(e, first):
        place = (energies // here - 1 - e // here) * here + e % here
        return in_ref[place, first:first + step]

    copies = []
    for group in range(groups):
        for lag in range(group * width, (group + 1) * width):
            for first in range(0, rows, step):
                real_sum = jnp.zeros((step, LANES), F32)
                imag_sum = jnp.zeros((step, LANES), F32)
                for e in range(energies - lag):
                    late_re, late_im = at(e + lag, first), at(e + lag, rows + first)
                    early_re, early_im = at(e, first), at(e, rows + first)
                    real_sum += late_re * early_re + late_im * early_im
                    imag_sum += late_im * early_re - late_re * early_im
                out_ref[lag, pl.ds(2 * first, step, 2), :] = real_sum * scale
                out_ref[lag, pl.ds(2 * first + 1, step, 2), :] = imag_sum * scale
        part = pl.ds(group * width, width)
        copies.append(pltpu.make_async_copy(out_ref.at[part], out_hbm.at[part], sems.at[group]))
        copies[-1].start()
    for copy in copies:
        copy.wait()


def lag_sums(here, owned):
    energies, double_rows, lanes = owned.shape
    rows = double_rows // 2
    sums = pl.pallas_call(
        functools.partial(lag_kernel, here),
        out_shape=jax.ShapeDtypeStruct((LAGS, double_rows, lanes), F32),
        in_specs=[pl.BlockSpec(memory_space=pltpu.VMEM)],
        out_specs=pl.BlockSpec(memory_space=pltpu.HBM),
        scratch_shapes=[
            pltpu.VMEM((LAGS, double_rows, lanes), F32),
            pltpu.SemaphoreType.DMA((4,)),
        ],
        name="lag_sums",
    )(owned)
    sums = sums.reshape(LAGS, rows, 2, lanes)
    return jnp.swapaxes(sums, 1, 2).reshape(LAGS, 2, rows * lanes)


def per_device(retarded, lesser_sigma, coupling, coupling_pattern, kept_blocks, lead_lesser):
    cells = retarded.shape[1]
    keep = kept_blocks.shape[0]
    owners = lax.axis_size("energy")
    length = lax.axis_size("chain")
    share_rows = cells * keep * BLOCK * BLOCK // (owners * LANES)
    ring = [(i, (i + 1) % length) for i in range(length)]
    before = lax.ppermute(retarded, "chain", ring)
    leaving, fresh, factor, green, bridge = head(retarded, lesser_sigma, coupling, coupling_pattern, lead_lesser)
    incoming = lax.ppermute(leaving, "chain", ring)
    send, left, right = middle(keep, share_rows, owners, before, leaving, fresh, factor, green, bridge, kept_blocks)
    for hop in range(length - 1):
        if hop > 0:
            incoming = lax.ppermute(leaving, "chain", ring)
        last = hop == length - 2
        leaving, send = tail(keep, share_rows, hop, last, incoming, left, right, fresh, kept_blocks, leaving, send)
    backwards = [list(range(owners))[::-1]]
    owned = lax.all_to_all(send, "energy", split_axis=1, concat_axis=0, axis_index_groups=backwards, tiled=True)
    return lag_sums(retarded.shape[0], owned.reshape((-1,) + owned.shape[2:]))


def solution(mesh):
    return jax.shard_map(
        per_device,
        mesh=mesh,
        in_specs=(
            P("energy", "chain", None, None, None),
            P("energy", "chain", None, None, None),
            P("chain", None, None, None),
            P("chain", None, None),
            P(),
            P("energy", None, None, None),
        ),
        out_specs=P(None, None, ("chain", "energy")),
        check_vma=False,
    )
```

```python
import functools

import jax
import jax.numpy as jnp
from jax import lax
from jax.experimental import pallas as pl
from jax.experimental.pallas import tpu as pltpu
from jax.sharding import PartitionSpec as P

BLOCK = 64
LAGS = 16
LANES = 128
F32 = jnp.float32
BF16 = jnp.bfloat16


def two_parts(value):
    high = value.astype(BF16)
    return high, (value - high.astype(F32)).astype(BF16)


def dot(left, right):
    return lax.dot_general(left, right, (((1,), (0,)), ((), ())), preferred_element_type=F32)


def parts(pair):
    return tuple(part for value in (pair[0], pair[1], pair[0] + pair[1]) for part in two_parts(value))


def adjoint(pair):
    return pair[0].T, -pair[1].T


def product(left, right):
    real = []
    for n in range(0, 6, 2):
        wide = jnp.concatenate([left[n], left[n], left[n + 1]], axis=1)
        tall = jnp.concatenate([right[n], right[n + 1], right[n]], axis=0)
        real.append(dot(wide, tall))
    return real[0] - real[1], real[2] - real[0] - real[1]


def put_parts(ref, values):
    for n, value in enumerate(values):
        ref[n] = value


def get_parts(ref):
    return tuple(ref[n] for n in range(6))


def plus(one, other):
    return one[0] + other[0], one[1] + other[1]


def put_state(state_ref, pair):
    for part in range(2):
        for group in range(state_ref.shape[1]):
            state_ref[part, group] = pair[part][:, group * LANES:(group + 1) * LANES]


def get_state(state_ref):
    groups = range(state_ref.shape[1])
    return tuple(jnp.concatenate([state_ref[part, group] for group in groups], axis=1) for part in range(2))


def block_mask(pattern_ref, cell, size):
    nblk = size // BLOCK
    column = lax.broadcasted_iota(jnp.int32, (BLOCK, size), 1) // BLOCK
    rows = []
    for r in range(nblk):
        row = jnp.zeros((BLOCK, size), F32)
        for c in range(nblk):
            row = jnp.where(column == c, pattern_ref[cell, r, c].astype(F32), row)
        rows.append(row)
    return jnp.concatenate(rows, axis=0)


def with_next_row(value):
    return pltpu.roll(value, value.shape[0] - 1, 0)


def with_row_before(value):
    return pltpu.roll(value, 1, 0)


def on_even_rows(shape):
    return lax.broadcasted_iota(jnp.int32, shape, 0) % 2 == 0


def pick_into(send_ref, e, cell, matrix_ref, kept_ref, keep, share_rows):
    nblk = matrix_ref.shape[-2] // BLOCK
    owners = send_ref.shape[1]
    half = BLOCK // 2
    shape = (BLOCK, LANES)
    even_row = on_even_rows(shape)
    left_lane = lax.broadcasted_iota(jnp.int32, shape, 1) < BLOCK
    piece = min(half, share_rows)
    for k in range(keep):
        number = kept_ref[k]
        top = pl.multiple_of((number // nblk) * BLOCK, BLOCK)
        across = (number % nblk) * BLOCK
        window = across // LANES
        in_upper = jnp.full(shape, across % LANES, jnp.int32) > 0
        re = matrix_ref[0, window, pl.ds(top, BLOCK), :]
        im = matrix_ref[1, window, pl.ds(top, BLOCK), :]
        first = jnp.where(even_row, re, with_row_before(im))
        second = jnp.where(even_row, with_next_row(re), im)
        moved = pltpu.roll(jnp.where(in_upper, first, second), BLOCK, 1)
        left = jnp.where(in_upper, moved, first)
        right = jnp.where(in_upper, second, moved)
        flat = jnp.where(left_lane, left, right)
        begin = (cell * keep + k) * half
        for s in range(0, half, piece):
            owner, inside = divmod(begin + s, share_rows)
            send_ref[e, owners - 1 - owner, pl.ds(2 * inside, 2 * piece), :] = flat[2 * s:2 * (s + piece)]


def head_kernel(g_hbm, s_hbm, b_hbm, pattern_hbm, lead_hbm,
                inner_ref, fresh_ref, factor_ref, green_ref, bridge_ref,
                pattern_ref, g_ref, s_ref, b_ref, lead_ref, sems):
    energies, cells, _, size, _ = s_ref.shape
    position = lax.axis_index("chain")
    final = cells - 1

    def fetch(slot, source, target):
        return pltpu.make_async_copy(source, target, sems.at[slot])

    def g_place(i):
        return green_ref if i == final else g_ref.at[:, i]

    lead_copy = fetch(0, lead_hbm, lead_ref)
    b_copies = [fetch(1 + i, b_hbm.at[i], b_ref.at[i]) for i in range(cells)]
    g_copies = [fetch(1 + cells + i, g_hbm.at[:, i], g_place(i)) for i in range(cells)]
    s_copies = [fetch(1 + 2 * cells + i, s_hbm.at[:, i], s_ref.at[:, i]) for i in range(cells)]
    pattern_copy = fetch(1 + 3 * cells, pattern_hbm, pattern_ref)
    pattern_copy.start()

    @pl.when(position == 0)
    def _():
        lead_copy.start()

    for i in range(cells):
        b_copies[i].start()
        g_copies[i].start()
        s_copies[i].start()
    pattern_copy.wait()

    def bridge_of(i):
        mask = block_mask(pattern_ref, i, size)
        return b_ref[i, 0] * mask, b_ref[i, 1] * mask

    def green_of(e, i):
        if i == final:
            return green_ref[e, 0], green_ref[e, 1]
        return g_ref[e, i, 0], g_ref[e, i, 1]

    @pl.when(position == 0)
    def _():
        lead_copy.wait()
        states = [(lead_ref[e, 0], lead_ref[e, 1]) for e in range(energies)]
        for i in range(cells):
            b_copies[i].wait()
            bridge = bridge_of(i)
            bridge_left, bridge_right = parts(bridge), parts(adjoint(bridge))
            for e in range(energies):
                entered = product(parts(product(bridge_left, parts(states[e]))), bridge_right)
                if e == 0:
                    g_copies[i].wait()
                    s_copies[i].wait()
                inner = plus((s_ref[e, i, 0], s_ref[e, i, 1]), entered)
                if i == final:
                    put_state(inner_ref.at[e], inner)
                else:
                    green = green_of(e, i)
                    states[e] = product(parts(product(parts(green), parts(inner))), parts(adjoint(green)))
                    put_state(fresh_ref.at[e, i], states[e])

    @pl.when(position > 0)
    def _():
        states = [None] * energies
        for i in range(cells):
            b_copies[i].wait()
            g_copies[i].wait()
            s_copies[i].wait()
            bridge = bridge_of(i)
            if i == final:
                bridge_ref[0], bridge_ref[1] = bridge
            for e in range(energies):
                green = green_of(e, i)
                green_left, green_right = parts(green), parts(adjoint(green))
                inner = s_ref[e, i, 0], s_ref[e, i, 1]
                if i < final:
                    put_parts(factor_ref.at[e, i], parts(product(green_left, parts(bridge))))
                if i > 0:
                    half = parts(product(parts(bridge), parts(states[e])))
                    inner = plus(inner, product(half, parts(adjoint(bridge))))
                states[e] = product(parts(product(green_left, parts(inner))), green_right)
                put_state(fresh_ref.at[e, i], states[e])


def in_hbm(value):
    return pltpu.with_memory_space_constraint(value, pltpu.HBM)


def head(retarded, lesser_sigma, coupling, pattern, lead):
    energies, cells, _, size, _ = retarded.shape
    hbm = pl.BlockSpec(memory_space=pltpu.HBM)
    vmem = pl.BlockSpec(memory_space=pltpu.VMEM)
    state_shape = (2, size // LANES, size, LANES)
    others = max(cells - 1, 1)
    return pl.pallas_call(
        head_kernel,
        out_shape=(
            jax.ShapeDtypeStruct((energies,) + state_shape, F32),
            jax.ShapeDtypeStruct((energies, cells) + state_shape, F32),
            jax.ShapeDtypeStruct((energies, others, 6, size, size), BF16),
            jax.ShapeDtypeStruct((energies, 2, size, size), F32),
            jax.ShapeDtypeStruct((2, size, size), F32),
        ),
        in_specs=[hbm] * 5,
        out_specs=(vmem,) * 5,
        scratch_shapes=[
            pltpu.SMEM(pattern.shape, jnp.int32),
            pltpu.VMEM((energies, others, 2, size, size), F32),
            pltpu.VMEM(lesser_sigma.shape, F32),
            pltpu.VMEM(coupling.shape, F32),
            pltpu.VMEM(lead.shape, F32),
            pltpu.SemaphoreType.DMA((2 + 3 * cells,)),
        ],
        compiler_params=pltpu.CompilerParams(vmem_limit_bytes=32 << 20),
        name="head_cells",
    )(*(in_hbm(x) for x in (retarded, lesser_sigma, coupling, pattern, lead)))


def middle_kernel(keep, share_rows, before_ref, inner_ref, fresh_ref, factor_ref, green_ref, bridge_ref, kept_hbm,
                  send_ref, left_ref, right_ref, kept_ref, state_ref, sem):
    energies, cells = fresh_ref.shape[:2]
    final = cells - 1
    position = lax.axis_index("chain")
    kept_copy = pltpu.make_async_copy(kept_hbm, kept_ref, sem)
    kept_copy.start()

    @pl.when(position == 0)
    def _():
        for e in range(energies):
            green = green_ref[e, 0], green_ref[e, 1]
            inner = parts(get_state(inner_ref.at[e]))
            put_state(state_ref.at[e], product(parts(product(parts(green), inner)), parts(adjoint(green))))
            if e == 0:
                kept_copy.wait()
            for i in range(cells):
                matrix_ref = state_ref.at[e] if i == final else fresh_ref.at[e, i]
                pick_into(send_ref, e, i, matrix_ref, kept_ref, keep, share_rows)

    def chain_of_factors(with_before):
        for e in range(energies):
            last_factor = product(parts((green_ref[e, 0], green_ref[e, 1])), parts((bridge_ref[0], bridge_ref[1])))
            joined = None
            if with_before:
                joined = before_ref[e, final, 0], before_ref[e, final, 1]
            for i in range(cells):
                if joined is not None:
                    factor = parts(last_factor) if i == final else get_parts(factor_ref.at[e, i])
                    joined = product(factor, parts(joined))
                    put_parts(left_ref.at[e, i], parts(joined))
                    put_parts(right_ref.at[e, i], parts(adjoint(joined)))
                    continue
                if i == final:
                    joined = last_factor
                else:
                    whole = get_parts(factor_ref.at[e, i])
                    joined = tuple(whole[n].astype(F32) + whole[n + 1].astype(F32) for n in (0, 2))
                put_parts(left_ref.at[e, i], parts(joined))
                put_parts(right_ref.at[e, i], parts(adjoint(joined)))

    @pl.when(position == 1)
    def _():
        chain_of_factors(True)
        kept_copy.wait()

    if lax.axis_size("chain") > 2:
        @pl.when(position > 1)
        def _():
            chain_of_factors(False)
            kept_copy.wait()


def middle(keep, share_rows, owners, before, inner, fresh, factor, green, bridge, kept_blocks):
    energies, cells = fresh.shape[:2]
    size = bridge.shape[-1]
    hbm = pl.BlockSpec(memory_space=pltpu.HBM)
    vmem = pl.BlockSpec(memory_space=pltpu.VMEM)
    return pl.pallas_call(
        functools.partial(middle_kernel, keep, share_rows),
        out_shape=(
            jax.ShapeDtypeStruct((energies, owners, 2 * share_rows, LANES), F32),
            jax.ShapeDtypeStruct((energies, cells, 6, size, size), BF16),
            jax.ShapeDtypeStruct((energies, cells, 6, size, size), BF16),
        ),
        in_specs=[vmem] * 6 + [hbm],
        out_specs=(vmem,) * 3,
        scratch_shapes=[
            pltpu.SMEM(kept_blocks.shape, jnp.int32),
            pltpu.VMEM(inner.shape, F32),
            pltpu.SemaphoreType.DMA,
        ],
        compiler_params=pltpu.CompilerParams(vmem_limit_bytes=32 << 20),
        cost_estimate=pl.CostEstimate(flops=12 * 2 * size**3, bytes_accessed=4 * size * size, transcendentals=0),
        name="middle_cells",
    )(before, inner, fresh, factor, green, bridge, in_hbm(kept_blocks))


def tail_kernel(keep, share_rows, hop, last, incoming_ref, left_ref, right_ref, fresh_ref, kept_hbm, *refs):
    if last:
        (_, send_ref), refs = refs[:2], refs[2:]
        leaving_ref = None
    else:
        (_, _, leaving_ref, send_ref), refs = refs[:4], refs[4:]
    kept_ref, state_ref, sem = refs
    energies, cells = fresh_ref.shape[:2]

    @pl.when(lax.axis_index("chain") == hop + 1)
    def _():
        kept_copy = pltpu.make_async_copy(kept_hbm, kept_ref, sem)
        kept_copy.start()
        for e in range(energies):
            state = parts(get_state(incoming_ref.at[e]))
            halves = []
            for i in range(cells):
                halves.append(parts(product(get_parts(left_ref.at[e, i]), state)))
            for i in range(cells):
                grown = product(halves[i], get_parts(right_ref.at[e, i]))
                put_state(state_ref.at[e, i], plus(get_state(fresh_ref.at[e, i]), grown))
                if i == 0 and e == 0:
                    kept_copy.wait()
                pick_into(send_ref, e, i, state_ref.at[e, i], kept_ref, keep, share_rows)
            if not last:
                leaving_ref[e] = state_ref[e, cells - 1]


def tail(keep, share_rows, hop, last, incoming, left, right, fresh, kept_blocks, leaving, send):
    energies, cells = fresh.shape[:2]
    hbm = pl.BlockSpec(memory_space=pltpu.HBM)
    vmem = pl.BlockSpec(memory_space=pltpu.VMEM)
    carried = (send,) if last else (leaving, send)
    result = pl.pallas_call(
        functools.partial(tail_kernel, keep, share_rows, hop, last),
        out_shape=tuple(jax.ShapeDtypeStruct(value.shape, F32) for value in carried),
        in_specs=[vmem] * 4 + [hbm] + [vmem] * len(carried),
        out_specs=(vmem,) * len(carried),
        input_output_aliases={5 + i: i for i in range(len(carried))},
        scratch_shapes=[
            pltpu.SMEM(kept_blocks.shape, jnp.int32),
            pltpu.VMEM((energies, cells) + incoming.shape[1:], F32),
            pltpu.SemaphoreType.DMA,
        ],
        compiler_params=pltpu.CompilerParams(vmem_limit_bytes=32 << 20),
        name="tail_cells",
    )(incoming, left, right, fresh, in_hbm(kept_blocks), *carried)
    return (leaving, result[0]) if last else result


def lag_kernel(here, in_ref, out_hbm, swapped_ref, out_ref, sems):
    energies, double_rows, _ = in_ref.shape
    step = min(8, double_rows)
    blocks = range(0, double_rows, step)
    scale = 1.0 / energies
    groups = sems.shape[0]
    width = LAGS // groups
    even_row = on_even_rows((double_rows, LANES))
    even_in_step = on_even_rows((step, LANES))
    for e in range(energies):
        value = in_ref[e]
        swapped_ref[e] = jnp.where(even_row, with_next_row(value), with_row_before(value))

    def place(e):
        return (energies // here - 1 - e // here) * here + e % here

    copies = []
    for group in range(groups):
        lags = range(group * width, (group + 1) * width)
        for pair in range(0, len(blocks), 2):
            sums = {}
            for e in range(energies - lags[0]):
                for first in blocks[pair:pair + 2]:
                    early = in_ref[place(e), first:first + step]
                    early_swapped = swapped_ref[place(e), first:first + step]
                    for lag in lags:
                        if e + lag >= energies:
                            continue
                        late = in_ref[place(e + lag), first:first + step]
                        straight, crossed = late * early, late * early_swapped
                        if (lag, first) in sums:
                            straight, crossed = sums[lag, first][0] + straight, sums[lag, first][1] + crossed
                        sums[lag, first] = straight, crossed
            for (lag, first), (straight, crossed) in sums.items():
                both = jnp.where(even_in_step, straight + with_next_row(straight), crossed - with_row_before(crossed))
                out_ref[lag, first:first + step] = both * scale
        part = pl.ds(group * width, width)
        copies.append(pltpu.make_async_copy(out_ref.at[part], out_hbm.at[part], sems.at[group]))
        copies[-1].start()
    for copy in copies:
        copy.wait()


def lag_sums(here, owned):
    energies, double_rows, lanes = owned.shape
    rows = double_rows // 2
    sums = pl.pallas_call(
        functools.partial(lag_kernel, here),
        out_shape=jax.ShapeDtypeStruct((LAGS, double_rows, lanes), F32),
        in_specs=[pl.BlockSpec(memory_space=pltpu.VMEM)],
        out_specs=pl.BlockSpec(memory_space=pltpu.HBM),
        scratch_shapes=[
            pltpu.VMEM((energies, double_rows, lanes), F32),
            pltpu.VMEM((LAGS, double_rows, lanes), F32),
            pltpu.SemaphoreType.DMA((4,)),
        ],
        name="lag_sums",
    )(owned)
    sums = sums.reshape(LAGS, rows, 2, lanes)
    return jnp.swapaxes(sums, 1, 2).reshape(LAGS, 2, rows * lanes)


def per_device(retarded, lesser_sigma, coupling, coupling_pattern, kept_blocks, lead_lesser):
    cells = retarded.shape[1]
    keep = kept_blocks.shape[0]
    owners = lax.axis_size("energy")
    length = lax.axis_size("chain")
    share_rows = cells * keep * BLOCK * BLOCK // (owners * LANES)
    ring = [(i, (i + 1) % length) for i in range(length)]
    before = lax.ppermute(retarded, "chain", ring)
    leaving, fresh, factor, green, bridge = head(retarded, lesser_sigma, coupling, coupling_pattern, lead_lesser)
    incoming = lax.ppermute(leaving, "chain", ring)
    send, left, right = middle(keep, share_rows, owners, before, leaving, fresh, factor, green, bridge, kept_blocks)
    for hop in range(length - 1):
        if hop > 0:
            incoming = lax.ppermute(leaving, "chain", ring)
        last = hop == length - 2
        leaving, send = tail(keep, share_rows, hop, last, incoming, left, right, fresh, kept_blocks, leaving, send)
    backwards = [list(range(owners))[::-1]]
    owned = lax.all_to_all(send, "energy", split_axis=1, concat_axis=0, axis_index_groups=backwards, tiled=True)
    return lag_sums(retarded.shape[0], owned.reshape((-1,) + owned.shape[2:]))


def solution(mesh):
    return jax.shard_map(
        per_device,
        mesh=mesh,
        in_specs=(
            P("energy", "chain", None, None, None),
            P("energy", "chain", None, None, None),
            P("chain", None, None, None),
            P("chain", None, None),
            P(),
            P("energy", None, None, None),
        ),
        out_specs=P(None, None, ("chain", "energy")),
        check_vma=False,
    )
```

```python
import functools

import jax
import jax.numpy as jnp
from jax import lax
from jax.experimental import pallas as pl
from jax.experimental.pallas import tpu as pltpu
from jax.sharding import PartitionSpec as P

BLOCK = 64
LAGS = 16
LANES = 128
F32 = jnp.float32
BF16 = jnp.bfloat16


def two_parts(value):
    high = value.astype(BF16)
    return high, (value - high.astype(F32)).astype(BF16)


def dot(left, right):
    return lax.dot_general(left, right, (((1,), (0,)), ((), ())), preferred_element_type=F32)


def parts(pair):
    return tuple(part for value in (pair[0], pair[1], pair[0] + pair[1]) for part in two_parts(value))


def adjoint(pair):
    return pair[0].T, -pair[1].T


def product(left, right):
    real = []
    for n in range(0, 6, 2):
        wide = jnp.concatenate([left[n], left[n], left[n + 1]], axis=1)
        tall = jnp.concatenate([right[n], right[n + 1], right[n]], axis=0)
        real.append(dot(wide, tall))
    return real[0] - real[1], real[2] - real[0] - real[1]


def put_parts(ref, values):
    for n, value in enumerate(values):
        ref[n] = value


def get_parts(ref):
    return tuple(ref[n] for n in range(6))


def plus(one, other):
    return one[0] + other[0], one[1] + other[1]


def put_state(state_ref, pair):
    for part in range(2):
        for group in range(state_ref.shape[1]):
            state_ref[part, group] = pair[part][:, group * LANES:(group + 1) * LANES]


def get_state(state_ref):
    groups = range(state_ref.shape[1])
    return tuple(jnp.concatenate([state_ref[part, group] for group in groups], axis=1) for part in range(2))


def block_mask(pattern_ref, cell, size):
    nblk = size // BLOCK
    column = lax.broadcasted_iota(jnp.int32, (BLOCK, size), 1) // BLOCK
    rows = []
    for r in range(nblk):
        row = jnp.zeros((BLOCK, size), F32)
        for c in range(nblk):
            row = jnp.where(column == c, pattern_ref[cell, r, c].astype(F32), row)
        rows.append(row)
    return jnp.concatenate(rows, axis=0)


def sending_order(owners):
    inner = 1
    while inner * inner < owners:
        inner *= 2
    if owners % inner:
        inner = 1
    return [start + n for n in range(inner)[::-1] for start in range(0, owners, inner)[::-1]]


def pick_into(send_ref, e, cell, matrix_ref, kept_ref, keep, share_rows):
    order = sending_order(send_ref.shape[1])
    nblk = matrix_ref.shape[-2] // BLOCK
    half = BLOCK // 2
    lane = lax.broadcasted_iota(jnp.int32, (half, LANES), 1)
    piece = min(half, share_rows)
    for k in range(keep):
        number = kept_ref[k]
        top = (number // nblk) * BLOCK
        across = (number % nblk) * BLOCK
        window = across // LANES
        in_upper = jnp.full((half, LANES), across % LANES, jnp.int32) > 0
        for part in range(2):
            even = matrix_ref[part, window, pl.ds(top, half, 2), :]
            odd = matrix_ref[part, window, pl.ds(top + 1, half, 2), :]
            left = jnp.where(in_upper, pltpu.roll(even, BLOCK, 1), even)
            right = jnp.where(in_upper, odd, pltpu.roll(odd, BLOCK, 1))
            flat = jnp.where(lane < BLOCK, left, right)
            first = (cell * keep + k) * half
            for s in range(0, half, piece):
                owner, inside = divmod(first + s, share_rows)
                send_ref[e, order.index(owner), pl.ds(part * share_rows + inside, piece), :] = flat[s:s + piece]


def head_kernel(g_hbm, s_hbm, b_hbm, pattern_hbm, lead_hbm,
                inner_ref, fresh_ref, factor_ref, green_ref, bridge_ref,
                pattern_ref, g_ref, s_ref, b_ref, lead_ref, sems):
    energies, cells, _, size, _ = s_ref.shape
    position = lax.axis_index("chain")
    final = cells - 1

    def fetch(slot, source, target):
        return pltpu.make_async_copy(source, target, sems.at[slot])

    def g_place(i):
        return green_ref if i == final else g_ref.at[:, i]

    lead_copy = fetch(0, lead_hbm, lead_ref)
    b_copies = [fetch(1 + i, b_hbm.at[i], b_ref.at[i]) for i in range(cells)]
    g_copies = [fetch(1 + cells + i, g_hbm.at[:, i], g_place(i)) for i in range(cells)]
    s_copies = [fetch(1 + 2 * cells + i, s_hbm.at[:, i], s_ref.at[:, i]) for i in range(cells)]
    pattern_copy = fetch(1 + 3 * cells, pattern_hbm, pattern_ref)
    pattern_copy.start()

    @pl.when(position == 0)
    def _():
        lead_copy.start()

    for i in range(cells):
        b_copies[i].start()
        g_copies[i].start()
        s_copies[i].start()
    pattern_copy.wait()

    def bridge_of(i):
        mask = block_mask(pattern_ref, i, size)
        return b_ref[i, 0] * mask, b_ref[i, 1] * mask

    def green_of(e, i):
        if i == final:
            return green_ref[e, 0], green_ref[e, 1]
        return g_ref[e, i, 0], g_ref[e, i, 1]

    @pl.when(position == 0)
    def _():
        lead_copy.wait()
        states = [(lead_ref[e, 0], lead_ref[e, 1]) for e in range(energies)]
        for i in range(cells):
            b_copies[i].wait()
            bridge = bridge_of(i)
            bridge_left, bridge_right = parts(bridge), parts(adjoint(bridge))
            for e in range(energies):
                entered = product(parts(product(bridge_left, parts(states[e]))), bridge_right)
                if e == 0:
                    g_copies[i].wait()
                    s_copies[i].wait()
                inner = plus((s_ref[e, i, 0], s_ref[e, i, 1]), entered)
                if i == final:
                    put_state(inner_ref.at[e], inner)
                else:
                    green = green_of(e, i)
                    states[e] = product(parts(product(parts(green), parts(inner))), parts(adjoint(green)))
                    put_state(fresh_ref.at[e, i], states[e])

    @pl.when(position > 0)
    def _():
        states = [None] * energies
        for i in range(cells):
            b_copies[i].wait()
            g_copies[i].wait()
            s_copies[i].wait()
            bridge = bridge_of(i)
            if i == final:
                bridge_ref[0], bridge_ref[1] = bridge
            for e in range(energies):
                green = green_of(e, i)
                green_left, green_right = parts(green), parts(adjoint(green))
                inner = s_ref[e, i, 0], s_ref[e, i, 1]
                if i < final:
                    put_parts(factor_ref.at[e, i], parts(product(green_left, parts(bridge))))
                if i > 0:
                    half = parts(product(parts(bridge), parts(states[e])))
                    inner = plus(inner, product(half, parts(adjoint(bridge))))
                states[e] = product(parts(product(green_left, parts(inner))), green_right)
                put_state(fresh_ref.at[e, i], states[e])


def in_hbm(value):
    return pltpu.with_memory_space_constraint(value, pltpu.HBM)


def head(retarded, lesser_sigma, coupling, pattern, lead):
    energies, cells, _, size, _ = retarded.shape
    hbm = pl.BlockSpec(memory_space=pltpu.HBM)
    vmem = pl.BlockSpec(memory_space=pltpu.VMEM)
    state_shape = (2, size // LANES, size, LANES)
    others = max(cells - 1, 1)
    return pl.pallas_call(
        head_kernel,
        out_shape=(
            jax.ShapeDtypeStruct((energies,) + state_shape, F32),
            jax.ShapeDtypeStruct((energies, cells) + state_shape, F32),
            jax.ShapeDtypeStruct((energies, others, 6, size, size), BF16),
            jax.ShapeDtypeStruct((energies, 2, size, size), F32),
            jax.ShapeDtypeStruct((2, size, size), F32),
        ),
        in_specs=[hbm] * 5,
        out_specs=(vmem,) * 5,
        scratch_shapes=[
            pltpu.SMEM(pattern.shape, jnp.int32),
            pltpu.VMEM((energies, others, 2, size, size), F32),
            pltpu.VMEM(lesser_sigma.shape, F32),
            pltpu.VMEM(coupling.shape, F32),
            pltpu.VMEM(lead.shape, F32),
            pltpu.SemaphoreType.DMA((2 + 3 * cells,)),
        ],
        compiler_params=pltpu.CompilerParams(vmem_limit_bytes=32 << 20),
        name="head_cells",
    )(*(in_hbm(x) for x in (retarded, lesser_sigma, coupling, pattern, lead)))


def middle_kernel(keep, share_rows, before_ref, inner_ref, fresh_ref, factor_ref, green_ref, bridge_ref, kept_hbm,
                  send_ref, left_ref, right_ref, kept_ref, state_ref, sem):
    energies, cells = fresh_ref.shape[:2]
    final = cells - 1
    position = lax.axis_index("chain")
    kept_copy = pltpu.make_async_copy(kept_hbm, kept_ref, sem)
    kept_copy.start()

    @pl.when(position == 0)
    def _():
        for e in range(energies):
            green = green_ref[e, 0], green_ref[e, 1]
            inner = parts(get_state(inner_ref.at[e]))
            put_state(state_ref.at[e], product(parts(product(parts(green), inner)), parts(adjoint(green))))
            if e == 0:
                kept_copy.wait()
            for i in range(cells):
                matrix_ref = state_ref.at[e] if i == final else fresh_ref.at[e, i]
                pick_into(send_ref, e, i, matrix_ref, kept_ref, keep, share_rows)

    def chain_of_factors(with_before):
        for e in range(energies):
            last_factor = product(parts((green_ref[e, 0], green_ref[e, 1])), parts((bridge_ref[0], bridge_ref[1])))
            joined = None
            if with_before:
                joined = before_ref[e, final, 0], before_ref[e, final, 1]
            for i in range(cells):
                if joined is not None:
                    factor = parts(last_factor) if i == final else get_parts(factor_ref.at[e, i])
                    joined = product(factor, parts(joined))
                    put_parts(left_ref.at[e, i], parts(joined))
                    put_parts(right_ref.at[e, i], parts(adjoint(joined)))
                    continue
                if i == final:
                    joined = last_factor
                else:
                    whole = get_parts(factor_ref.at[e, i])
                    joined = tuple(whole[n].astype(F32) + whole[n + 1].astype(F32) for n in (0, 2))
                put_parts(left_ref.at[e, i], parts(joined))
                put_parts(right_ref.at[e, i], parts(adjoint(joined)))

    @pl.when(position == 1)
    def _():
        chain_of_factors(True)
        kept_copy.wait()

    if lax.axis_size("chain") > 2:
        @pl.when(position > 1)
        def _():
            chain_of_factors(False)
            kept_copy.wait()


def middle(keep, share_rows, owners, before, inner, fresh, factor, green, bridge, kept_blocks):
    energies, cells = fresh.shape[:2]
    size = bridge.shape[-1]
    hbm = pl.BlockSpec(memory_space=pltpu.HBM)
    vmem = pl.BlockSpec(memory_space=pltpu.VMEM)
    return pl.pallas_call(
        functools.partial(middle_kernel, keep, share_rows),
        out_shape=(
            jax.ShapeDtypeStruct((energies, owners, 2 * share_rows, LANES), F32),
            jax.ShapeDtypeStruct((energies, cells, 6, size, size), BF16),
            jax.ShapeDtypeStruct((energies, cells, 6, size, size), BF16),
        ),
        in_specs=[vmem] * 6 + [hbm],
        out_specs=(vmem,) * 3,
        scratch_shapes=[
            pltpu.SMEM(kept_blocks.shape, jnp.int32),
            pltpu.VMEM(inner.shape, F32),
            pltpu.SemaphoreType.DMA,
        ],
        compiler_params=pltpu.CompilerParams(vmem_limit_bytes=32 << 20),
        cost_estimate=pl.CostEstimate(flops=12 * 2 * size**3, bytes_accessed=4 * size * size, transcendentals=0),
        name="middle_cells",
    )(before, inner, fresh, factor, green, bridge, in_hbm(kept_blocks))


def tail_kernel(keep, share_rows, hop, last, incoming_ref, left_ref, right_ref, fresh_ref, kept_hbm, *refs):
    if last:
        (_, send_ref), refs = refs[:2], refs[2:]
        leaving_ref = None
    else:
        (_, _, leaving_ref, send_ref), refs = refs[:4], refs[4:]
    kept_ref, state_ref, sem = refs
    energies, cells = fresh_ref.shape[:2]

    @pl.when(lax.axis_index("chain") == hop + 1)
    def _():
        kept_copy = pltpu.make_async_copy(kept_hbm, kept_ref, sem)
        kept_copy.start()
        for e in range(energies):
            state = parts(get_state(incoming_ref.at[e]))
            halves = []
            for i in range(cells):
                halves.append(parts(product(get_parts(left_ref.at[e, i]), state)))
            for i in range(cells):
                grown = product(halves[i], get_parts(right_ref.at[e, i]))
                put_state(state_ref.at[e, i], plus(get_state(fresh_ref.at[e, i]), grown))
                if i == 0 and e == 0:
                    kept_copy.wait()
                pick_into(send_ref, e, i, state_ref.at[e, i], kept_ref, keep, share_rows)
            if not last:
                leaving_ref[e] = state_ref[e, cells - 1]


def tail(keep, share_rows, hop, last, incoming, left, right, fresh, kept_blocks, leaving, send):
    energies, cells = fresh.shape[:2]
    hbm = pl.BlockSpec(memory_space=pltpu.HBM)
    vmem = pl.BlockSpec(memory_space=pltpu.VMEM)
    carried = (send,) if last else (leaving, send)
    result = pl.pallas_call(
        functools.partial(tail_kernel, keep, share_rows, hop, last),
        out_shape=tuple(jax.ShapeDtypeStruct(value.shape, F32) for value in carried),
        in_specs=[vmem] * 4 + [hbm] + [vmem] * len(carried),
        out_specs=(vmem,) * len(carried),
        input_output_aliases={5 + i: i for i in range(len(carried))},
        scratch_shapes=[
            pltpu.SMEM(kept_blocks.shape, jnp.int32),
            pltpu.VMEM((energies, cells) + incoming.shape[1:], F32),
            pltpu.SemaphoreType.DMA,
        ],
        compiler_params=pltpu.CompilerParams(vmem_limit_bytes=32 << 20),
        name="tail_cells",
    )(incoming, left, right, fresh, in_hbm(kept_blocks), *carried)
    return (leaving, result[0]) if last else result


def lag_kernel(here, in_ref, out_hbm, out_ref, sems):
    energies, double_rows, _ = in_ref.shape
    rows = double_rows // 2
    step = min(8, rows)
    scale = 1.0 / energies
    groups = sems.shape[0]
    width = LAGS // groups

    order = sending_order(energies // here)

    def at(e, first):
        place = order.index(e // here) * here + e % here
        return in_ref[place, first:first + step]

    copies = []
    for group in range(groups):
        for lag in range(group * width, (group + 1) * width):
            for first in range(0, rows, step):
                real_sum = jnp.zeros((step, LANES), F32)
                imag_sum = jnp.zeros((step, LANES), F32)
                for e in range(energies - lag):
                    late_re, late_im = at(e + lag, first), at(e + lag, rows + first)
                    early_re, early_im = at(e, first), at(e, rows + first)
                    real_sum += late_re * early_re + late_im * early_im
                    imag_sum += late_im * early_re - late_re * early_im
                out_ref[lag, pl.ds(2 * first, step, 2), :] = real_sum * scale
                out_ref[lag, pl.ds(2 * first + 1, step, 2), :] = imag_sum * scale
        part = pl.ds(group * width, width)
        copies.append(pltpu.make_async_copy(out_ref.at[part], out_hbm.at[part], sems.at[group]))
        copies[-1].start()
    for copy in copies:
        copy.wait()


def lag_sums(here, owned):
    energies, double_rows, lanes = owned.shape
    rows = double_rows // 2
    sums = pl.pallas_call(
        functools.partial(lag_kernel, here),
        out_shape=jax.ShapeDtypeStruct((LAGS, double_rows, lanes), F32),
        in_specs=[pl.BlockSpec(memory_space=pltpu.VMEM)],
        out_specs=pl.BlockSpec(memory_space=pltpu.HBM),
        scratch_shapes=[
            pltpu.VMEM((LAGS, double_rows, lanes), F32),
            pltpu.SemaphoreType.DMA((4,)),
        ],
        name="lag_sums",
    )(owned)
    sums = sums.reshape(LAGS, rows, 2, lanes)
    return jnp.swapaxes(sums, 1, 2).reshape(LAGS, 2, rows * lanes)


def per_device(retarded, lesser_sigma, coupling, coupling_pattern, kept_blocks, lead_lesser):
    cells = retarded.shape[1]
    keep = kept_blocks.shape[0]
    owners = lax.axis_size("energy")
    length = lax.axis_size("chain")
    share_rows = cells * keep * BLOCK * BLOCK // (owners * LANES)
    ring = [(i, (i + 1) % length) for i in range(length)]
    before = lax.ppermute(retarded, "chain", ring)
    leaving, fresh, factor, green, bridge = head(retarded, lesser_sigma, coupling, coupling_pattern, lead_lesser)
    incoming = lax.ppermute(leaving, "chain", ring)
    send, left, right = middle(keep, share_rows, owners, before, leaving, fresh, factor, green, bridge, kept_blocks)
    for hop in range(length - 1):
        if hop > 0:
            incoming = lax.ppermute(leaving, "chain", ring)
        last = hop == length - 2
        leaving, send = tail(keep, share_rows, hop, last, incoming, left, right, fresh, kept_blocks, leaving, send)
    groups = [sending_order(owners)]
    owned = lax.all_to_all(send, "energy", split_axis=1, concat_axis=0, axis_index_groups=groups, tiled=True)
    return lag_sums(retarded.shape[0], owned.reshape((-1,) + owned.shape[2:]))


def solution(mesh):
    return jax.shard_map(
        per_device,
        mesh=mesh,
        in_specs=(
            P("energy", "chain", None, None, None),
            P("energy", "chain", None, None, None),
            P("chain", None, None, None),
            P("chain", None, None),
            P(),
            P("energy", None, None, None),
        ),
        out_specs=P(None, None, ("chain", "energy")),
        check_vma=False,
    )
```

```python
import functools

import jax
import jax.numpy as jnp
from jax import lax
from jax.experimental import pallas as pl
from jax.experimental.pallas import tpu as pltpu
from jax.sharding import PartitionSpec as P

BLOCK = 64
LAGS = 16
LANES = 128
F32 = jnp.float32
BF16 = jnp.bfloat16


def two_parts(value):
    high = value.astype(BF16)
    return high, (value - high.astype(F32)).astype(BF16)


def dot(left, right):
    return lax.dot_general(left, right, (((1,), (0,)), ((), ())), preferred_element_type=F32)


def parts(pair):
    return tuple(part for value in (pair[0], pair[1], pair[0] + pair[1]) for part in two_parts(value))


def adjoint(pair):
    return pair[0].T, -pair[1].T


def product(left, right):
    real = []
    for n in range(0, 6, 2):
        wide = jnp.concatenate([left[n], left[n], left[n + 1]], axis=1)
        tall = jnp.concatenate([right[n], right[n + 1], right[n]], axis=0)
        real.append(dot(wide, tall))
    return real[0] - real[1], real[2] - real[0] - real[1]


def sandwich(left, inner, right):
    rows = left[0].shape[0] // 2
    halves = [product(tuple(part[n * rows:(n + 1) * rows] for part in left), inner) for n in range(2)]
    done = [product(parts(half), right) for half in halves]
    return tuple(jnp.concatenate(both, axis=0) for both in zip(*done))


def put_parts(ref, values):
    for n, value in enumerate(values):
        ref[n] = value


def get_parts(ref):
    return tuple(ref[n] for n in range(6))


def plus(one, other):
    return one[0] + other[0], one[1] + other[1]


def put_state(state_ref, pair):
    for part in range(2):
        for group in range(state_ref.shape[1]):
            state_ref[part, group] = pair[part][:, group * LANES:(group + 1) * LANES]


def get_state(state_ref):
    groups = range(state_ref.shape[1])
    return tuple(jnp.concatenate([state_ref[part, group] for group in groups], axis=1) for part in range(2))


def block_mask(pattern_ref, cell, size):
    nblk = size // BLOCK
    column = lax.broadcasted_iota(jnp.int32, (BLOCK, size), 1) // BLOCK
    rows = []
    for r in range(nblk):
        row = jnp.zeros((BLOCK, size), F32)
        for c in range(nblk):
            row = jnp.where(column == c, pattern_ref[cell, r, c].astype(F32), row)
        rows.append(row)
    return jnp.concatenate(rows, axis=0)


def pick_into(send_ref, e, cell, matrix_ref, kept_ref, keep, share_rows):
    nblk = matrix_ref.shape[-2] // BLOCK
    half = BLOCK // 2
    lane = lax.broadcasted_iota(jnp.int32, (half, LANES), 1)
    piece = min(half, share_rows)
    for k in range(keep):
        number = kept_ref[k]
        top = (number // nblk) * BLOCK
        across = (number % nblk) * BLOCK
        window = across // LANES
        in_upper = jnp.full((half, LANES), across % LANES, jnp.int32) > 0
        for part in range(2):
            even = matrix_ref[part, window, pl.ds(top, half, 2), :]
            odd = matrix_ref[part, window, pl.ds(top + 1, half, 2), :]
            left = jnp.where(in_upper, pltpu.roll(even, BLOCK, 1), even)
            right = jnp.where(in_upper, odd, pltpu.roll(odd, BLOCK, 1))
            flat = jnp.where(lane < BLOCK, left, right)
            first = (cell * keep + k) * half
            for s in range(0, half, piece):
                owner, inside = divmod(first + s, share_rows)
                send_ref[e, send_ref.shape[1] - 1 - owner, pl.ds(part * share_rows + inside, piece), :] = flat[s:s + piece]


def head_kernel(g_hbm, s_hbm, b_hbm, pattern_hbm, lead_hbm,
                inner_ref, fresh_ref, factor_ref, green_ref, bridge_ref,
                pattern_ref, g_ref, s_ref, b_ref, lead_ref, sems):
    energies, cells, _, size, _ = s_ref.shape
    position = lax.axis_index("chain")
    final = cells - 1

    def fetch(slot, source, target):
        return pltpu.make_async_copy(source, target, sems.at[slot])

    def g_place(i):
        return green_ref if i == final else g_ref.at[:, i]

    lead_copy = fetch(0, lead_hbm, lead_ref)
    b_copies = [fetch(1 + i, b_hbm.at[i], b_ref.at[i]) for i in range(cells)]
    g_copies = [fetch(1 + cells + i, g_hbm.at[:, i], g_place(i)) for i in range(cells)]
    s_copies = [fetch(1 + 2 * cells + i, s_hbm.at[:, i], s_ref.at[:, i]) for i in range(cells)]
    pattern_copy = fetch(1 + 3 * cells, pattern_hbm, pattern_ref)
    pattern_copy.start()

    @pl.when(position == 0)
    def _():
        lead_copy.start()

    for i in range(cells):
        b_copies[i].start()
        g_copies[i].start()
        s_copies[i].start()
    pattern_copy.wait()

    def bridge_of(i):
        mask = block_mask(pattern_ref, i, size)
        return b_ref[i, 0] * mask, b_ref[i, 1] * mask

    def green_of(e, i):
        if i == final:
            return green_ref[e, 0], green_ref[e, 1]
        return g_ref[e, i, 0], g_ref[e, i, 1]

    @pl.when(position == 0)
    def _():
        lead_copy.wait()
        states = [(lead_ref[e, 0], lead_ref[e, 1]) for e in range(energies)]
        for i in range(cells):
            b_copies[i].wait()
            bridge = bridge_of(i)
            bridge_left, bridge_right = parts(bridge), parts(adjoint(bridge))
            for e in range(energies):
                entered = sandwich(bridge_left, parts(states[e]), bridge_right)
                if e == 0:
                    g_copies[i].wait()
                    s_copies[i].wait()
                inner = plus((s_ref[e, i, 0], s_ref[e, i, 1]), entered)
                if i == final:
                    put_state(inner_ref.at[e], inner)
                else:
                    green = green_of(e, i)
                    states[e] = sandwich(parts(green), parts(inner), parts(adjoint(green)))
                    put_state(fresh_ref.at[e, i], states[e])

    @pl.when(position > 0)
    def _():
        states = [None] * energies
        for i in range(cells):
            b_copies[i].wait()
            g_copies[i].wait()
            s_copies[i].wait()
            bridge = bridge_of(i)
            if i == final:
                bridge_ref[0], bridge_ref[1] = bridge
            for e in range(energies):
                green = green_of(e, i)
                green_left, green_right = parts(green), parts(adjoint(green))
                inner = s_ref[e, i, 0], s_ref[e, i, 1]
                if i < final:
                    put_parts(factor_ref.at[e, i], parts(product(green_left, parts(bridge))))
                if i > 0:
                    inner = plus(inner, sandwich(parts(bridge), parts(states[e]), parts(adjoint(bridge))))
                states[e] = sandwich(green_left, parts(inner), green_right)
                put_state(fresh_ref.at[e, i], states[e])


def in_hbm(value):
    return pltpu.with_memory_space_constraint(value, pltpu.HBM)


def head(retarded, lesser_sigma, coupling, pattern, lead):
    energies, cells, _, size, _ = retarded.shape
    hbm = pl.BlockSpec(memory_space=pltpu.HBM)
    vmem = pl.BlockSpec(memory_space=pltpu.VMEM)
    state_shape = (2, size // LANES, size, LANES)
    others = max(cells - 1, 1)
    return pl.pallas_call(
        head_kernel,
        out_shape=(
            jax.ShapeDtypeStruct((energies,) + state_shape, F32),
            jax.ShapeDtypeStruct((energies, cells) + state_shape, F32),
            jax.ShapeDtypeStruct((energies, others, 6, size, size), BF16),
            jax.ShapeDtypeStruct((energies, 2, size, size), F32),
            jax.ShapeDtypeStruct((2, size, size), F32),
        ),
        in_specs=[hbm] * 5,
        out_specs=(vmem,) * 5,
        scratch_shapes=[
            pltpu.SMEM(pattern.shape, jnp.int32),
            pltpu.VMEM((energies, others, 2, size, size), F32),
            pltpu.VMEM(lesser_sigma.shape, F32),
            pltpu.VMEM(coupling.shape, F32),
            pltpu.VMEM(lead.shape, F32),
            pltpu.SemaphoreType.DMA((2 + 3 * cells,)),
        ],
        compiler_params=pltpu.CompilerParams(vmem_limit_bytes=32 << 20),
        name="head_cells",
    )(*(in_hbm(x) for x in (retarded, lesser_sigma, coupling, pattern, lead)))


def middle_kernel(keep, share_rows, before_ref, inner_ref, fresh_ref, factor_ref, green_ref, bridge_ref, kept_hbm,
                  send_ref, left_ref, right_ref, kept_ref, state_ref, sem):
    energies, cells = fresh_ref.shape[:2]
    final = cells - 1
    position = lax.axis_index("chain")
    kept_copy = pltpu.make_async_copy(kept_hbm, kept_ref, sem)
    kept_copy.start()

    @pl.when(position == 0)
    def _():
        for e in range(energies):
            green = green_ref[e, 0], green_ref[e, 1]
            inner = parts(get_state(inner_ref.at[e]))
            put_state(state_ref.at[e], sandwich(parts(green), inner, parts(adjoint(green))))
            if e == 0:
                kept_copy.wait()
            for i in range(cells):
                matrix_ref = state_ref.at[e] if i == final else fresh_ref.at[e, i]
                pick_into(send_ref, e, i, matrix_ref, kept_ref, keep, share_rows)

    def chain_of_factors(with_before):
        for e in range(energies):
            last_factor = product(parts((green_ref[e, 0], green_ref[e, 1])), parts((bridge_ref[0], bridge_ref[1])))
            joined = None
            if with_before:
                joined = before_ref[e, final, 0], before_ref[e, final, 1]
            for i in range(cells):
                if joined is not None:
                    factor = parts(last_factor) if i == final else get_parts(factor_ref.at[e, i])
                    joined = product(factor, parts(joined))
                    put_parts(left_ref.at[e, i], parts(joined))
                    put_parts(right_ref.at[e, i], parts(adjoint(joined)))
                    continue
                if i == final:
                    joined = last_factor
                else:
                    whole = get_parts(factor_ref.at[e, i])
                    joined = tuple(whole[n].astype(F32) + whole[n + 1].astype(F32) for n in (0, 2))
                put_parts(left_ref.at[e, i], parts(joined))
                put_parts(right_ref.at[e, i], parts(adjoint(joined)))

    @pl.when(position == 1)
    def _():
        chain_of_factors(True)
        kept_copy.wait()

    if lax.axis_size("chain") > 2:
        @pl.when(position > 1)
        def _():
            chain_of_factors(False)
            kept_copy.wait()


def middle(keep, share_rows, owners, before, inner, fresh, factor, green, bridge, kept_blocks):
    energies, cells = fresh.shape[:2]
    size = bridge.shape[-1]
    hbm = pl.BlockSpec(memory_space=pltpu.HBM)
    vmem = pl.BlockSpec(memory_space=pltpu.VMEM)
    return pl.pallas_call(
        functools.partial(middle_kernel, keep, share_rows),
        out_shape=(
            jax.ShapeDtypeStruct((energies, owners, 2 * share_rows, LANES), F32),
            jax.ShapeDtypeStruct((energies, cells, 6, size, size), BF16),
            jax.ShapeDtypeStruct((energies, cells, 6, size, size), BF16),
        ),
        in_specs=[vmem] * 6 + [hbm],
        out_specs=(vmem,) * 3,
        scratch_shapes=[
            pltpu.SMEM(kept_blocks.shape, jnp.int32),
            pltpu.VMEM(inner.shape, F32),
            pltpu.SemaphoreType.DMA,
        ],
        compiler_params=pltpu.CompilerParams(vmem_limit_bytes=32 << 20),
        cost_estimate=pl.CostEstimate(flops=12 * 2 * size**3, bytes_accessed=4 * size * size, transcendentals=0),
        name="middle_cells",
    )(before, inner, fresh, factor, green, bridge, in_hbm(kept_blocks))


def tail_kernel(keep, share_rows, hop, last, incoming_ref, left_ref, right_ref, fresh_ref, kept_hbm, *refs):
    if last:
        (_, send_ref), refs = refs[:2], refs[2:]
        leaving_ref = None
    else:
        (_, _, leaving_ref, send_ref), refs = refs[:4], refs[4:]
    kept_ref, state_ref, sem = refs
    energies, cells = fresh_ref.shape[:2]

    @pl.when(lax.axis_index("chain") == hop + 1)
    def _():
        kept_copy = pltpu.make_async_copy(kept_hbm, kept_ref, sem)
        kept_copy.start()
        for e in range(energies):
            state = parts(get_state(incoming_ref.at[e]))
            halves = []
            for i in range(cells):
                halves.append(parts(product(get_parts(left_ref.at[e, i]), state)))
            for i in range(cells):
                grown = product(halves[i], get_parts(right_ref.at[e, i]))
                put_state(state_ref.at[e, i], plus(get_state(fresh_ref.at[e, i]), grown))
                if i == 0 and e == 0:
                    kept_copy.wait()
                pick_into(send_ref, e, i, state_ref.at[e, i], kept_ref, keep, share_rows)
            if not last:
                leaving_ref[e] = state_ref[e, cells - 1]


def tail(keep, share_rows, hop, last, incoming, left, right, fresh, kept_blocks, leaving, send):
    energies, cells = fresh.shape[:2]
    hbm = pl.BlockSpec(memory_space=pltpu.HBM)
    vmem = pl.BlockSpec(memory_space=pltpu.VMEM)
    carried = (send,) if last else (leaving, send)
    result = pl.pallas_call(
        functools.partial(tail_kernel, keep, share_rows, hop, last),
        out_shape=tuple(jax.ShapeDtypeStruct(value.shape, F32) for value in carried),
        in_specs=[vmem] * 4 + [hbm] + [vmem] * len(carried),
        out_specs=(vmem,) * len(carried),
        input_output_aliases={5 + i: i for i in range(len(carried))},
        scratch_shapes=[
            pltpu.SMEM(kept_blocks.shape, jnp.int32),
            pltpu.VMEM((energies, cells) + incoming.shape[1:], F32),
            pltpu.SemaphoreType.DMA,
        ],
        compiler_params=pltpu.CompilerParams(vmem_limit_bytes=32 << 20),
        name="tail_cells",
    )(incoming, left, right, fresh, in_hbm(kept_blocks), *carried)
    return (leaving, result[0]) if last else result


def lag_kernel(here, in_ref, out_hbm, out_ref, mixed_ref, sems):
    energies, double_rows, _ = in_ref.shape
    rows = double_rows // 2
    step = min(8, rows)
    scale = 1.0 / energies
    groups = sems.shape[0]
    width = LAGS // groups

    def at(e, first):
        place = (energies // here - 1 - e // here) * here + e % here
        return in_ref[place, first:first + step]

    for e in range(energies):
        for first in range(0, rows, step):
            re, im = at(e, first), at(e, rows + first)
            mixed_ref[0, e, first:first + step] = re + im
            mixed_ref[1, e, first:first + step] = re - im

    def at_all(e, first, kind):
        return mixed_ref[kind, e, first:first + step]

    copies = []
    for group in range(groups):
        for lag in range(group * width, (group + 1) * width):
            for first in range(0, rows, step):
                re_sum = jnp.zeros((step, LANES), F32)
                im_sum = jnp.zeros((step, LANES), F32)
                mixed_sum = jnp.zeros((step, LANES), F32)
                for e in range(energies - lag):
                    late_re, late_im = at(e + lag, first), at(e + lag, rows + first)
                    early_re, early_im = at(e, first), at(e, rows + first)
                    re_sum += late_re * early_re
                    im_sum += late_im * early_im
                    mixed_sum += at_all(e + lag, first, 0) * at_all(e, first, 1)
                real_sum, imag_sum = re_sum + im_sum, mixed_sum - re_sum + im_sum
                out_ref[lag, pl.ds(2 * first, step, 2), :] = real_sum * scale
                out_ref[lag, pl.ds(2 * first + 1, step, 2), :] = imag_sum * scale
        part = pl.ds(group * width, width)
        copies.append(pltpu.make_async_copy(out_ref.at[part], out_hbm.at[part], sems.at[group]))
        copies[-1].start()
    for copy in copies:
        copy.wait()


def lag_sums(here, owned):
    energies, double_rows, lanes = owned.shape
    rows = double_rows // 2
    sums = pl.pallas_call(
        functools.partial(lag_kernel, here),
        out_shape=jax.ShapeDtypeStruct((LAGS, double_rows, lanes), F32),
        in_specs=[pl.BlockSpec(memory_space=pltpu.VMEM)],
        out_specs=pl.BlockSpec(memory_space=pltpu.HBM),
        scratch_shapes=[
            pltpu.VMEM((LAGS, double_rows, lanes), F32),
            pltpu.VMEM((2, energies, rows, lanes), F32),
            pltpu.SemaphoreType.DMA((4,)),
        ],
        name="lag_sums",
    )(owned)
    sums = sums.reshape(LAGS, rows, 2, lanes)
    return jnp.swapaxes(sums, 1, 2).reshape(LAGS, 2, rows * lanes)


def per_device(retarded, lesser_sigma, coupling, coupling_pattern, kept_blocks, lead_lesser):
    cells = retarded.shape[1]
    keep = kept_blocks.shape[0]
    owners = lax.axis_size("energy")
    length = lax.axis_size("chain")
    share_rows = cells * keep * BLOCK * BLOCK // (owners * LANES)
    ring = [(i, (i + 1) % length) for i in range(length)]
    before = lax.ppermute(retarded, "chain", ring)
    leaving, fresh, factor, green, bridge = head(retarded, lesser_sigma, coupling, coupling_pattern, lead_lesser)
    incoming = lax.ppermute(leaving, "chain", ring)
    send, left, right = middle(keep, share_rows, owners, before, leaving, fresh, factor, green, bridge, kept_blocks)
    for hop in range(length - 1):
        if hop > 0:
            incoming = lax.ppermute(leaving, "chain", ring)
        last = hop == length - 2
        leaving, send = tail(keep, share_rows, hop, last, incoming, left, right, fresh, kept_blocks, leaving, send)
    backwards = [list(range(owners))[::-1]]
    owned = lax.all_to_all(send, "energy", split_axis=1, concat_axis=0, axis_index_groups=backwards, tiled=True)
    return lag_sums(retarded.shape[0], owned.reshape((-1,) + owned.shape[2:]))


def solution(mesh):
    return jax.shard_map(
        per_device,
        mesh=mesh,
        in_specs=(
            P("energy", "chain", None, None, None),
            P("energy", "chain", None, None, None),
            P("chain", None, None, None),
            P("chain", None, None),
            P(),
            P("energy", None, None, None),
        ),
        out_specs=P(None, None, ("chain", "energy")),
        check_vma=False,
    )
```

```python
import functools

import jax
import jax.numpy as jnp
from jax import lax
from jax.experimental import pallas as pl
from jax.experimental.pallas import tpu as pltpu
from jax.sharding import PartitionSpec as P

BLOCK = 64
LAGS = 16
LANES = 128
F32 = jnp.float32
BF16 = jnp.bfloat16


def two_parts(value):
    high = value.astype(BF16)
    return high, (value - high.astype(F32)).astype(BF16)


def dot(left, right):
    return lax.dot_general(left, right, (((1,), (0,)), ((), ())), preferred_element_type=F32)


def parts(pair):
    return tuple(part for value in (pair[0], pair[1], pair[0] + pair[1]) for part in two_parts(value))


def adjoint(pair):
    return pair[0].T, -pair[1].T


def product(left, right):
    real = []
    for n in range(0, 6, 2):
        wide = jnp.concatenate([left[n], left[n], left[n + 1]], axis=1)
        tall = jnp.concatenate([right[n], right[n + 1], right[n]], axis=0)
        real.append(dot(wide, tall))
    return real[0] - real[1], real[2] - real[0] - real[1]


def sandwich(left, inner, right):
    rows = left[0].shape[0] // 2
    halves = [product(tuple(part[n * rows:(n + 1) * rows] for part in left), inner) for n in range(2)]
    done = [product(parts(half), right) for half in halves]
    return tuple(jnp.concatenate(both, axis=0) for both in zip(*done))


def put_parts(ref, values):
    for n, value in enumerate(values):
        ref[n] = value


def get_parts(ref):
    return tuple(ref[n] for n in range(6))


def plus(one, other):
    return one[0] + other[0], one[1] + other[1]


def put_state(state_ref, pair):
    for part in range(2):
        for group in range(state_ref.shape[1]):
            state_ref[part, group] = pair[part][:, group * LANES:(group + 1) * LANES]


def get_state(state_ref):
    groups = range(state_ref.shape[1])
    return tuple(jnp.concatenate([state_ref[part, group] for group in groups], axis=1) for part in range(2))


def block_mask(pattern_ref, cell, size):
    nblk = size // BLOCK
    column = lax.broadcasted_iota(jnp.int32, (BLOCK, size), 1) // BLOCK
    rows = []
    for r in range(nblk):
        row = jnp.zeros((BLOCK, size), F32)
        for c in range(nblk):
            row = jnp.where(column == c, pattern_ref[cell, r, c].astype(F32), row)
        rows.append(row)
    return jnp.concatenate(rows, axis=0)


def pick_into(send_ref, e, cell, matrix_ref, kept_ref, keep, share_rows):
    nblk = matrix_ref.shape[-2] // BLOCK
    half = BLOCK // 2
    lane = lax.broadcasted_iota(jnp.int32, (half, LANES), 1)
    piece = min(half, share_rows)
    for k in range(keep):
        number = kept_ref[k]
        top = (number // nblk) * BLOCK
        across = (number % nblk) * BLOCK
        window = across // LANES
        in_upper = jnp.full((half, LANES), across % LANES, jnp.int32) > 0
        for part in range(2):
            even = matrix_ref[part, window, pl.ds(top, half, 2), :]
            odd = matrix_ref[part, window, pl.ds(top + 1, half, 2), :]
            left = jnp.where(in_upper, pltpu.roll(even, BLOCK, 1), even)
            right = jnp.where(in_upper, odd, pltpu.roll(odd, BLOCK, 1))
            flat = jnp.where(lane < BLOCK, left, right)
            first = (cell * keep + k) * half
            for s in range(0, half, piece):
                owner, inside = divmod(first + s, share_rows)
                send_ref[e, send_ref.shape[1] - 1 - owner, pl.ds(part * share_rows + inside, piece), :] = flat[s:s + piece]


def head_kernel(g_hbm, s_hbm, b_hbm, pattern_hbm, lead_hbm,
                inner_ref, fresh_ref, factor_ref, green_ref, bridge_ref,
                pattern_ref, s_ref, b_ref, lead_ref, sems):
    energies, cells, _, size, _ = s_ref.shape
    position = lax.axis_index("chain")
    final = cells - 1

    def fetch(slot, source, target):
        return pltpu.make_async_copy(source, target, sems.at[slot])

    lead_copy = fetch(0, lead_hbm, lead_ref)
    b_copies = [fetch(1 + i, b_hbm.at[i], b_ref.at[i]) for i in range(cells)]
    g_copies = [fetch(1 + cells + i, g_hbm.at[:, i], green_ref.at[:, i]) for i in range(cells)]
    s_copies = [fetch(1 + 2 * cells + i, s_hbm.at[:, i], s_ref.at[:, i]) for i in range(cells)]
    pattern_copy = fetch(1 + 3 * cells, pattern_hbm, pattern_ref)
    pattern_copy.start()

    @pl.when(position == 0)
    def _():
        lead_copy.start()

    for i in range(cells):
        b_copies[i].start()
        g_copies[i].start()
        s_copies[i].start()
    pattern_copy.wait()

    def bridge_of(i):
        mask = block_mask(pattern_ref, i, size)
        return b_ref[i, 0] * mask, b_ref[i, 1] * mask

    def green_of(e, i):
        return green_ref[e, i, 0], green_ref[e, i, 1]

    @pl.when(position == 0)
    def _():
        lead_copy.wait()
        states = [(lead_ref[e, 0], lead_ref[e, 1]) for e in range(energies)]
        for i in range(cells):
            b_copies[i].wait()
            bridge = parts(bridge_of(i))
            if i == 0 or i < final:
                bridge_right = parts(adjoint(bridge_of(i)))
            for e in range(energies):
                if i == 0 or i < final:
                    entered = sandwich(bridge, parts(states[e]), bridge_right)
                else:
                    across = product(bridge, parts(green_of(e, i - 1)))
                    entered = sandwich(parts(across), parts(states[e]), parts(adjoint(across)))
                if e == 0:
                    g_copies[i].wait()
                    s_copies[i].wait()
                inner = plus((s_ref[e, i, 0], s_ref[e, i, 1]), entered)
                if i == final:
                    put_state(inner_ref.at[e], inner)
                    continue
                states[e] = inner
                if i < final - 1:
                    green = green_of(e, i)
                    states[e] = sandwich(parts(green), parts(inner), parts(adjoint(green)))
                put_state(fresh_ref.at[e, i], states[e])

    @pl.when(position > 0)
    def _():
        for i in range(cells):
            b_copies[i].wait()
            g_copies[i].wait()
            s_copies[i].wait()
            bridge = bridge_of(i)
            if i == final:
                bridge_ref[0], bridge_ref[1] = bridge
            for e in range(energies):
                green = green_of(e, i)
                green_left = parts(green)
                if i < final:
                    factor_ref[e, i, 0], factor_ref[e, i, 1] = product(green_left, parts(bridge))
                inner = parts((s_ref[e, i, 0], s_ref[e, i, 1]))
                put_state(fresh_ref.at[e, i], sandwich(green_left, inner, parts(adjoint(green))))


def in_hbm(value):
    return pltpu.with_memory_space_constraint(value, pltpu.HBM)


def head(retarded, lesser_sigma, coupling, pattern, lead):
    energies, cells, _, size, _ = retarded.shape
    hbm = pl.BlockSpec(memory_space=pltpu.HBM)
    vmem = pl.BlockSpec(memory_space=pltpu.VMEM)
    state_shape = (2, size // LANES, size, LANES)
    others = max(cells - 1, 1)
    return pl.pallas_call(
        head_kernel,
        out_shape=(
            jax.ShapeDtypeStruct((energies,) + state_shape, F32),
            jax.ShapeDtypeStruct((energies, cells) + state_shape, F32),
            jax.ShapeDtypeStruct((energies, others, 2, size, size), F32),
            jax.ShapeDtypeStruct(retarded.shape, F32),
            jax.ShapeDtypeStruct((2, size, size), F32),
        ),
        in_specs=[hbm] * 5,
        out_specs=(vmem,) * 5,
        scratch_shapes=[
            pltpu.SMEM(pattern.shape, jnp.int32),
            pltpu.VMEM(lesser_sigma.shape, F32),
            pltpu.VMEM(coupling.shape, F32),
            pltpu.VMEM(lead.shape, F32),
            pltpu.SemaphoreType.DMA((2 + 3 * cells,)),
        ],
        compiler_params=pltpu.CompilerParams(vmem_limit_bytes=32 << 20),
        name="head_cells",
    )(*(in_hbm(x) for x in (retarded, lesser_sigma, coupling, pattern, lead)))


def middle_kernel(keep, share_rows, before_ref, inner_ref, fresh_ref, factor_ref, green_ref, bridge_ref, kept_hbm,
                  send_ref, left_ref, right_ref, kept_ref, state_ref, sem):
    energies, cells = fresh_ref.shape[:2]
    final = cells - 1
    position = lax.axis_index("chain")
    kept_copy = pltpu.make_async_copy(kept_hbm, kept_ref, sem)
    kept_copy.start()

    @pl.when(position == 0)
    def _():
        for e in range(energies):
            for i in range(cells):
                matrix_ref = fresh_ref.at[e, i]
                if i >= final - 1:
                    green = green_ref[e, i, 0], green_ref[e, i, 1]
                    inner = get_state(inner_ref.at[e] if i == final else matrix_ref)
                    matrix_ref = state_ref.at[e, i - max(final - 1, 0)]
                    put_state(matrix_ref, sandwich(parts(green), parts(inner), parts(adjoint(green))))
                if i == 0 and e == 0:
                    kept_copy.wait()
                pick_into(send_ref, e, i, matrix_ref, kept_ref, keep, share_rows)

    def factors(with_before):
        for e in range(energies):
            for i in range(cells):
                if i < final:
                    factor = factor_ref[e, i, 0], factor_ref[e, i, 1]
                else:
                    green = parts((green_ref[e, i, 0], green_ref[e, i, 1]))
                    factor = product(green, parts((bridge_ref[0], bridge_ref[1])))
                if i == 0 and with_before:
                    factor = product(parts(factor), parts((before_ref[e, final, 0], before_ref[e, final, 1])))
                put_parts(left_ref.at[e, i], parts(factor))
                put_parts(right_ref.at[e, i], parts(adjoint(factor)))

    @pl.when(position == 1)
    def _():
        factors(True)
        kept_copy.wait()

    if lax.axis_size("chain") > 2:
        @pl.when(position > 1)
        def _():
            factors(False)
            kept_copy.wait()


def middle(keep, share_rows, owners, before, inner, fresh, factor, green, bridge, kept_blocks):
    energies, cells = fresh.shape[:2]
    size = bridge.shape[-1]
    hbm = pl.BlockSpec(memory_space=pltpu.HBM)
    vmem = pl.BlockSpec(memory_space=pltpu.VMEM)
    return pl.pallas_call(
        functools.partial(middle_kernel, keep, share_rows),
        out_shape=(
            jax.ShapeDtypeStruct((energies, owners, 2 * share_rows, LANES), F32),
            jax.ShapeDtypeStruct((energies, cells, 6, size, size), BF16),
            jax.ShapeDtypeStruct((energies, cells, 6, size, size), BF16),
        ),
        in_specs=[vmem] * 6 + [hbm],
        out_specs=(vmem,) * 3,
        scratch_shapes=[
            pltpu.SMEM(kept_blocks.shape, jnp.int32),
            pltpu.VMEM((energies, 2) + inner.shape[1:], F32),
            pltpu.SemaphoreType.DMA,
        ],
        compiler_params=pltpu.CompilerParams(vmem_limit_bytes=32 << 20),
        cost_estimate=pl.CostEstimate(flops=12 * 2 * size**3, bytes_accessed=4 * size * size, transcendentals=0),
        name="middle_cells",
    )(before, inner, fresh, factor, green, bridge, in_hbm(kept_blocks))


def tail_kernel(keep, share_rows, hop, last, incoming_ref, left_ref, right_ref, fresh_ref, kept_hbm, *refs):
    if last:
        (_, send_ref), refs = refs[:2], refs[2:]
        leaving_ref = None
    else:
        (_, _, leaving_ref, send_ref), refs = refs[:4], refs[4:]
    kept_ref, state_ref, sem = refs
    energies, cells = fresh_ref.shape[:2]

    @pl.when(lax.axis_index("chain") == hop + 1)
    def _():
        kept_copy = pltpu.make_async_copy(kept_hbm, kept_ref, sem)
        kept_copy.start()
        for e in range(energies):
            state = get_state(incoming_ref.at[e])
            for i in range(cells):
                grown = sandwich(get_parts(left_ref.at[e, i]), parts(state), get_parts(right_ref.at[e, i]))
                state = plus(get_state(fresh_ref.at[e, i]), grown)
                put_state(state_ref.at[e, i], state)
                if i == 0 and e == 0:
                    kept_copy.wait()
                pick_into(send_ref, e, i, state_ref.at[e, i], kept_ref, keep, share_rows)
            if not last:
                leaving_ref[e] = state_ref[e, cells - 1]


def tail(keep, share_rows, hop, last, incoming, left, right, fresh, kept_blocks, leaving, send):
    energies, cells = fresh.shape[:2]
    hbm = pl.BlockSpec(memory_space=pltpu.HBM)
    vmem = pl.BlockSpec(memory_space=pltpu.VMEM)
    carried = (send,) if last else (leaving, send)
    result = pl.pallas_call(
        functools.partial(tail_kernel, keep, share_rows, hop, last),
        out_shape=tuple(jax.ShapeDtypeStruct(value.shape, F32) for value in carried),
        in_specs=[vmem] * 4 + [hbm] + [vmem] * len(carried),
        out_specs=(vmem,) * len(carried),
        input_output_aliases={5 + i: i for i in range(len(carried))},
        scratch_shapes=[
            pltpu.SMEM(kept_blocks.shape, jnp.int32),
            pltpu.VMEM((energies, cells) + incoming.shape[1:], F32),
            pltpu.SemaphoreType.DMA,
        ],
        compiler_params=pltpu.CompilerParams(vmem_limit_bytes=32 << 20),
        name="tail_cells",
    )(incoming, left, right, fresh, in_hbm(kept_blocks), *carried)
    return (leaving, result[0]) if last else result


def lag_kernel(here, in_ref, out_hbm, out_ref, mixed_ref, sems):
    energies, double_rows, _ = in_ref.shape
    rows = double_rows // 2
    step = min(8, rows)
    scale = 1.0 / energies
    groups = sems.shape[0]
    width = LAGS // groups

    def at(e, first):
        place = (energies // here - 1 - e // here) * here + e % here
        return in_ref[place, first:first + step]

    for e in range(energies):
        for first in range(0, rows, step):
            re, im = at(e, first), at(e, rows + first)
            mixed_ref[0, e, first:first + step] = re + im
            mixed_ref[1, e, first:first + step] = re - im

    def at_all(e, first, kind):
        return mixed_ref[kind, e, first:first + step]

    copies = []
    for group in range(groups):
        for lag in range(group * width, (group + 1) * width):
            for first in range(0, rows, step):
                re_sum = jnp.zeros((step, LANES), F32)
                im_sum = jnp.zeros((step, LANES), F32)
                mixed_sum = jnp.zeros((step, LANES), F32)
                for e in range(energies - lag):
                    late_re, late_im = at(e + lag, first), at(e + lag, rows + first)
                    early_re, early_im = at(e, first), at(e, rows + first)
                    re_sum += late_re * early_re
                    im_sum += late_im * early_im
                    mixed_sum += at_all(e + lag, first, 0) * at_all(e, first, 1)
                real_sum, imag_sum = re_sum + im_sum, mixed_sum - re_sum + im_sum
                out_ref[lag, pl.ds(2 * first, step, 2), :] = real_sum * scale
                out_ref[lag, pl.ds(2 * first + 1, step, 2), :] = imag_sum * scale
        part = pl.ds(group * width, width)
        copies.append(pltpu.make_async_copy(out_ref.at[part], out_hbm.at[part], sems.at[group]))
        copies[-1].start()
    for copy in copies:
        copy.wait()


def lag_sums(here, owned):
    energies, double_rows, lanes = owned.shape
    rows = double_rows // 2
    sums = pl.pallas_call(
        functools.partial(lag_kernel, here),
        out_shape=jax.ShapeDtypeStruct((LAGS, double_rows, lanes), F32),
        in_specs=[pl.BlockSpec(memory_space=pltpu.VMEM)],
        out_specs=pl.BlockSpec(memory_space=pltpu.HBM),
        scratch_shapes=[
            pltpu.VMEM((LAGS, double_rows, lanes), F32),
            pltpu.VMEM((2, energies, rows, lanes), F32),
            pltpu.SemaphoreType.DMA((4,)),
        ],
        name="lag_sums",
    )(owned)
    sums = sums.reshape(LAGS, rows, 2, lanes)
    return jnp.swapaxes(sums, 1, 2).reshape(LAGS, 2, rows * lanes)


def per_device(retarded, lesser_sigma, coupling, coupling_pattern, kept_blocks, lead_lesser):
    cells = retarded.shape[1]
    keep = kept_blocks.shape[0]
    owners = lax.axis_size("energy")
    length = lax.axis_size("chain")
    share_rows = cells * keep * BLOCK * BLOCK // (owners * LANES)
    ring = [(i, (i + 1) % length) for i in range(length)]
    before = lax.ppermute(retarded, "chain", ring)
    leaving, fresh, factor, green, bridge = head(retarded, lesser_sigma, coupling, coupling_pattern, lead_lesser)
    incoming = lax.ppermute(leaving, "chain", ring)
    send, left, right = middle(keep, share_rows, owners, before, leaving, fresh, factor, green, bridge, kept_blocks)
    for hop in range(length - 1):
        if hop > 0:
            incoming = lax.ppermute(leaving, "chain", ring)
        last = hop == length - 2
        leaving, send = tail(keep, share_rows, hop, last, incoming, left, right, fresh, kept_blocks, leaving, send)
    backwards = [list(range(owners))[::-1]]
    owned = lax.all_to_all(send, "energy", split_axis=1, concat_axis=0, axis_index_groups=backwards, tiled=True)
    return lag_sums(retarded.shape[0], owned.reshape((-1,) + owned.shape[2:]))


def solution(mesh):
    return jax.shard_map(
        per_device,
        mesh=mesh,
        in_specs=(
            P("energy", "chain", None, None, None),
            P("energy", "chain", None, None, None),
            P("chain", None, None, None),
            P("chain", None, None),
            P(),
            P("energy", None, None, None),
        ),
        out_specs=P(None, None, ("chain", "energy")),
        check_vma=False,
    )
```

```python
import functools

import jax
import jax.numpy as jnp
from jax import lax
from jax.experimental import pallas as pl
from jax.experimental.pallas import tpu as pltpu
from jax.sharding import PartitionSpec as P

BLOCK = 64
LAGS = 16
LANES = 128
F32 = jnp.float32
BF16 = jnp.bfloat16


def two_parts(value):
    high = value.astype(BF16)
    return high, (value - high.astype(F32)).astype(BF16)


def dot(left, right):
    return lax.dot_general(left, right, (((1,), (0,)), ((), ())), preferred_element_type=F32)


def parts(pair):
    return tuple(part for value in (pair[0], pair[1], pair[0] + pair[1]) for part in two_parts(value))


def adjoint(pair):
    return pair[0].T, -pair[1].T


def product(left, right):
    real = []
    for n in range(0, 6, 2):
        wide = jnp.concatenate([left[n], left[n], left[n + 1]], axis=1)
        tall = jnp.concatenate([right[n], right[n + 1], right[n]], axis=0)
        real.append(dot(wide, tall))
    return real[0] - real[1], real[2] - real[0] - real[1]


def sandwich(left, inner, right):
    rows = left[0].shape[0] // 2
    halves = [product(tuple(part[n * rows:(n + 1) * rows] for part in left), inner) for n in range(2)]
    done = [product(parts(half), right) for half in halves]
    return tuple(jnp.concatenate(both, axis=0) for both in zip(*done))


def put_parts(ref, values):
    for n, value in enumerate(values):
        ref[n] = value


def get_parts(ref):
    return tuple(ref[n] for n in range(6))


def plus(one, other):
    return one[0] + other[0], one[1] + other[1]


def put_state(state_ref, pair):
    for part in range(2):
        for group in range(state_ref.shape[1]):
            state_ref[part, group] = pair[part][:, group * LANES:(group + 1) * LANES]


def get_state(state_ref):
    groups = range(state_ref.shape[1])
    return tuple(jnp.concatenate([state_ref[part, group] for group in groups], axis=1) for part in range(2))


def block_mask(pattern_ref, cell, size):
    nblk = size // BLOCK
    column = lax.broadcasted_iota(jnp.int32, (BLOCK, size), 1) // BLOCK
    rows = []
    for r in range(nblk):
        row = jnp.zeros((BLOCK, size), F32)
        for c in range(nblk):
            row = jnp.where(column == c, pattern_ref[cell, r, c].astype(F32), row)
        rows.append(row)
    return jnp.concatenate(rows, axis=0)


def pick_into(send_ref, e, cell, matrix_ref, kept_ref, keep, share_rows):
    nblk = matrix_ref.shape[-2] // BLOCK
    half = BLOCK // 2
    lane = lax.broadcasted_iota(jnp.int32, (half, LANES), 1)
    piece = min(half, share_rows)
    for k in range(keep):
        number = kept_ref[k]
        top = (number // nblk) * BLOCK
        across = (number % nblk) * BLOCK
        window = across // LANES
        in_upper = jnp.full((half, LANES), across % LANES, jnp.int32) > 0
        for part in range(2):
            even = matrix_ref[part, window, pl.ds(top, half, 2), :]
            odd = matrix_ref[part, window, pl.ds(top + 1, half, 2), :]
            left = jnp.where(in_upper, pltpu.roll(even, BLOCK, 1), even)
            right = jnp.where(in_upper, odd, pltpu.roll(odd, BLOCK, 1))
            flat = jnp.where(lane < BLOCK, left, right)
            first = (cell * keep + k) * half
            for s in range(0, half, piece):
                owner, inside = divmod(first + s, share_rows)
                send_ref[e, send_ref.shape[1] - 1 - owner, pl.ds(part * share_rows + inside, piece), :] = flat[s:s + piece]


def head_kernel(g_hbm, s_hbm, b_hbm, pattern_hbm, lead_hbm,
                inner_ref, fresh_ref, factor_ref, green_ref, bridge_ref,
                pattern_ref, s_ref, b_ref, lead_ref, sems):
    energies, cells, _, size, _ = s_ref.shape
    position = lax.axis_index("chain")
    final = cells - 1

    def fetch(slot, source, target):
        return pltpu.make_async_copy(source, target, sems.at[slot])

    lead_copy = fetch(0, lead_hbm, lead_ref)
    b_copies = [fetch(1 + i, b_hbm.at[i], b_ref.at[i]) for i in range(cells)]
    g_copies = [fetch(1 + cells + i, g_hbm.at[:, i], green_ref.at[:, i]) for i in range(cells)]
    s_copies = [fetch(1 + 2 * cells + i, s_hbm.at[:, i], s_ref.at[:, i]) for i in range(cells)]
    pattern_copy = fetch(1 + 3 * cells, pattern_hbm, pattern_ref)
    pattern_copy.start()

    @pl.when(position == 0)
    def _():
        lead_copy.start()

    for i in range(cells):
        b_copies[i].start()
        g_copies[i].start()
        s_copies[i].start()
    pattern_copy.wait()

    def bridge_of(i):
        mask = block_mask(pattern_ref, i, size)
        return b_ref[i, 0] * mask, b_ref[i, 1] * mask

    def green_of(e, i):
        return green_ref[e, i, 0], green_ref[e, i, 1]

    @pl.when(position == 0)
    def _():
        lead_copy.wait()
        states = [(lead_ref[e, 0], lead_ref[e, 1]) for e in range(energies)]
        for i in range(cells):
            b_copies[i].wait()
            bridge = bridge_of(i)
            bridge_left, bridge_right = parts(bridge), parts(adjoint(bridge))
            for e in range(energies):
                entered = sandwich(bridge_left, parts(states[e]), bridge_right)
                if e == 0:
                    g_copies[i].wait()
                    s_copies[i].wait()
                inner = plus((s_ref[e, i, 0], s_ref[e, i, 1]), entered)
                if i == final:
                    put_state(inner_ref.at[e], inner)
                else:
                    green = green_of(e, i)
                    states[e] = sandwich(parts(green), parts(inner), parts(adjoint(green)))
                    put_state(fresh_ref.at[e, i], states[e])

    @pl.when(position > 0)
    def _():
        for i in range(cells):
            b_copies[i].wait()
            g_copies[i].wait()
            s_copies[i].wait()
            bridge = bridge_of(i)
            if i == final:
                bridge_ref[0], bridge_ref[1] = bridge
            for e in range(energies):
                green = green_of(e, i)
                green_left = parts(green)
                if i < final:
                    factor_ref[e, i, 0], factor_ref[e, i, 1] = product(green_left, parts(bridge))
                inner = parts((s_ref[e, i, 0], s_ref[e, i, 1]))
                put_state(fresh_ref.at[e, i], sandwich(green_left, inner, parts(adjoint(green))))


def in_hbm(value):
    return pltpu.with_memory_space_constraint(value, pltpu.HBM)


def head(retarded, lesser_sigma, coupling, pattern, lead):
    energies, cells, _, size, _ = retarded.shape
    hbm = pl.BlockSpec(memory_space=pltpu.HBM)
    vmem = pl.BlockSpec(memory_space=pltpu.VMEM)
    state_shape = (2, size // LANES, size, LANES)
    others = max(cells - 1, 1)
    return pl.pallas_call(
        head_kernel,
        out_shape=(
            jax.ShapeDtypeStruct((energies,) + state_shape, F32),
            jax.ShapeDtypeStruct((energies, cells) + state_shape, F32),
            jax.ShapeDtypeStruct((energies, others, 2, size, size), F32),
            jax.ShapeDtypeStruct(retarded.shape, F32),
            jax.ShapeDtypeStruct((2, size, size), F32),
        ),
        in_specs=[hbm] * 5,
        out_specs=(vmem,) * 5,
        scratch_shapes=[
            pltpu.SMEM(pattern.shape, jnp.int32),
            pltpu.VMEM(lesser_sigma.shape, F32),
            pltpu.VMEM(coupling.shape, F32),
            pltpu.VMEM(lead.shape, F32),
            pltpu.SemaphoreType.DMA((2 + 3 * cells,)),
        ],
        compiler_params=pltpu.CompilerParams(vmem_limit_bytes=32 << 20),
        name="head_cells",
    )(*(in_hbm(x) for x in (retarded, lesser_sigma, coupling, pattern, lead)))


def middle_kernel(keep, share_rows, before_ref, inner_ref, fresh_ref, factor_ref, green_ref, bridge_ref, kept_hbm,
                  send_ref, left_ref, right_ref, kept_ref, state_ref, sem):
    energies, cells = fresh_ref.shape[:2]
    final = cells - 1
    position = lax.axis_index("chain")
    kept_copy = pltpu.make_async_copy(kept_hbm, kept_ref, sem)
    kept_copy.start()

    @pl.when(position == 0)
    def _():
        for e in range(energies):
            for i in range(cells)[::-1]:
                matrix_ref = fresh_ref.at[e, i]
                if i == final:
                    green = green_ref[e, i, 0], green_ref[e, i, 1]
                    inner = parts(get_state(inner_ref.at[e]))
                    matrix_ref = state_ref.at[e]
                    put_state(matrix_ref, sandwich(parts(green), inner, parts(adjoint(green))))
                if i == final and e == 0:
                    kept_copy.wait()
                pick_into(send_ref, e, i, matrix_ref, kept_ref, keep, share_rows)

    def factors(with_before):
        for e in range(energies):
            for i in range(cells):
                if i < final:
                    factor = factor_ref[e, i, 0], factor_ref[e, i, 1]
                else:
                    green = parts((green_ref[e, i, 0], green_ref[e, i, 1]))
                    factor = product(green, parts((bridge_ref[0], bridge_ref[1])))
                if i == 0 and with_before:
                    factor = product(parts(factor), parts((before_ref[e, final, 0], before_ref[e, final, 1])))
                put_parts(left_ref.at[e, i], parts(factor))
                put_parts(right_ref.at[e, i], parts(adjoint(factor)))

    @pl.when(position == 1)
    def _():
        factors(True)
        kept_copy.wait()

    if lax.axis_size("chain") > 2:
        @pl.when(position > 1)
        def _():
            factors(False)
            kept_copy.wait()


def middle(keep, share_rows, owners, before, inner, fresh, factor, green, bridge, kept_blocks):
    energies, cells = fresh.shape[:2]
    size = bridge.shape[-1]
    hbm = pl.BlockSpec(memory_space=pltpu.HBM)
    vmem = pl.BlockSpec(memory_space=pltpu.VMEM)
    return pl.pallas_call(
        functools.partial(middle_kernel, keep, share_rows),
        out_shape=(
            jax.ShapeDtypeStruct((energies, owners, 2 * share_rows, LANES), F32),
            jax.ShapeDtypeStruct((energies, cells, 6, size, size), BF16),
            jax.ShapeDtypeStruct((energies, cells, 6, size, size), BF16),
        ),
        in_specs=[vmem] * 6 + [hbm],
        out_specs=(vmem,) * 3,
        scratch_shapes=[
            pltpu.SMEM(kept_blocks.shape, jnp.int32),
            pltpu.VMEM(inner.shape, F32),
            pltpu.SemaphoreType.DMA,
        ],
        compiler_params=pltpu.CompilerParams(vmem_limit_bytes=32 << 20),
        cost_estimate=pl.CostEstimate(flops=12 * 2 * size**3, bytes_accessed=4 * size * size, transcendentals=0),
        name="middle_cells",
    )(before, inner, fresh, factor, green, bridge, in_hbm(kept_blocks))


def tail_kernel(keep, share_rows, hop, last, incoming_ref, left_ref, right_ref, fresh_ref, kept_hbm, *refs):
    if last:
        (_, send_ref), refs = refs[:2], refs[2:]
        leaving_ref = None
    else:
        (_, _, leaving_ref, send_ref), refs = refs[:4], refs[4:]
    kept_ref, state_ref, sem = refs
    energies, cells = fresh_ref.shape[:2]

    @pl.when(lax.axis_index("chain") == hop + 1)
    def _():
        kept_copy = pltpu.make_async_copy(kept_hbm, kept_ref, sem)
        kept_copy.start()
        for e in range(energies):
            state = get_state(incoming_ref.at[e])
            for i in range(cells):
                grown = sandwich(get_parts(left_ref.at[e, i]), parts(state), get_parts(right_ref.at[e, i]))
                state = plus(get_state(fresh_ref.at[e, i]), grown)
                put_state(state_ref.at[e, i], state)
                if i == 0 and e == 0:
                    kept_copy.wait()
                pick_into(send_ref, e, i, state_ref.at[e, i], kept_ref, keep, share_rows)
            if not last:
                leaving_ref[e] = state_ref[e, cells - 1]


def tail(keep, share_rows, hop, last, incoming, left, right, fresh, kept_blocks, leaving, send):
    energies, cells = fresh.shape[:2]
    hbm = pl.BlockSpec(memory_space=pltpu.HBM)
    vmem = pl.BlockSpec(memory_space=pltpu.VMEM)
    carried = (send,) if last else (leaving, send)
    result = pl.pallas_call(
        functools.partial(tail_kernel, keep, share_rows, hop, last),
        out_shape=tuple(jax.ShapeDtypeStruct(value.shape, F32) for value in carried),
        in_specs=[vmem] * 4 + [hbm] + [vmem] * len(carried),
        out_specs=(vmem,) * len(carried),
        input_output_aliases={5 + i: i for i in range(len(carried))},
        scratch_shapes=[
            pltpu.SMEM(kept_blocks.shape, jnp.int32),
            pltpu.VMEM((energies, cells) + incoming.shape[1:], F32),
            pltpu.SemaphoreType.DMA,
        ],
        compiler_params=pltpu.CompilerParams(vmem_limit_bytes=32 << 20),
        name="tail_cells",
    )(incoming, left, right, fresh, in_hbm(kept_blocks), *carried)
    return (leaving, result[0]) if last else result


def lag_kernel(here, in_ref, out_hbm, out_ref, mixed_ref, sems):
    energies, double_rows, _ = in_ref.shape
    rows = double_rows // 2
    step = min(8, rows)
    scale = 1.0 / energies
    groups = sems.shape[0]
    width = LAGS // groups

    def at(e, first):
        place = (energies // here - 1 - e // here) * here + e % here
        return in_ref[place, first:first + step]

    for e in range(energies):
        for first in range(0, rows, step):
            re, im = at(e, first), at(e, rows + first)
            mixed_ref[0, e, first:first + step] = re + im
            mixed_ref[1, e, first:first + step] = re - im

    def at_all(e, first, kind):
        return mixed_ref[kind, e, first:first + step]

    copies = []
    for group in range(groups):
        for lag in range(group * width, (group + 1) * width):
            for first in range(0, rows, step):
                re_sum = jnp.zeros((step, LANES), F32)
                im_sum = jnp.zeros((step, LANES), F32)
                mixed_sum = jnp.zeros((step, LANES), F32)
                for e in range(energies - lag):
                    late_re, late_im = at(e + lag, first), at(e + lag, rows + first)
                    early_re, early_im = at(e, first), at(e, rows + first)
                    re_sum += late_re * early_re
                    im_sum += late_im * early_im
                    mixed_sum += at_all(e + lag, first, 0) * at_all(e, first, 1)
                real_sum, imag_sum = re_sum + im_sum, mixed_sum - re_sum + im_sum
                out_ref[lag, pl.ds(2 * first, step, 2), :] = real_sum * scale
                out_ref[lag, pl.ds(2 * first + 1, step, 2), :] = imag_sum * scale
        part = pl.ds(group * width, width)
        copies.append(pltpu.make_async_copy(out_ref.at[part], out_hbm.at[part], sems.at[group]))
        copies[-1].start()
    for copy in copies:
        copy.wait()


def lag_sums(here, owned):
    energies, double_rows, lanes = owned.shape
    rows = double_rows // 2
    sums = pl.pallas_call(
        functools.partial(lag_kernel, here),
        out_shape=jax.ShapeDtypeStruct((LAGS, double_rows, lanes), F32),
        in_specs=[pl.BlockSpec(memory_space=pltpu.VMEM)],
        out_specs=pl.BlockSpec(memory_space=pltpu.HBM),
        scratch_shapes=[
            pltpu.VMEM((LAGS, double_rows, lanes), F32),
            pltpu.VMEM((2, energies, rows, lanes), F32),
            pltpu.SemaphoreType.DMA((4,)),
        ],
        name="lag_sums",
    )(owned)
    sums = sums.reshape(LAGS, rows, 2, lanes)
    return jnp.swapaxes(sums, 1, 2).reshape(LAGS, 2, rows * lanes)


def per_device(retarded, lesser_sigma, coupling, coupling_pattern, kept_blocks, lead_lesser):
    cells = retarded.shape[1]
    keep = kept_blocks.shape[0]
    owners = lax.axis_size("energy")
    length = lax.axis_size("chain")
    share_rows = cells * keep * BLOCK * BLOCK // (owners * LANES)
    ring = [(i, (i + 1) % length) for i in range(length)]
    before = lax.ppermute(retarded, "chain", ring)
    leaving, fresh, factor, green, bridge = head(retarded, lesser_sigma, coupling, coupling_pattern, lead_lesser)
    incoming = lax.ppermute(leaving, "chain", ring)
    send, left, right = middle(keep, share_rows, owners, before, leaving, fresh, factor, green, bridge, kept_blocks)
    for hop in range(length - 1):
        if hop > 0:
            incoming = lax.ppermute(leaving, "chain", ring)
        last = hop == length - 2
        leaving, send = tail(keep, share_rows, hop, last, incoming, left, right, fresh, kept_blocks, leaving, send)
    backwards = [list(range(owners))[::-1]]
    owned = lax.all_to_all(send, "energy", split_axis=1, concat_axis=0, axis_index_groups=backwards, tiled=True)
    return lag_sums(retarded.shape[0], owned.reshape((-1,) + owned.shape[2:]))


def solution(mesh):
    return jax.shard_map(
        per_device,
        mesh=mesh,
        in_specs=(
            P("energy", "chain", None, None, None),
            P("energy", "chain", None, None, None),
            P("chain", None, None, None),
            P("chain", None, None),
            P(),
            P("energy", None, None, None),
        ),
        out_specs=P(None, None, ("chain", "energy")),
        check_vma=False,
    )
```

```python
import functools

import jax
import jax.numpy as jnp
from jax import lax
from jax.experimental import pallas as pl
from jax.experimental.pallas import tpu as pltpu
from jax.sharding import PartitionSpec as P

BLOCK = 64
LAGS = 16
LANES = 128
F32 = jnp.float32
BF16 = jnp.bfloat16


def two_parts(value):
    high = value.astype(BF16)
    return high, (value - high.astype(F32)).astype(BF16)


def dot(left, right):
    return lax.dot_general(left, right, (((1,), (0,)), ((), ())), preferred_element_type=F32)


def parts(pair):
    return tuple(part for value in (pair[0], pair[1], pair[0] + pair[1]) for part in two_parts(value))


def adjoint(pair):
    return pair[0].T, -pair[1].T


def product(left, right):
    real = []
    for n in range(0, 6, 2):
        wide = jnp.concatenate([left[n], left[n], left[n + 1]], axis=1)
        tall = jnp.concatenate([right[n], right[n + 1], right[n]], axis=0)
        real.append(dot(wide, tall))
    return real[0] - real[1], real[2] - real[0] - real[1]


def sandwich(left, inner, right):
    rows = left[0].shape[0] // 2
    halves = [product(tuple(part[n * rows:(n + 1) * rows] for part in left), inner) for n in range(2)]
    done = [product(parts(half), right) for half in halves]
    return tuple(jnp.concatenate(both, axis=0) for both in zip(*done))


def put_parts(ref, values):
    for n, value in enumerate(values):
        ref[n] = value


def get_parts(ref):
    return tuple(ref[n] for n in range(6))


def plus(one, other):
    return one[0] + other[0], one[1] + other[1]


def put_state(state_ref, pair):
    for part in range(2):
        for group in range(state_ref.shape[1]):
            state_ref[part, group] = pair[part][:, group * LANES:(group + 1) * LANES]


def get_state(state_ref):
    groups = range(state_ref.shape[1])
    return tuple(jnp.concatenate([state_ref[part, group] for group in groups], axis=1) for part in range(2))


def row_masks(pattern_ref, cell, size):
    nblk = size // BLOCK
    column = lax.broadcasted_iota(jnp.int32, (1, size), 1) // BLOCK
    rows = []
    for r in range(nblk):
        row = jnp.zeros((1, size), F32)
        for c in range(nblk):
            row = jnp.where(column == c, pattern_ref[cell, r, c].astype(F32), row)
        rows.append(row)
    return rows


def pick_into(send_ref, e, cell, matrix_ref, kept_ref, keep, share_rows):
    nblk = matrix_ref.shape[-2] // BLOCK
    half = BLOCK // 2
    lane = lax.broadcasted_iota(jnp.int32, (half, LANES), 1)
    piece = min(half, share_rows)
    for k in range(keep):
        number = kept_ref[k]
        top = (number // nblk) * BLOCK
        across = (number % nblk) * BLOCK
        window = across // LANES
        in_upper = jnp.full((half, LANES), across % LANES, jnp.int32) > 0
        for part in range(2):
            even = matrix_ref[part, window, pl.ds(top, half, 2), :]
            odd = matrix_ref[part, window, pl.ds(top + 1, half, 2), :]
            left = jnp.where(in_upper, pltpu.roll(even, BLOCK, 1), even)
            right = jnp.where(in_upper, odd, pltpu.roll(odd, BLOCK, 1))
            flat = jnp.where(lane < BLOCK, left, right)
            first = (cell * keep + k) * half
            for s in range(0, half, piece):
                owner, inside = divmod(first + s, share_rows)
                send_ref[e, send_ref.shape[1] - 1 - owner, pl.ds(part * share_rows + inside, piece), :] = flat[s:s + piece]


def head_kernel(g_hbm, s_hbm, b_hbm, pattern_hbm, lead_hbm,
                inner_ref, fresh_ref, factor_ref, green_ref, bridge_ref,
                pattern_ref, s_ref, b_ref, lead_ref, sems):
    energies, cells, _, size, _ = s_ref.shape
    position = lax.axis_index("chain")
    final = cells - 1

    def fetch(slot, source, target):
        return pltpu.make_async_copy(source, target, sems.at[slot])

    lead_copy = fetch(0, lead_hbm, lead_ref)
    b_copies = [fetch(1 + i, b_hbm.at[i], b_ref.at[i]) for i in range(cells)]
    g_copies = [fetch(1 + cells + i, g_hbm.at[:, i], green_ref.at[:, i]) for i in range(cells)]
    s_copies = [fetch(1 + 2 * cells + i, s_hbm.at[:, i], s_ref.at[:, i]) for i in range(cells)]
    pattern_copy = fetch(1 + 3 * cells, pattern_hbm, pattern_ref)
    pattern_copy.start()

    @pl.when(position == 0)
    def _():
        lead_copy.start()

    for i in range(cells):
        b_copies[i].start()
        g_copies[i].start()
        s_copies[i].start()
    pattern_copy.wait()

    def bridge_of(i):
        rows = row_masks(pattern_ref, i, size)
        return tuple(
            jnp.concatenate([b_ref[i, part, r * BLOCK:(r + 1) * BLOCK] * row for r, row in enumerate(rows)], axis=0)
            for part in range(2)
        )

    def green_of(e, i):
        return green_ref[e, i, 0], green_ref[e, i, 1]

    @pl.when(position == 0)
    def _():
        lead_copy.wait()
        states = [(lead_ref[e, 0], lead_ref[e, 1]) for e in range(energies)]
        for i in range(cells):
            b_copies[i].wait()
            bridge = bridge_of(i)
            bridge_left, bridge_right = parts(bridge), parts(adjoint(bridge))
            for e in range(energies):
                entered = sandwich(bridge_left, parts(states[e]), bridge_right)
                if e == 0:
                    g_copies[i].wait()
                    s_copies[i].wait()
                inner = plus((s_ref[e, i, 0], s_ref[e, i, 1]), entered)
                if i == final:
                    put_state(inner_ref.at[e], inner)
                else:
                    green = green_of(e, i)
                    states[e] = sandwich(parts(green), parts(inner), parts(adjoint(green)))
                    put_state(fresh_ref.at[e, i], states[e])

    @pl.when(position > 0)
    def _():
        for i in range(cells):
            b_copies[i].wait()
            g_copies[i].wait()
            s_copies[i].wait()
            bridge = bridge_of(i)
            if i == final:
                bridge_ref[0], bridge_ref[1] = bridge
            for e in range(energies):
                green = green_of(e, i)
                green_left = parts(green)
                if i < final:
                    factor_ref[e, i, 0], factor_ref[e, i, 1] = product(green_left, parts(bridge))
                inner = parts((s_ref[e, i, 0], s_ref[e, i, 1]))
                put_state(fresh_ref.at[e, i], sandwich(green_left, inner, parts(adjoint(green))))


def in_hbm(value):
    return pltpu.with_memory_space_constraint(value, pltpu.HBM)


def head(retarded, lesser_sigma, coupling, pattern, lead):
    energies, cells, _, size, _ = retarded.shape
    hbm = pl.BlockSpec(memory_space=pltpu.HBM)
    vmem = pl.BlockSpec(memory_space=pltpu.VMEM)
    state_shape = (2, size // LANES, size, LANES)
    others = max(cells - 1, 1)
    return pl.pallas_call(
        head_kernel,
        out_shape=(
            jax.ShapeDtypeStruct((energies,) + state_shape, F32),
            jax.ShapeDtypeStruct((energies, cells) + state_shape, F32),
            jax.ShapeDtypeStruct((energies, others, 2, size, size), F32),
            jax.ShapeDtypeStruct(retarded.shape, F32),
            jax.ShapeDtypeStruct((2, size, size), F32),
        ),
        in_specs=[hbm] * 5,
        out_specs=(vmem,) * 5,
        scratch_shapes=[
            pltpu.SMEM(pattern.shape, jnp.int32),
            pltpu.VMEM(lesser_sigma.shape, F32),
            pltpu.VMEM(coupling.shape, F32),
            pltpu.VMEM(lead.shape, F32),
            pltpu.SemaphoreType.DMA((2 + 3 * cells,)),
        ],
        compiler_params=pltpu.CompilerParams(vmem_limit_bytes=32 << 20),
        name="head_cells",
    )(*(in_hbm(x) for x in (retarded, lesser_sigma, coupling, pattern, lead)))


def middle_kernel(keep, share_rows, before_ref, inner_ref, fresh_ref, factor_ref, green_ref, bridge_ref, kept_hbm,
                  send_ref, left_ref, right_ref, kept_ref, state_ref, sem):
    energies, cells = fresh_ref.shape[:2]
    final = cells - 1
    position = lax.axis_index("chain")
    kept_copy = pltpu.make_async_copy(kept_hbm, kept_ref, sem)
    kept_copy.start()

    @pl.when(position == 0)
    def _():
        for e in range(energies):
            for i in range(cells)[::-1]:
                matrix_ref = fresh_ref.at[e, i]
                if i == final:
                    green = green_ref[e, i, 0], green_ref[e, i, 1]
                    inner = parts(get_state(inner_ref.at[e]))
                    matrix_ref = state_ref.at[e]
                    put_state(matrix_ref, sandwich(parts(green), inner, parts(adjoint(green))))
                if i == final and e == 0:
                    kept_copy.wait()
                pick_into(send_ref, e, i, matrix_ref, kept_ref, keep, share_rows)

    def factors(with_before):
        for e in range(energies):
            for i in range(cells):
                if i < final:
                    factor = factor_ref[e, i, 0], factor_ref[e, i, 1]
                else:
                    green = parts((green_ref[e, i, 0], green_ref[e, i, 1]))
                    factor = product(green, parts((bridge_ref[0], bridge_ref[1])))
                if i == 0 and with_before:
                    factor = product(parts(factor), parts((before_ref[e, final, 0], before_ref[e, final, 1])))
                put_parts(left_ref.at[e, i], parts(factor))
                put_parts(right_ref.at[e, i], parts(adjoint(factor)))

    @pl.when(position == 1)
    def _():
        factors(True)
        kept_copy.wait()

    if lax.axis_size("chain") > 2:
        @pl.when(position > 1)
        def _():
            factors(False)
            kept_copy.wait()


def middle(keep, share_rows, owners, before, inner, fresh, factor, green, bridge, kept_blocks):
    energies, cells = fresh.shape[:2]
    size = bridge.shape[-1]
    hbm = pl.BlockSpec(memory_space=pltpu.HBM)
    vmem = pl.BlockSpec(memory_space=pltpu.VMEM)
    return pl.pallas_call(
        functools.partial(middle_kernel, keep, share_rows),
        out_shape=(
            jax.ShapeDtypeStruct((energies, owners, 2 * share_rows, LANES), F32),
            jax.ShapeDtypeStruct((energies, cells, 6, size, size), BF16),
            jax.ShapeDtypeStruct((energies, cells, 6, size, size), BF16),
        ),
        in_specs=[vmem] * 6 + [hbm],
        out_specs=(vmem,) * 3,
        scratch_shapes=[
            pltpu.SMEM(kept_blocks.shape, jnp.int32),
            pltpu.VMEM(inner.shape, F32),
            pltpu.SemaphoreType.DMA,
        ],
        compiler_params=pltpu.CompilerParams(vmem_limit_bytes=32 << 20),
        cost_estimate=pl.CostEstimate(flops=12 * 2 * size**3, bytes_accessed=4 * size * size, transcendentals=0),
        name="middle_cells",
    )(before, inner, fresh, factor, green, bridge, in_hbm(kept_blocks))


def tail_kernel(keep, share_rows, hop, last, incoming_ref, left_ref, right_ref, fresh_ref, kept_hbm, *refs):
    if last:
        (_, send_ref), refs = refs[:2], refs[2:]
        leaving_ref = None
    else:
        (_, _, leaving_ref, send_ref), refs = refs[:4], refs[4:]
    kept_ref, state_ref, sem = refs
    energies, cells = fresh_ref.shape[:2]

    @pl.when(lax.axis_index("chain") == hop + 1)
    def _():
        kept_copy = pltpu.make_async_copy(kept_hbm, kept_ref, sem)
        kept_copy.start()
        for e in range(energies):
            state = get_state(incoming_ref.at[e])
            for i in range(cells):
                grown = sandwich(get_parts(left_ref.at[e, i]), parts(state), get_parts(right_ref.at[e, i]))
                state = plus(get_state(fresh_ref.at[e, i]), grown)
                put_state(state_ref.at[e, i], state)
                if i == 0 and e == 0:
                    kept_copy.wait()
                pick_into(send_ref, e, i, state_ref.at[e, i], kept_ref, keep, share_rows)
            if not last:
                leaving_ref[e] = state_ref[e, cells - 1]


def tail(keep, share_rows, hop, last, incoming, left, right, fresh, kept_blocks, leaving, send):
    energies, cells = fresh.shape[:2]
    hbm = pl.BlockSpec(memory_space=pltpu.HBM)
    vmem = pl.BlockSpec(memory_space=pltpu.VMEM)
    carried = (send,) if last else (leaving, send)
    result = pl.pallas_call(
        functools.partial(tail_kernel, keep, share_rows, hop, last),
        out_shape=tuple(jax.ShapeDtypeStruct(value.shape, F32) for value in carried),
        in_specs=[vmem] * 4 + [hbm] + [vmem] * len(carried),
        out_specs=(vmem,) * len(carried),
        input_output_aliases={5 + i: i for i in range(len(carried))},
        scratch_shapes=[
            pltpu.SMEM(kept_blocks.shape, jnp.int32),
            pltpu.VMEM((energies, cells) + incoming.shape[1:], F32),
            pltpu.SemaphoreType.DMA,
        ],
        compiler_params=pltpu.CompilerParams(vmem_limit_bytes=32 << 20),
        name="tail_cells",
    )(incoming, left, right, fresh, in_hbm(kept_blocks), *carried)
    return (leaving, result[0]) if last else result


def lag_kernel(here, in_ref, out_hbm, out_ref, mixed_ref, sems):
    energies, double_rows, _ = in_ref.shape
    rows = double_rows // 2
    step = min(8, rows)
    scale = 1.0 / energies
    groups = sems.shape[0]
    width = LAGS // groups

    def at(e, first):
        place = (energies // here - 1 - e // here) * here + e % here
        return in_ref[place, first:first + step]

    for e in range(energies):
        for first in range(0, rows, step):
            re, im = at(e, first), at(e, rows + first)
            mixed_ref[0, e, first:first + step] = re + im
            mixed_ref[1, e, first:first + step] = re - im

    def at_all(e, first, kind):
        return mixed_ref[kind, e, first:first + step]

    copies = []
    for group in range(groups):
        for lag in range(group * width, (group + 1) * width):
            for first in range(0, rows, step):
                re_sum = jnp.zeros((step, LANES), F32)
                im_sum = jnp.zeros((step, LANES), F32)
                mixed_sum = jnp.zeros((step, LANES), F32)
                for e in range(energies - lag):
                    late_re, late_im = at(e + lag, first), at(e + lag, rows + first)
                    early_re, early_im = at(e, first), at(e, rows + first)
                    re_sum += late_re * early_re
                    im_sum += late_im * early_im
                    mixed_sum += at_all(e + lag, first, 0) * at_all(e, first, 1)
                real_sum, imag_sum = re_sum + im_sum, mixed_sum - re_sum + im_sum
                out_ref[lag, pl.ds(2 * first, step, 2), :] = real_sum * scale
                out_ref[lag, pl.ds(2 * first + 1, step, 2), :] = imag_sum * scale
        part = pl.ds(group * width, width)
        copies.append(pltpu.make_async_copy(out_ref.at[part], out_hbm.at[part], sems.at[group]))
        copies[-1].start()
    for copy in copies:
        copy.wait()


def lag_sums(here, owned):
    energies, double_rows, lanes = owned.shape
    rows = double_rows // 2
    sums = pl.pallas_call(
        functools.partial(lag_kernel, here),
        out_shape=jax.ShapeDtypeStruct((LAGS, double_rows, lanes), F32),
        in_specs=[pl.BlockSpec(memory_space=pltpu.VMEM)],
        out_specs=pl.BlockSpec(memory_space=pltpu.HBM),
        scratch_shapes=[
            pltpu.VMEM((LAGS, double_rows, lanes), F32),
            pltpu.VMEM((2, energies, rows, lanes), F32),
            pltpu.SemaphoreType.DMA((4,)),
        ],
        name="lag_sums",
    )(owned)
    sums = sums.reshape(LAGS, rows, 2, lanes)
    return jnp.swapaxes(sums, 1, 2).reshape(LAGS, 2, rows * lanes)


def per_device(retarded, lesser_sigma, coupling, coupling_pattern, kept_blocks, lead_lesser):
    cells = retarded.shape[1]
    keep = kept_blocks.shape[0]
    owners = lax.axis_size("energy")
    length = lax.axis_size("chain")
    share_rows = cells * keep * BLOCK * BLOCK // (owners * LANES)
    ring = [(i, (i + 1) % length) for i in range(length)]
    before = lax.ppermute(retarded, "chain", ring)
    leaving, fresh, factor, green, bridge = head(retarded, lesser_sigma, coupling, coupling_pattern, lead_lesser)
    incoming = lax.ppermute(leaving, "chain", ring)
    send, left, right = middle(keep, share_rows, owners, before, leaving, fresh, factor, green, bridge, kept_blocks)
    for hop in range(length - 1):
        if hop > 0:
            incoming = lax.ppermute(leaving, "chain", ring)
        last = hop == length - 2
        leaving, send = tail(keep, share_rows, hop, last, incoming, left, right, fresh, kept_blocks, leaving, send)
    backwards = [list(range(owners))[::-1]]
    owned = lax.all_to_all(send, "energy", split_axis=1, concat_axis=0, axis_index_groups=backwards, tiled=True)
    return lag_sums(retarded.shape[0], owned.reshape((-1,) + owned.shape[2:]))


def solution(mesh):
    return jax.shard_map(
        per_device,
        mesh=mesh,
        in_specs=(
            P("energy", "chain", None, None, None),
            P("energy", "chain", None, None, None),
            P("chain", None, None, None),
            P("chain", None, None),
            P(),
            P("energy", None, None, None),
        ),
        out_specs=P(None, None, ("chain", "energy")),
        check_vma=False,
    )
```

```python
import functools

import jax
import jax.numpy as jnp
from jax import lax
from jax.experimental import pallas as pl
from jax.experimental.pallas import tpu as pltpu
from jax.sharding import PartitionSpec as P

BLOCK = 64
LAGS = 16
LANES = 128
F32 = jnp.float32
BF16 = jnp.bfloat16


def two_parts(value):
    high = value.astype(BF16)
    return high, (value - high.astype(F32)).astype(BF16)


def dot(left, right):
    return lax.dot_general(left, right, (((1,), (0,)), ((), ())), preferred_element_type=F32)


def parts(pair):
    return tuple(part for value in (pair[0], pair[1], pair[0] + pair[1]) for part in two_parts(value))


def adjoint(pair):
    return pair[0].T, -pair[1].T


def product(left, right):
    real = []
    for n in range(0, 6, 2):
        wide = jnp.concatenate([left[n], left[n], left[n + 1]], axis=1)
        tall = jnp.concatenate([right[n], right[n + 1], right[n]], axis=0)
        real.append(dot(wide, tall))
    return real[0] - real[1], real[2] - real[0] - real[1]


def sandwich(left, inner, right):
    rows = left[0].shape[0] // 2
    halves = [product(tuple(part[n * rows:(n + 1) * rows] for part in left), inner) for n in range(2)]
    done = [product(parts(half), right) for half in halves]
    return tuple(jnp.concatenate(both, axis=0) for both in zip(*done))


def put_parts(ref, values):
    for n, value in enumerate(values):
        ref[n] = value


def get_parts(ref):
    return tuple(ref[n] for n in range(6))


def plus(one, other):
    return one[0] + other[0], one[1] + other[1]


def put_state(state_ref, pair):
    for part in range(2):
        for group in range(state_ref.shape[1]):
            state_ref[part, group] = pair[part][:, group * LANES:(group + 1) * LANES]


def get_state(state_ref):
    groups = range(state_ref.shape[1])
    return tuple(jnp.concatenate([state_ref[part, group] for group in groups], axis=1) for part in range(2))


def block_mask(pattern_ref, cell, size):
    nblk = size // BLOCK
    column = lax.broadcasted_iota(jnp.int32, (BLOCK, size), 1) // BLOCK
    rows = []
    for r in range(nblk):
        row = jnp.zeros((BLOCK, size), F32)
        for c in range(nblk):
            row = jnp.where(column == c, pattern_ref[cell, r, c].astype(F32), row)
        rows.append(row)
    return jnp.concatenate(rows, axis=0)


def pick_into(send_ref, e, cell, matrix_ref, kept_ref, keep, share_rows):
    nblk = matrix_ref.shape[-2] // BLOCK
    half = BLOCK // 2
    lane = lax.broadcasted_iota(jnp.int32, (half, LANES), 1)
    piece = min(half, share_rows)
    for k in range(keep):
        number = kept_ref[k]
        top = (number // nblk) * BLOCK
        across = (number % nblk) * BLOCK
        window = across // LANES
        in_upper = jnp.full((half, LANES), across % LANES, jnp.int32) > 0
        for part in range(2):
            even = matrix_ref[part, window, pl.ds(top, half, 2), :]
            odd = matrix_ref[part, window, pl.ds(top + 1, half, 2), :]
            left = jnp.where(in_upper, pltpu.roll(even, BLOCK, 1), even)
            right = jnp.where(in_upper, odd, pltpu.roll(odd, BLOCK, 1))
            flat = jnp.where(lane < BLOCK, left, right)
            first = (cell * keep + k) * half
            for s in range(0, half, piece):
                owner, inside = divmod(first + s, share_rows)
                send_ref[e, send_ref.shape[1] - 1 - owner, pl.ds(part * share_rows + inside, piece), :] = flat[s:s + piece]


def head_kernel(g_hbm, s_hbm, b_hbm, pattern_hbm, lead_hbm,
                inner_ref, fresh_ref, factor_ref, green_ref, bridge_ref,
                pattern_ref, s_ref, b_ref, lead_ref, sems):
    energies, cells, _, size, _ = s_ref.shape
    position = lax.axis_index("chain")
    final = cells - 1

    def fetch(slot, source, target):
        return pltpu.make_async_copy(source, target, sems.at[slot])

    lead_copy = fetch(0, lead_hbm, lead_ref)
    b_copies = [fetch(1 + i, b_hbm.at[i], b_ref.at[i]) for i in range(cells)]
    g_copies = [fetch(1 + cells + i, g_hbm.at[:, i], green_ref.at[:, i]) for i in range(cells)]
    s_copies = [fetch(1 + 2 * cells + i, s_hbm.at[:, i], s_ref.at[:, i]) for i in range(cells)]
    pattern_copy = fetch(1 + 3 * cells, pattern_hbm, pattern_ref)
    pattern_copy.start()

    @pl.when(position == 0)
    def _():
        lead_copy.start()

    for i in range(cells):
        b_copies[i].start()
        g_copies[i].start()
        s_copies[i].start()
    pattern_copy.wait()

    def bridge_of(i):
        mask = block_mask(pattern_ref, i, size)
        return b_ref[i, 0] * mask, b_ref[i, 1] * mask

    def green_of(e, i):
        return green_ref[e, i, 0], green_ref[e, i, 1]

    @pl.when(position == 0)
    def _():
        lead_copy.wait()
        states = [(lead_ref[e, 0], lead_ref[e, 1]) for e in range(energies)]
        for i in range(cells):
            b_copies[i].wait()
            bridge = bridge_of(i)
            bridge_left, bridge_right = parts(bridge), parts(adjoint(bridge))
            for e in range(energies):
                entered = sandwich(bridge_left, parts(states[e]), bridge_right)
                if e == 0:
                    g_copies[i].wait()
                    s_copies[i].wait()
                inner = plus((s_ref[e, i, 0], s_ref[e, i, 1]), entered)
                if i == final:
                    put_state(inner_ref.at[e], inner)
                else:
                    green = green_of(e, i)
                    states[e] = sandwich(parts(green), parts(inner), parts(adjoint(green)))
                    put_state(fresh_ref.at[e, i], states[e])

    @pl.when(position > 0)
    def _():
        for i in range(cells):
            b_copies[i].wait()
            g_copies[i].wait()
            s_copies[i].wait()
            bridge = bridge_of(i)
            if i == final:
                bridge_ref[0], bridge_ref[1] = bridge
            for e in range(energies):
                green = green_of(e, i)
                green_left = parts(green)
                if i < final:
                    factor_ref[e, i, 0], factor_ref[e, i, 1] = product(green_left, parts(bridge))
                inner = parts((s_ref[e, i, 0], s_ref[e, i, 1]))
                put_state(fresh_ref.at[e, i], sandwich(green_left, inner, parts(adjoint(green))))


def in_hbm(value):
    return pltpu.with_memory_space_constraint(value, pltpu.HBM)


def head(retarded, lesser_sigma, coupling, pattern, lead):
    energies, cells, _, size, _ = retarded.shape
    hbm = pl.BlockSpec(memory_space=pltpu.HBM)
    vmem = pl.BlockSpec(memory_space=pltpu.VMEM)
    state_shape = (2, size // LANES, size, LANES)
    others = max(cells - 1, 1)
    return pl.pallas_call(
        head_kernel,
        out_shape=(
            jax.ShapeDtypeStruct((energies,) + state_shape, F32),
            jax.ShapeDtypeStruct((energies, cells) + state_shape, F32),
            jax.ShapeDtypeStruct((energies, others, 2, size, size), F32),
            jax.ShapeDtypeStruct(retarded.shape, F32),
            jax.ShapeDtypeStruct((2, size, size), F32),
        ),
        in_specs=[hbm] * 5,
        out_specs=(vmem,) * 5,
        scratch_shapes=[
            pltpu.SMEM(pattern.shape, jnp.int32),
            pltpu.VMEM(lesser_sigma.shape, F32),
            pltpu.VMEM(coupling.shape, F32),
            pltpu.VMEM(lead.shape, F32),
            pltpu.SemaphoreType.DMA((2 + 3 * cells,)),
        ],
        compiler_params=pltpu.CompilerParams(vmem_limit_bytes=32 << 20),
        name="head_cells",
    )(*(in_hbm(x) for x in (retarded, lesser_sigma, coupling, pattern, lead)))


def middle_kernel(keep, share_rows, before_ref, inner_ref, fresh_ref, factor_ref, green_ref, bridge_ref, kept_hbm,
                  send_ref, left_ref, right_ref, kept_ref, state_ref, sem):
    energies, cells = fresh_ref.shape[:2]
    final = cells - 1
    position = lax.axis_index("chain")
    kept_copy = pltpu.make_async_copy(kept_hbm, kept_ref, sem)
    kept_copy.start()

    @pl.when(position == 0)
    def _():
        for e in range(energies):
            for i in range(cells)[::-1]:
                matrix_ref = fresh_ref.at[e, i]
                if i == final:
                    green = green_ref[e, i, 0], green_ref[e, i, 1]
                    inner = parts(get_state(inner_ref.at[e]))
                    matrix_ref = state_ref.at[e]
                    put_state(matrix_ref, sandwich(parts(green), inner, parts(adjoint(green))))
                if i == final and e == 0:
                    kept_copy.wait()
                pick_into(send_ref, e, i, matrix_ref, kept_ref, keep, share_rows)

    def factors(with_before):
        for e in range(energies):
            for i in range(cells):
                if i < final:
                    factor = factor_ref[e, i, 0], factor_ref[e, i, 1]
                else:
                    green = parts((green_ref[e, i, 0], green_ref[e, i, 1]))
                    factor = product(green, parts((bridge_ref[0], bridge_ref[1])))
                if i == 0 and with_before:
                    factor = product(parts(factor), parts((before_ref[e, final, 0], before_ref[e, final, 1])))
                put_parts(left_ref.at[e, i], parts(factor))
                put_parts(right_ref.at[e, i], parts(adjoint(factor)))

    @pl.when(position == 1)
    def _():
        factors(True)
        kept_copy.wait()

    if lax.axis_size("chain") > 2:
        @pl.when(position > 1)
        def _():
            factors(False)
            kept_copy.wait()


def middle(keep, share_rows, owners, before, inner, fresh, factor, green, bridge, kept_blocks):
    energies, cells = fresh.shape[:2]
    size = bridge.shape[-1]
    hbm = pl.BlockSpec(memory_space=pltpu.HBM)
    vmem = pl.BlockSpec(memory_space=pltpu.VMEM)
    return pl.pallas_call(
        functools.partial(middle_kernel, keep, share_rows),
        out_shape=(
            jax.ShapeDtypeStruct((energies, owners, 2 * share_rows, LANES), F32),
            jax.ShapeDtypeStruct((energies, cells, 6, size, size), BF16),
            jax.ShapeDtypeStruct((energies, cells, 6, size, size), BF16),
        ),
        in_specs=[vmem] * 6 + [hbm],
        out_specs=(vmem,) * 3,
        scratch_shapes=[
            pltpu.SMEM(kept_blocks.shape, jnp.int32),
            pltpu.VMEM(inner.shape, F32),
            pltpu.SemaphoreType.DMA,
        ],
        compiler_params=pltpu.CompilerParams(vmem_limit_bytes=32 << 20),
        cost_estimate=pl.CostEstimate(flops=12 * 2 * size**3, bytes_accessed=4 * size * size, transcendentals=0),
        name="middle_cells",
    )(before, inner, fresh, factor, green, bridge, in_hbm(kept_blocks))


def tail_kernel(keep, share_rows, hop, last, incoming_ref, left_ref, right_ref, fresh_ref, kept_hbm, *refs):
    if last:
        (_, send_ref), refs = refs[:2], refs[2:]
        leaving_ref = None
    else:
        (_, _, leaving_ref, send_ref), refs = refs[:4], refs[4:]
    kept_ref, state_ref, sem = refs
    energies, cells = fresh_ref.shape[:2]

    @pl.when(lax.axis_index("chain") == hop + 1)
    def _():
        kept_copy = pltpu.make_async_copy(kept_hbm, kept_ref, sem)
        kept_copy.start()
        for e in range(energies):
            state = get_state(incoming_ref.at[e])
            for i in range(cells):
                grown = sandwich(get_parts(left_ref.at[e, i]), parts(state), get_parts(right_ref.at[e, i]))
                state = plus(get_state(fresh_ref.at[e, i]), grown)
                put_state(state_ref.at[e, i], state)
                if i == 0 and e == 0:
                    kept_copy.wait()
                pick_into(send_ref, e, i, state_ref.at[e, i], kept_ref, keep, share_rows)
            if not last:
                leaving_ref[e] = state_ref[e, cells - 1]


def tail(keep, share_rows, hop, last, incoming, left, right, fresh, kept_blocks, leaving, send):
    energies, cells = fresh.shape[:2]
    hbm = pl.BlockSpec(memory_space=pltpu.HBM)
    vmem = pl.BlockSpec(memory_space=pltpu.VMEM)
    carried = (send,) if last else (leaving, send)
    result = pl.pallas_call(
        functools.partial(tail_kernel, keep, share_rows, hop, last),
        out_shape=tuple(jax.ShapeDtypeStruct(value.shape, F32) for value in carried),
        in_specs=[vmem] * 4 + [hbm] + [vmem] * len(carried),
        out_specs=(vmem,) * len(carried),
        input_output_aliases={5 + i: i for i in range(len(carried))},
        scratch_shapes=[
            pltpu.SMEM(kept_blocks.shape, jnp.int32),
            pltpu.VMEM((energies, cells) + incoming.shape[1:], F32),
            pltpu.SemaphoreType.DMA,
        ],
        compiler_params=pltpu.CompilerParams(vmem_limit_bytes=32 << 20),
        name="tail_cells",
    )(incoming, left, right, fresh, in_hbm(kept_blocks), *carried)
    return (leaving, result[0]) if last else result


def lag_kernel(here, in_ref, out_hbm, out_ref, mixed_ref, sems):
    energies, double_rows, _ = in_ref.shape
    rows = double_rows // 2
    step = min(8, rows)
    scale = 1.0 / energies
    groups = sems.shape[0]
    width = LAGS // groups

    def at(e, first):
        place = (energies // here - 1 - e // here) * here + e % here
        return in_ref[place, first:first + step]

    for e in range(energies):
        for first in range(0, rows, step):
            re, im = at(e, first), at(e, rows + first)
            mixed_ref[0, e, first:first + step] = re + im
            mixed_ref[1, e, first:first + step] = re - im

    def at_all(e, first, kind):
        return mixed_ref[kind, e, first:first + step]

    copies = []
    for group in range(groups):
        for lag in range(group * width, (group + 1) * width):
            for first in range(0, rows, step):
                re_sum = jnp.zeros((step, LANES), F32)
                im_sum = jnp.zeros((step, LANES), F32)
                mixed_sum = jnp.zeros((step, LANES), F32)
                for e in range(energies - lag):
                    late_re, late_im = at(e + lag, first), at(e + lag, rows + first)
                    early_re, early_im = at(e, first), at(e, rows + first)
                    re_sum += late_re * early_re
                    im_sum += late_im * early_im
                    mixed_sum += at_all(e + lag, first, 0) * at_all(e, first, 1)
                real_sum, imag_sum = re_sum + im_sum, mixed_sum - re_sum + im_sum
                out_ref[lag, pl.ds(2 * first, step, 2), :] = real_sum * scale
                out_ref[lag, pl.ds(2 * first + 1, step, 2), :] = imag_sum * scale
        part = pl.ds(group * width, width)
        copies.append(pltpu.make_async_copy(out_ref.at[part], out_hbm.at[part], sems.at[group]))
        copies[-1].start()
    for copy in copies:
        copy.wait()


def lag_sums(here, owned):
    energies, double_rows, lanes = owned.shape
    rows = double_rows // 2
    sums = pl.pallas_call(
        functools.partial(lag_kernel, here),
        out_shape=jax.ShapeDtypeStruct((LAGS, double_rows, lanes), F32),
        in_specs=[pl.BlockSpec(memory_space=pltpu.VMEM)],
        out_specs=pl.BlockSpec(memory_space=pltpu.HBM),
        scratch_shapes=[
            pltpu.VMEM((LAGS, double_rows, lanes), F32),
            pltpu.VMEM((2, energies, rows, lanes), F32),
            pltpu.SemaphoreType.DMA((8,)),
        ],
        name="lag_sums",
    )(owned)
    sums = sums.reshape(LAGS, rows, 2, lanes)
    return jnp.swapaxes(sums, 1, 2).reshape(LAGS, 2, rows * lanes)


def per_device(retarded, lesser_sigma, coupling, coupling_pattern, kept_blocks, lead_lesser):
    cells = retarded.shape[1]
    keep = kept_blocks.shape[0]
    owners = lax.axis_size("energy")
    length = lax.axis_size("chain")
    share_rows = cells * keep * BLOCK * BLOCK // (owners * LANES)
    ring = [(i, (i + 1) % length) for i in range(length)]
    before = lax.ppermute(retarded, "chain", ring)
    leaving, fresh, factor, green, bridge = head(retarded, lesser_sigma, coupling, coupling_pattern, lead_lesser)
    incoming = lax.ppermute(leaving, "chain", ring)
    send, left, right = middle(keep, share_rows, owners, before, leaving, fresh, factor, green, bridge, kept_blocks)
    for hop in range(length - 1):
        if hop > 0:
            incoming = lax.ppermute(leaving, "chain", ring)
        last = hop == length - 2
        leaving, send = tail(keep, share_rows, hop, last, incoming, left, right, fresh, kept_blocks, leaving, send)
    backwards = [list(range(owners))[::-1]]
    owned = lax.all_to_all(send, "energy", split_axis=1, concat_axis=0, axis_index_groups=backwards, tiled=True)
    return lag_sums(retarded.shape[0], owned.reshape((-1,) + owned.shape[2:]))


def solution(mesh):
    return jax.shard_map(
        per_device,
        mesh=mesh,
        in_specs=(
            P("energy", "chain", None, None, None),
            P("energy", "chain", None, None, None),
            P("chain", None, None, None),
            P("chain", None, None),
            P(),
            P("energy", None, None, None),
        ),
        out_specs=P(None, None, ("chain", "energy")),
        check_vma=False,
    )
```
